128 devices in a mesh: policy: 4 (over x_lo, core), fsdp: 32 (over y, z, x_hi).
Axes of the slice: x: 4 (x_hi: 2, x_lo: 2; x = x_hi * 2 + x_lo), y: 4, z: 4, core: 2. Of those that a mesh axis runs over, the one named last changes fastest.
Arguments:
- policies: float32 [4, 8192, 8192], P('policy', 'fsdp'), may hold values from -6 to 6
- anchor: bfloat16 [8192, 8192], P(None, 'fsdp'), may hold values from -6 to 6
Outputs:
- blended: float32 [8192, 8192], P('fsdp')
- next_anchor: bfloat16 [8192, 8192], P(None, 'fsdp')
The draws below stay inside these ranges and needn't reach their ends.
All inputs are finite; a program needn't handle non-finite values.
Results may differ from the reference program's by a relative error of at most 0.0065.
Values may be sent and summed in bfloat16 or wider, within the bound.
No kernel may reach another device: no remote copies, remote signals or barrier semaphores. Data moves between devices by JAX's collectives and lax.ppermute only.
A program may use at most 128 MiB of HBM per device.

```python
import jax
import jax.numpy as jnp

D = 8192
GROUPS = 4


def block_scale(key, dims, shards, least, top_value):
    gain, own = 1.0, jax.random.fold_in(key, 6)
    for axis_at, blocks in shards:
        draws = jnp.exp(jax.random.uniform(jax.random.fold_in(own, axis_at), (blocks,), jnp.float32, least / len(shards), top_value / len(shards)))
        gain = gain * jnp.repeat(draws, dims[axis_at] // blocks).reshape([-1 if axis == axis_at else 1 for axis in range(len(dims))])
    return gain


def centred(stream_key, shape, width, most, split=(), held_as=jnp.bfloat16):
    level = block_scale(stream_key, shape, split, -0.22, 0.18) if split else 1.0
    result = jax.random.normal(stream_key, shape, jnp.float32) * width * level
    return jnp.minimum(jnp.maximum(result, -most), most).astype(held_as)


def setup_inputs(seed: int = 0) -> dict:
    splits = jax.random.split(jax.random.key(seed), 3)
    return {
        "policies": centred(splits[0], (GROUPS, D, D), 1.0, 6.0, ((0, 4), (1, 32)), jnp.float32),
        "anchor": centred(splits[1], (D, D), 1.0, 6.0, ((1, 32),)),
    }


blend_rate = 0.3


def reference(policies, anchor):
    summed = jnp.sum(policies.astype(jnp.float32), axis=0)
    average = summed / GROUPS
    blended = (1.0 - blend_rate) * anchor.astype(jnp.float32) + blend_rate * average
    next_anchor = blended.astype(jnp.bfloat16)
    return blended, next_anchor
```

```python
import jax
import jax.numpy as jnp
import numpy as np
from jax import lax
from jax.experimental import pallas as pl
from jax.experimental.pallas import tpu as pltpu
from jax.sharding import Mesh, PartitionSpec as P

blend_rate = 0.3

AXES = ("xl", "c", "y", "z", "xh")
SIZES = (2, 2, 4, 4, 2)
SHARDS = 32
ROWS = 256
WIDTH = 256
D = 8192
HALF = 128
QUARTER = 64
R = 32
BF = jnp.bfloat16
F32 = jnp.float32
VMEM_LIMIT = 10 << 20
PARTS = 8
PER = SHARDS // PARTS
SUM_COST = 30 << 20
WRITE_COST = 11 << 20
LAST_COST = 37 << 20
HBM = pl.BlockSpec(memory_space=pltpu.HBM)
VMEM = pl.BlockSpec(memory_space=pltpu.VMEM)
TOKEN = pltpu.VMEM((8, 128), jnp.int32)


def exchange_groups():
    ids = np.arange(128).reshape(SIZES)
    return [
        [int(ids[flip ^ xh, c, y, z, xh]) for y in range(4) for z in range(4) for xh in range(2)]
        for flip in range(2)
        for c in range(2)
    ]


def in_vmem(x):
    return pltpu.with_memory_space_constraint(x, pltpu.VMEM)


class Order:
    def __init__(self, place):
        self.place = place
        self.token = None

    def run(self, body, name, args, specs, outs, out_specs, scratch, aliases=None, size=1024):
        held = [] if self.token is None else [self.token]

        def ordered(at, *refs):
            ins, rest = refs[: len(args)], refs[len(args) + len(held) :]
            results, token, others = rest[: len(outs)], rest[len(outs)], rest[len(outs) + 1 :]
            body(at, *ins, *results, *others)
            token[...] = jnp.zeros_like(token)

        *results, self.token = pl.pallas_call(
            ordered,
            out_shape=[*outs, TOKEN],
            grid_spec=pltpu.PrefetchScalarGridSpec(
                num_scalar_prefetch=1,
                grid=(),
                in_specs=[*specs, *[VMEM] * len(held)],
                out_specs=[*out_specs, VMEM],
                scratch_shapes=scratch,
            ),
            input_output_aliases=aliases or {},
            compiler_params=pltpu.CompilerParams(vmem_limit_bytes=VMEM_LIMIT),
            cost_estimate=pl.CostEstimate(flops=0, bytes_accessed=size, transcendentals=0),
            name=name,
        )(self.place, *args, *held)
        return results


def columns(g):
    return pl.ds(pl.multiple_of(g * WIDTH, WIDTH), WIDTH)


def each(count, work):
    pl.loop(0, count)(work)


def first_row(at, core, chip, start, xl=None):
    xl = at[0] if xl is None else xl
    half = at[1] if core else 1 - at[1]
    quarter = xl if chip else 1 - xl
    return pl.multiple_of(half * HALF + quarter * QUARTER + start, 16)


def member_row(at, where, xh):
    differs = at[2] if xh == 0 else 1 - at[2]
    return first_row(at, *where, at[0] + differs - 2 * at[0] * differs)


def tiles_out(rows):
    return pltpu.VMEM((SHARDS, rows, WIDTH), BF)


def span_of(p):
    return pl.ds(pl.multiple_of(p * PER * WIDTH, WIDTH), PER * WIDTH)


def cast_rows(order, policy):
    def body(at, x_ref, o_ref, wide, sems):
        held = pl.ds(first_row(at, False, False, 0), QUARTER)

        def copy(p):
            return pltpu.make_async_copy(x_ref.at[held, span_of(p)], wide.at[:, span_of(p)], sems.at[p])

        def work(p):
            copy(p).wait()
            for k in range(PER):
                g = p * PER + k
                o_ref[g] = wide[:, columns(g)].astype(BF)

        each(PARTS, lambda p: copy(p).start())
        each(PARTS, work)

    (out,) = order.run(
        body,
        "cast_rows",
        (policy,),
        [HBM],
        [tiles_out(QUARTER)],
        [VMEM],
        [pltpu.VMEM((QUARTER, D), F32), pltpu.SemaphoreType.DMA((PARTS,))],
    )
    return out


def add_theirs(order, policy, tiles):
    def body(at, x_ref, t_ref, o_ref, wide, held, in_sems, out_sems):
        rows = pl.ds(first_row(at, True, False, 0), QUARTER)

        def fetch(p):
            return pltpu.make_async_copy(x_ref.at[rows, span_of(p)], wide.at[:, span_of(p)], in_sems.at[p])

        def store(p):
            some = pl.ds(p * PER, PER)
            return pltpu.make_async_copy(held.at[some], o_ref.at[some], out_sems.at[p])

        def work(p):
            fetch(p).wait()
            for k in range(PER):
                g = p * PER + k
                held[g] = (wide[:, columns(g)] + t_ref[g].astype(F32)).astype(BF)
            store(p).start()

        each(PARTS, lambda p: fetch(p).start())
        each(PARTS, work)
        each(PARTS, lambda p: store(p).wait())

    (out,) = order.run(
        body,
        "add_theirs",
        (policy, in_vmem(tiles)),
        [HBM, VMEM],
        [pltpu.HBM((SHARDS, QUARTER, WIDTH), BF)],
        [HBM],
        [
            pltpu.VMEM((QUARTER, D), F32),
            pltpu.VMEM((SHARDS, QUARTER, WIDTH), BF),
            pltpu.SemaphoreType.DMA((PARTS,)),
            pltpu.SemaphoreType.DMA((PARTS,)),
        ],
    )
    return out


def add_rows(order, policy, tiles):
    def body(at, x_ref, t_ref, o_ref, wide, sems):
        held = pl.ds(first_row(at, True, True, 0), QUARTER)

        def copy(p):
            return pltpu.make_async_copy(x_ref.at[held, span_of(p)], wide.at[:, span_of(p)], sems.at[p])

        def work(p):
            copy(p).wait()
            for k in range(PER):
                g = p * PER + k
                o_ref[g] = (wide[:, columns(g)] + t_ref[g].astype(F32)).astype(BF)

        each(PARTS, lambda p: copy(p).start())
        each(PARTS, work)

    (out,) = order.run(
        body,
        "add_rows",
        (policy, in_vmem(tiles)),
        [HBM, VMEM],
        [tiles_out(QUARTER)],
        [VMEM],
        [pltpu.VMEM((QUARTER, D), F32), pltpu.SemaphoreType.DMA((PARTS,))],
    )
    return out


def pick_and_cast(order, anchor, policy):
    def body(at, a_ref, x_ref, p_ref, o_ref, held, wide, in_sems, out_sems, x_sems):
        rows = [member_row(at, (True, True, 0), xh) for xh in range(2)]
        mine = pl.ds(first_row(at, False, True, 0), QUARTER)

        def fetch(p, xh):
            some = pl.ds(4 * p, 4)
            return pltpu.make_async_copy(
                a_ref.at[some, xh, pl.ds(rows[xh], QUARTER), :], held.at[some, xh], in_sems.at[xh, p]
            )

        def store(p, xh):
            some = pl.ds(4 * p, 4)
            return pltpu.make_async_copy(held.at[some, xh], p_ref.at[some, xh], out_sems.at[xh, p])

        def copy(p):
            return pltpu.make_async_copy(x_ref.at[mine, span_of(p)], wide.at[:, span_of(p)], x_sems.at[p])

        def forward(p, xh):
            fetch(p, xh).wait()
            store(p, xh).start()

        def work(p):
            copy(p).wait()
            for k in range(PER):
                g = p * PER + k
                o_ref[g] = wide[:, columns(g)].astype(BF)

        for xh in range(2):
            each(4, lambda p, xh=xh: fetch(p, xh).start())
        each(PARTS, lambda p: copy(p).start())
        for xh in range(2):
            each(4, lambda p, xh=xh: forward(p, xh))
        each(PARTS, work)
        for xh in range(2):
            each(4, lambda p, xh=xh: store(p, xh).wait())

    picked, cast = order.run(
        body,
        "pick_and_cast",
        (anchor, policy),
        [HBM, HBM],
        [pltpu.HBM((16, 2, QUARTER, WIDTH), BF), tiles_out(QUARTER)],
        [HBM, VMEM],
        [
            pltpu.VMEM((16, 2, QUARTER, WIDTH), BF),
            pltpu.VMEM((QUARTER, D), F32),
            pltpu.SemaphoreType.DMA((2, 4)),
            pltpu.SemaphoreType.DMA((2, 4)),
            pltpu.SemaphoreType.DMA((PARTS,)),
        ],
    )
    return picked.reshape(SHARDS, QUARTER, WIDTH), cast


def add_tiles(order, a, b, size):
    def body(at, a_ref, b_ref, o_ref):
        def work(g):
            o_ref[g] = (a_ref[g].astype(F32) + b_ref[g].astype(F32)).astype(BF)

        each(SHARDS, work)

    args = [in_vmem(a), in_vmem(b)]
    (out,) = order.run(body, "add_tiles", args, [VMEM] * 2, [tiles_out(a.shape[1])], [VMEM], [], size=size)
    return out


def blend_rows(order, total, anchor):
    def body(at, t_ref, a_ref, o_ref, held, sems):
        def store(p):
            some = pl.ds(p * PER, PER)
            return pltpu.make_async_copy(held.at[some], o_ref.at[some], sems.at[p])

        def work(p):
            for k in range(PER):
                g = p * PER + k
                average = t_ref[g].astype(F32) / 4
                held[g] = ((1.0 - blend_rate) * a_ref[g].astype(F32) + blend_rate * average).astype(BF)
            store(p).start()

        each(PARTS, work)
        each(PARTS, lambda p: store(p).wait())

    args = [in_vmem(total), in_vmem(anchor)]
    (out,) = order.run(
        body,
        "blend_rows",
        args,
        [VMEM] * 2,
        [pltpu.HBM((SHARDS, QUARTER, WIDTH), BF)],
        [HBM],
        [pltpu.VMEM((SHARDS, QUARTER, WIDTH), BF), pltpu.SemaphoreType.DMA((PARTS,))],
    )
    return out


def split_rows(order, finished, back):
    def body(at, f_ref, b_ref, first_ref, second_ref, low_ref, high_ref, held, sems):
        def store(p):
            some = pl.ds(p * PER, PER)
            return pltpu.make_async_copy(held.at[some], first_ref.at[some], sems.at[p])

        def work(p):
            for k in range(PER):
                held[p * PER + k] = f_ref[p * PER + k, :R]
            store(p).start()

        def others(g):
            low_ref[g] = b_ref[g, :R]
            high_ref[g] = b_ref[g, R:]
            second_ref[g] = f_ref[g, R:]

        each(PARTS, work)
        each(SHARDS, others)
        each(PARTS, lambda p: store(p).wait())

    return order.run(
        body,
        "split_rows",
        [in_vmem(finished), in_vmem(back)],
        [VMEM] * 2,
        [pltpu.HBM((SHARDS, R, WIDTH), BF), tiles_out(R), tiles_out(R), tiles_out(R)],
        [HBM, VMEM, VMEM, VMEM],
        [pltpu.VMEM((SHARDS, R, WIDTH), BF), pltpu.SemaphoreType.DMA((PARTS,))],
    )


def copy_tiles(order, tiles):
    def body(at, x_ref, o_ref):
        def work(g):
            o_ref[g] = x_ref[g]

        each(SHARDS, work)

    (out,) = order.run(body, "copy_tiles", [in_vmem(tiles)], [VMEM], [tiles_out(R)], [VMEM], [])
    return out


def widen_rows(order, pieces, blended, size=1024):
    n = len(pieces)
    rows = [tiles.shape[1] for tiles, _ in pieces]

    def body(at, *refs):
        tiles, out_ref, wide, sems = refs[:n], refs[-3], refs[-2], refs[-1]

        def copy(i, p):
            span = pl.ds(pl.multiple_of(p * PER * WIDTH, WIDTH), PER * WIDTH)
            held = pl.ds(first_row(at, *pieces[i][1]), rows[i])
            return pltpu.make_async_copy(
                wide.at[i, pl.ds(0, rows[i]), span], out_ref.at[held, span], sems.at[i, p]
            )

        def work(i, p):
            for k in range(PER):
                g = p * PER + k
                wide[i, : rows[i], columns(g)] = tiles[i][g].astype(F32)
            copy(i, p).start()

        for i in range(n):
            each(PARTS, lambda p, i=i: work(i, p))
        for i in range(n):
            each(PARTS, lambda p, i=i: copy(i, p).wait())

    earlier = [] if blended is None else [blended]
    (out,) = order.run(
        body,
        "widen_rows",
        [in_vmem(tiles) for tiles, _ in pieces] + earlier,
        [VMEM] * n + [HBM] * len(earlier),
        [pltpu.HBM((ROWS, D), F32)],
        [HBM],
        [pltpu.VMEM((n, max(rows), D), F32), pltpu.SemaphoreType.DMA((n, PARTS))],
        {n + 1: 0} if earlier else {},
        size,
    )
    return out


def place_rows(order, pieces, anchor, size=1024):
    n = len(pieces)
    rows = [tiles.shape[1] for tiles, _ in pieces]

    def body(at, *refs):
        tiles, out_ref, sems = refs[:n], refs[-2], refs[-1]

        def copy(i, xh, p):
            some = pl.ds(8 * p, 8)
            held = pl.ds(member_row(at, pieces[i][1], xh), rows[i])
            return pltpu.make_async_copy(
                tiles[i].at[some, xh], out_ref.at[some, xh, held, :], sems.at[i, xh, p]
            )

        both = [(i, xh) for i in range(n) for xh in range(2)]
        for i, xh in both:
            each(2, lambda p, i=i, xh=xh: copy(i, xh, p).start())
        for i, xh in both:
            each(2, lambda p, i=i, xh=xh: copy(i, xh, p).wait())

    earlier = [] if anchor is None else [anchor]
    (out,) = order.run(
        body,
        "place_rows",
        [in_vmem(t.reshape(16, 2, r, WIDTH)) for (t, _), r in zip(pieces, rows)] + earlier,
        [VMEM] * n + [HBM] * len(earlier),
        [pltpu.HBM((16, 2, ROWS, WIDTH), BF)],
        [HBM],
        [pltpu.SemaphoreType.DMA((n, 2, 2))],
        {n + 1: 0} if earlier else {},
        size,
    )
    return out


def per_device(policies, anchor):
    policy = pltpu.with_memory_space_constraint(policies[0], pltpu.HBM)
    shards = pltpu.with_memory_space_constraint(anchor.reshape(16, 2, ROWS, WIDTH), pltpu.HBM)
    order = Order(jnp.stack([lax.axis_index(name) for name in ("xl", "c", "xh")]).astype(jnp.int32))
    swap = [(0, 1), (1, 0)]
    groups = exchange_groups()

    def exchange(tiles):
        return lax.all_to_all(
            tiles, AXES, split_axis=0, concat_axis=0, axis_index_groups=groups, tiled=True
        )

    def core(tiles):
        return lax.ppermute(tiles, "c", swap)

    def chip(tiles):
        return lax.ppermute(tiles, "xl", swap)

    theirs = core(cast_rows(order, policy))
    picked, own = pick_and_cast(order, shards, policy)
    own = core(own)
    other = chip(add_theirs(order, policy, theirs))
    fetched = exchange(picked)
    own = add_rows(order, policy, own)

    own = add_tiles(order, own, other, SUM_COST)
    own = blend_rows(order, own, fetched)
    finished = chip(own)
    back = exchange(own)
    pieces = [(own, (True, True, 0)), (core(own), (False, True, 0))]
    blended = widen_rows(order, pieces, None, WRITE_COST)

    first, second, *back = split_rows(order, finished, back)
    back_first = exchange(first)
    back_second = chip(back[1])
    pieces = []
    for j, tiles in enumerate(back):
        pieces += [(tiles, (True, True, j * R)), (core(tiles), (False, True, j * R))]
    new_anchor = place_rows(order, pieces, None)
    pieces = []
    for j, tiles in enumerate((first, second)):
        pieces += [(tiles, (True, False, j * R)), (core(tiles), (False, False, j * R))]
    blended = widen_rows(order, pieces, blended)
    new_anchor = place_rows(order, [(back_second, (True, False, R))], new_anchor)
    back_first = copy_tiles(order, back_first)
    pieces = [(back_first, (True, False, 0)), (core(back_second), (False, False, R))]
    new_anchor = place_rows(order, pieces, new_anchor, LAST_COST)
    new_anchor = place_rows(order, [(core(back_first), (False, False, 0))], new_anchor)
    return blended, new_anchor.reshape(SHARDS * ROWS, WIDTH)


def solution(mesh):
    fine = Mesh(mesh.devices.reshape(SIZES), AXES)
    shards = ("y", "z", "xh")
    return jax.shard_map(
        per_device,
        mesh=fine,
        in_specs=(P(("xl", "c"), shards, None), P(None, shards)),
        out_specs=(P(shards, None), P(None, shards)),
        check_vma=False,
    )
```

```python
import jax
import jax.numpy as jnp
import numpy as np
from jax import lax
from jax.experimental import pallas as pl
from jax.experimental.pallas import tpu as pltpu
from jax.sharding import Mesh, PartitionSpec as P

blend_rate = 0.3

AXES = ("xl", "c", "y", "z", "xh")
SIZES = (2, 2, 4, 4, 2)
SHARDS = 32
ROWS = 256
WIDTH = 256
D = 8192
HALF = 128
QUARTER = 64
R = 32
BF = jnp.bfloat16
F32 = jnp.float32
VMEM_LIMIT = 10 << 20
PARTS = 8
PER = SHARDS // PARTS
WRITE_COST = 11 << 20
LAST_COST = 37 << 20
ANY = pl.BlockSpec(memory_space=pl.ANY)
HBM = pl.BlockSpec(memory_space=pltpu.HBM)
VMEM = pl.BlockSpec(memory_space=pltpu.VMEM)
TOKEN = jax.ShapeDtypeStruct((8, 128), jnp.int32)


def exchange_groups():
    ids = np.arange(128).reshape(SIZES)
    return [
        [int(ids[flip ^ xh, c, y, z, xh]) for y in range(4) for z in range(4) for xh in range(2)]
        for flip in range(2)
        for c in range(2)
    ]


def in_vmem(x):
    return pltpu.with_memory_space_constraint(x, pltpu.VMEM)


class Order:
    def __init__(self, place):
        self.place = place
        self.token = None

    def run(self, body, name, args, specs, outs, out_specs, scratch, aliases=None, size=1024):
        held = [] if self.token is None else [self.token]

        def ordered(at, *refs):
            ins, rest = refs[: len(args)], refs[len(args) + len(held) :]
            results, others = rest[: len(outs)], rest[len(outs) + 1 :]
            body(at, *ins, *results, *others)

        *results, self.token = pl.pallas_call(
            ordered,
            out_shape=[*outs, TOKEN],
            grid_spec=pltpu.PrefetchScalarGridSpec(
                num_scalar_prefetch=1,
                grid=(),
                in_specs=[*specs, *[ANY] * len(held)],
                out_specs=[*out_specs, ANY],
                scratch_shapes=scratch,
            ),
            input_output_aliases=aliases or {},
            compiler_params=pltpu.CompilerParams(vmem_limit_bytes=VMEM_LIMIT),
            cost_estimate=pl.CostEstimate(flops=0, bytes_accessed=size, transcendentals=0),
            name=name,
        )(self.place, *args, *held)
        return results


def columns(g):
    return pl.ds(pl.multiple_of(g * WIDTH, WIDTH), WIDTH)


def each(count, work):
    pl.loop(0, count)(work)


def first_row(at, core, chip, start, xl=None):
    xl = at[0] if xl is None else xl
    half = at[1] if core else 1 - at[1]
    quarter = xl if chip else 1 - xl
    return pl.multiple_of(half * HALF + quarter * QUARTER + start, 16)


def member_row(at, where, xh):
    differs = at[2] if xh == 0 else 1 - at[2]
    return first_row(at, *where, at[0] + differs - 2 * at[0] * differs)


def tiles_out(rows):
    return pltpu.VMEM((SHARDS, rows, WIDTH), BF)


def span_of(p):
    return pl.ds(pl.multiple_of(p * PER * WIDTH, WIDTH), PER * WIDTH)


def cast_rows(order, policy):
    def body(at, x_ref, o_ref, wide, sems):
        held = pl.ds(first_row(at, False, False, 0), QUARTER)

        def copy(p):
            return pltpu.make_async_copy(x_ref.at[held, span_of(p)], wide.at[:, span_of(p)], sems.at[p])

        def work(p):
            copy(p).wait()
            for k in range(PER):
                g = p * PER + k
                o_ref[g] = wide[:, columns(g)].astype(BF)

        each(PARTS, lambda p: copy(p).start())
        each(PARTS, work)

    (out,) = order.run(
        body,
        "cast_rows",
        (policy,),
        [HBM],
        [tiles_out(QUARTER)],
        [VMEM],
        [pltpu.VMEM((QUARTER, D), F32), pltpu.SemaphoreType.DMA((PARTS,))],
    )
    return out


def add_theirs(order, policy, tiles):
    def body(at, x_ref, t_ref, o_ref, wide, held, in_sems, out_sems):
        rows = pl.ds(first_row(at, True, False, 0), QUARTER)

        def fetch(p):
            return pltpu.make_async_copy(x_ref.at[rows, span_of(p)], wide.at[:, span_of(p)], in_sems.at[p])

        def store(p):
            some = pl.ds(p * PER, PER)
            return pltpu.make_async_copy(held.at[some], o_ref.at[some], out_sems.at[p])

        def work(p):
            fetch(p).wait()
            for k in range(PER):
                g = p * PER + k
                held[g] = (wide[:, columns(g)] + t_ref[g].astype(F32)).astype(BF)
            store(p).start()

        each(PARTS, lambda p: fetch(p).start())
        each(PARTS, work)
        each(PARTS, lambda p: store(p).wait())

    (out,) = order.run(
        body,
        "add_theirs",
        (policy, in_vmem(tiles)),
        [HBM, VMEM],
        [pltpu.HBM((SHARDS, QUARTER, WIDTH), BF)],
        [HBM],
        [
            pltpu.VMEM((QUARTER, D), F32),
            pltpu.VMEM((SHARDS, QUARTER, WIDTH), BF),
            pltpu.SemaphoreType.DMA((PARTS,)),
            pltpu.SemaphoreType.DMA((PARTS,)),
        ],
    )
    return out


def cast_own(order, policy):
    def body(at, x_ref, low_ref, high_ref, wide, sems):
        held = pl.ds(first_row(at, False, True, 0), QUARTER)

        def copy(p):
            return pltpu.make_async_copy(x_ref.at[held, span_of(p)], wide.at[:, span_of(p)], sems.at[p])

        def work(p):
            copy(p).wait()
            for k in range(PER):
                g = p * PER + k
                low_ref[g] = wide[:R, columns(g)].astype(BF)
                high_ref[g] = wide[R:, columns(g)].astype(BF)

        each(PARTS, lambda p: copy(p).start())
        each(PARTS, work)

    return order.run(
        body,
        "cast_own",
        (policy,),
        [HBM],
        [tiles_out(R)] * 2,
        [VMEM] * 2,
        [pltpu.VMEM((QUARTER, D), F32), pltpu.SemaphoreType.DMA((PARTS,))],
    )


def add_own(order, policy, chunks):
    def body(at, x_ref, low_ref, high_ref, o_ref, wide, sems):
        held = pl.ds(first_row(at, True, True, 0), QUARTER)

        def copy(p):
            return pltpu.make_async_copy(x_ref.at[held, span_of(p)], wide.at[:, span_of(p)], sems.at[p])

        def work(p):
            copy(p).wait()
            for k in range(PER):
                g = p * PER + k
                o_ref[g, :R] = (wide[:R, columns(g)] + low_ref[g].astype(F32)).astype(BF)
                o_ref[g, R:] = (wide[R:, columns(g)] + high_ref[g].astype(F32)).astype(BF)

        each(PARTS, lambda p: copy(p).start())
        each(PARTS, work)

    (out,) = order.run(
        body,
        "add_own",
        (policy, *[in_vmem(tiles) for tiles in chunks]),
        [HBM, VMEM, VMEM],
        [tiles_out(QUARTER)],
        [VMEM],
        [pltpu.VMEM((QUARTER, D), F32), pltpu.SemaphoreType.DMA((PARTS,))],
    )
    return out


def pick_rows(order, anchor):
    def body(at, a_ref, p_ref, held, in_sems, out_sems):
        rows = [member_row(at, (True, True, 0), xh) for xh in range(2)]

        def fetch(p, xh):
            some = pl.ds(4 * p, 4)
            return pltpu.make_async_copy(
                a_ref.at[some, xh, pl.ds(rows[xh], QUARTER), :], held.at[some, xh], in_sems.at[xh, p]
            )

        def store(p, xh):
            some = pl.ds(4 * p, 4)
            return pltpu.make_async_copy(held.at[some, xh], p_ref.at[some, xh], out_sems.at[xh, p])

        def forward(p, xh):
            fetch(p, xh).wait()
            store(p, xh).start()

        for xh in range(2):
            each(4, lambda p, xh=xh: fetch(p, xh).start())
        for xh in range(2):
            each(4, lambda p, xh=xh: forward(p, xh))
        for xh in range(2):
            each(4, lambda p, xh=xh: store(p, xh).wait())

    (picked,) = order.run(
        body,
        "pick_rows",
        (anchor,),
        [HBM],
        [pltpu.HBM((16, 2, QUARTER, WIDTH), BF)],
        [HBM],
        [
            pltpu.VMEM((16, 2, QUARTER, WIDTH), BF),
            pltpu.SemaphoreType.DMA((2, 4)),
            pltpu.SemaphoreType.DMA((2, 4)),
        ],
    )
    return picked.reshape(SHARDS, QUARTER, WIDTH)


def blend_rows(order, own, other, anchor):
    def body(at, x_ref, t_ref, a_ref, o_ref, held, sems):
        def store(p):
            some = pl.ds(p * PER, PER)
            return pltpu.make_async_copy(held.at[some], o_ref.at[some], sems.at[p])

        def work(p):
            for k in range(PER):
                g = p * PER + k
                average = (x_ref[g].astype(F32) + t_ref[g].astype(F32)) / 4
                held[g] = ((1.0 - blend_rate) * a_ref[g].astype(F32) + blend_rate * average).astype(BF)
            store(p).start()

        each(PARTS, work)
        each(PARTS, lambda p: store(p).wait())

    (out,) = order.run(
        body,
        "blend_rows",
        [in_vmem(x) for x in (own, other, anchor)],
        [VMEM] * 3,
        [pltpu.HBM((SHARDS, QUARTER, WIDTH), BF)],
        [HBM],
        [pltpu.VMEM((SHARDS, QUARTER, WIDTH), BF), pltpu.SemaphoreType.DMA((PARTS,))],
    )
    return out


def split_back(order, back):
    def body(at, b_ref, low_ref, high_ref):
        def work(g):
            high_ref[g] = b_ref[g, R:]
            low_ref[g] = b_ref[g, :R]

        each(SHARDS, work)

    return order.run(
        body, "split_back", [in_vmem(back)], [VMEM], [tiles_out(R)] * 2, [VMEM] * 2, []
    )


def split_finished(order, finished):
    def body(at, f_ref, first_ref, second_ref, sems):
        def store(p):
            some = pl.ds(p * PER, PER)
            return pltpu.make_async_copy(f_ref.at[some, pl.ds(0, R)], first_ref.at[some], sems.at[p])

        def work(g):
            second_ref[g] = f_ref[g, R:]

        each(PARTS, lambda p: store(p).start())
        each(SHARDS, work)
        each(PARTS, lambda p: store(p).wait())

    return order.run(
        body,
        "split_finished",
        [in_vmem(finished)],
        [VMEM],
        [pltpu.HBM((SHARDS, R, WIDTH), BF), tiles_out(R)],
        [HBM, VMEM],
        [pltpu.SemaphoreType.DMA((PARTS,))],
    )


def copy_tiles(order, tiles):
    def body(at, x_ref, o_ref):
        def work(g):
            o_ref[g] = x_ref[g]

        each(SHARDS, work)

    (out,) = order.run(body, "copy_tiles", [in_vmem(tiles)], [VMEM], [tiles_out(R)], [VMEM], [])
    return out


def write_rows(order, wide_pieces, placed_pieces, blended, anchor, size=1024):
    n, m = len(wide_pieces), len(placed_pieces)
    rows = [tiles.shape[1] for tiles, _ in wide_pieces]
    placed_rows = [tiles.shape[1] for tiles, _ in placed_pieces]
    outs = [pltpu.HBM((ROWS, D), F32)] * (n > 0) + [pltpu.HBM((16, 2, ROWS, WIDTH), BF)] * (m > 0)
    earlier = [x for x, k in ((blended, n), (anchor, m)) if k and x is not None]
    tops = max(rows, default=16)

    def body(at, *refs):
        tiles, refs = refs[:n], refs[n:]
        placed, refs = refs[:m], refs[m + len(earlier) :]
        out_refs, (wide, held, sems, placed_sems, held_sem) = refs[: len(outs)], refs[len(outs) :]

        def place(i, xh, p):
            some = pl.ds(8 * p, 8)
            there = pl.ds(member_row(at, placed_pieces[i][1], xh), placed_rows[i])
            return pltpu.make_async_copy(
                placed[i].at[some, xh], out_refs[-1].at[some, xh, there, :], placed_sems.at[i, xh, p]
            )

        def copy(i, p):
            some = pl.ds(0, rows[i])
            there = pl.ds(first_row(at, *wide_pieces[i][1]), rows[i])
            return pltpu.make_async_copy(
                wide.at[i, some, span_of(p)], out_refs[0].at[there, span_of(p)], sems.at[i, p]
            )

        def work(i, ref, p):
            for k in range(PER):
                g = p * PER + k
                wide[i, : rows[i], columns(g)] = ref[g].astype(F32)
            copy(i, p).start()

        both = [(i, xh) for i in range(m) for xh in range(2)]
        if n:
            last = pltpu.make_async_copy(tiles[-1], held, held_sem)
            last.start()
        for i, xh in both:
            each(2, lambda p, i=i, xh=xh: place(i, xh, p).start())
        for i in range(n):
            if i == n - 1:
                last.wait()
            each(PARTS, lambda p, i=i: work(i, held if i == n - 1 else tiles[i], p))
        for i in range(n):
            each(PARTS, lambda p, i=i: copy(i, p).wait())
        for i, xh in both:
            each(2, lambda p, i=i, xh=xh: place(i, xh, p).wait())

    args = [in_vmem(t) for t, _ in wide_pieces[:-1]]
    args += [pltpu.with_memory_space_constraint(t, pltpu.HBM) for t, _ in wide_pieces[-1:]]
    args += [in_vmem(t.reshape(16, 2, r, WIDTH)) for (t, _), r in zip(placed_pieces, placed_rows)]
    specs = [VMEM] * (n - 1) + [HBM] * (n > 0) + [VMEM] * m
    return order.run(
        body,
        "write_rows",
        args + earlier,
        specs + [HBM] * len(earlier),
        outs,
        [HBM] * len(outs),
        [
            pltpu.VMEM((max(n, 1), tops, D if n else 128), F32),
            pltpu.VMEM((SHARDS, rows[-1] if n else 16, WIDTH), BF),
            pltpu.SemaphoreType.DMA((max(n, 1), PARTS)),
            pltpu.SemaphoreType.DMA((max(m, 1), 2, 2)),
            pltpu.SemaphoreType.DMA,
        ],
        {n + m + 1 + k: k for k in range(len(earlier))},
        size,
    )


def per_device(policies, anchor):
    policy = pltpu.with_memory_space_constraint(policies[0], pltpu.HBM)
    shards = pltpu.with_memory_space_constraint(anchor.reshape(16, 2, ROWS, WIDTH), pltpu.HBM)
    order = Order(jnp.stack([lax.axis_index(name) for name in ("xl", "c", "xh")]).astype(jnp.int32))
    swap = [(0, 1), (1, 0)]
    groups = exchange_groups()

    def exchange(tiles):
        return lax.all_to_all(
            tiles, AXES, split_axis=0, concat_axis=0, axis_index_groups=groups, tiled=True
        )

    def core(tiles):
        return lax.ppermute(tiles, "c", swap)

    def chip(tiles):
        return lax.ppermute(tiles, "xl", swap)

    theirs = core(cast_rows(order, policy))
    picked = pick_rows(order, shards)
    other = chip(add_theirs(order, policy, theirs))
    fetched = exchange(picked)
    own = add_own(order, policy, [core(tiles) for tiles in cast_own(order, policy)])

    own = blend_rows(order, own, other, fetched)
    finished = chip(own)
    back = exchange(own)
    pieces = [(core(own), (False, True, 0)), (own, (True, True, 0))]
    (blended,) = write_rows(order, pieces, [], None, None, WRITE_COST)

    back = split_back(order, back)
    first, second = split_finished(order, finished)
    back_first = exchange(first)
    back_second = chip(back[1])
    pieces = []
    for j, tiles in enumerate(back):
        pieces += [(tiles, (True, True, j * R)), (core(tiles), (False, True, j * R))]
    (new_anchor,) = write_rows(order, [], pieces, None, None)
    pieces = []
    for j, tiles in ((1, second), (0, first)):
        pieces += [(core(tiles), (False, False, j * R)), (tiles, (True, False, j * R))]
    blended, new_anchor = write_rows(
        order, pieces, [(back_second, (True, False, R))], blended, new_anchor
    )
    back_first = copy_tiles(order, back_first)
    pieces = [(back_first, (True, False, 0)), (core(back_second), (False, False, R))]
    (new_anchor,) = write_rows(order, [], pieces, None, new_anchor, LAST_COST)
    pieces = [(core(back_first), (False, False, 0))]
    (new_anchor,) = write_rows(order, [], pieces, None, new_anchor)
    return blended, new_anchor.reshape(SHARDS * ROWS, WIDTH)


def solution(mesh):
    fine = Mesh(mesh.devices.reshape(SIZES), AXES)
    shards = ("y", "z", "xh")
    return jax.shard_map(
        per_device,
        mesh=fine,
        in_specs=(P(("xl", "c"), shards, None), P(None, shards)),
        out_specs=(P(shards, None), P(None, shards)),
        check_vma=False,
    )
```

```python
import jax
import jax.numpy as jnp
import numpy as np
from jax import lax
from jax.experimental import pallas as pl
from jax.experimental.pallas import tpu as pltpu
from jax.sharding import Mesh, PartitionSpec as P

blend_rate = 0.3

AXES = ("xl", "c", "y", "z", "xh")
SIZES = (2, 2, 4, 4, 2)
SHARDS = 32
ROWS = 256
WIDTH = 256
D = 8192
HALF = 128
QUARTER = 64
R = 32
BF = jnp.bfloat16
F32 = jnp.float32
VMEM_LIMIT = 10 << 20
PARTS = 8
PER = SHARDS // PARTS
WRITE_COST = 11 << 20
LAST_COST = 37 << 20
ANY = pl.BlockSpec(memory_space=pl.ANY)
HBM = pl.BlockSpec(memory_space=pltpu.HBM)
VMEM = pl.BlockSpec(memory_space=pltpu.VMEM)
TOKEN = jax.ShapeDtypeStruct((8, 128), jnp.int32)


def exchange_groups():
    ids = np.arange(128).reshape(SIZES)
    return [
        [int(ids[flip ^ xh, c, y, z, xh]) for y in range(4) for z in range(4) for xh in range(2)]
        for flip in range(2)
        for c in range(2)
    ]


def in_vmem(x):
    return pltpu.with_memory_space_constraint(x, pltpu.VMEM)


class Order:
    def __init__(self, place):
        self.place = place
        self.token = None

    def run(self, body, name, args, specs, outs, out_specs, scratch, aliases=None, size=1024):
        held = [] if self.token is None else [self.token]

        def ordered(at, *refs):
            ins, rest = refs[: len(args)], refs[len(args) + len(held) :]
            results, others = rest[: len(outs)], rest[len(outs) + 1 :]
            body(at, *ins, *results, *others)

        *results, self.token = pl.pallas_call(
            ordered,
            out_shape=[*outs, TOKEN],
            grid_spec=pltpu.PrefetchScalarGridSpec(
                num_scalar_prefetch=1,
                grid=(),
                in_specs=[*specs, *[ANY] * len(held)],
                out_specs=[*out_specs, ANY],
                scratch_shapes=scratch,
            ),
            input_output_aliases=aliases or {},
            compiler_params=pltpu.CompilerParams(vmem_limit_bytes=VMEM_LIMIT),
            cost_estimate=pl.CostEstimate(flops=0, bytes_accessed=size, transcendentals=0),
            name=name,
        )(self.place, *args, *held)
        return results


def columns(g):
    return pl.ds(pl.multiple_of(g * WIDTH, WIDTH), WIDTH)


def each(count, work):
    pl.loop(0, count)(work)


def first_row(at, core, chip, start, xl=None):
    xl = at[0] if xl is None else xl
    half = at[1] if core else 1 - at[1]
    quarter = xl if chip else 1 - xl
    return pl.multiple_of(half * HALF + quarter * QUARTER + start, 16)


def member_row(at, where, xh):
    differs = at[2] if xh == 0 else 1 - at[2]
    return first_row(at, *where, at[0] + differs - 2 * at[0] * differs)


def tiles_out(rows):
    return pltpu.VMEM((SHARDS, rows, WIDTH), BF)


def span_of(p):
    return pl.ds(pl.multiple_of(p * PER * WIDTH, WIDTH), PER * WIDTH)


def cast_rows(order, policy):
    def body(at, x_ref, o_ref, wide, sems):
        held = pl.ds(first_row(at, False, False, 0), QUARTER)

        def copy(p):
            return pltpu.make_async_copy(x_ref.at[held, span_of(p)], wide.at[:, span_of(p)], sems.at[p])

        def work(p):
            copy(p).wait()
            for k in range(PER):
                g = p * PER + k
                o_ref[g] = wide[:, columns(g)].astype(BF)

        each(PARTS, lambda p: copy(p).start())
        each(PARTS, work)

    (out,) = order.run(
        body,
        "cast_rows",
        (policy,),
        [HBM],
        [tiles_out(QUARTER)],
        [VMEM],
        [pltpu.VMEM((QUARTER, D), F32), pltpu.SemaphoreType.DMA((PARTS,))],
    )
    return out


def add_theirs(order, policy, tiles):
    def body(at, x_ref, t_ref, o_ref, wide, held, in_sems, out_sems):
        rows = pl.ds(first_row(at, True, False, 0), QUARTER)

        def fetch(p):
            return pltpu.make_async_copy(x_ref.at[rows, span_of(p)], wide.at[:, span_of(p)], in_sems.at[p])

        def store(p):
            some = pl.ds(p * PER, PER)
            return pltpu.make_async_copy(held.at[some], o_ref.at[some], out_sems.at[p])

        def work(p):
            fetch(p).wait()
            for k in range(PER):
                g = p * PER + k
                held[g] = (wide[:, columns(g)] + t_ref[g].astype(F32)).astype(BF)
            store(p).start()

        each(PARTS, lambda p: fetch(p).start())
        each(PARTS, work)
        each(PARTS, lambda p: store(p).wait())

    (out,) = order.run(
        body,
        "add_theirs",
        (policy, in_vmem(tiles)),
        [HBM, VMEM],
        [pltpu.HBM((SHARDS, QUARTER, WIDTH), BF)],
        [HBM],
        [
            pltpu.VMEM((QUARTER, D), F32),
            pltpu.VMEM((SHARDS, QUARTER, WIDTH), BF),
            pltpu.SemaphoreType.DMA((PARTS,)),
            pltpu.SemaphoreType.DMA((PARTS,)),
        ],
    )
    return out


def cast_own(order, policy):
    def body(at, x_ref, low_ref, high_ref, wide, sems):
        held = pl.ds(first_row(at, False, True, 0), QUARTER)

        def copy(p):
            return pltpu.make_async_copy(x_ref.at[held, span_of(p)], wide.at[:, span_of(p)], sems.at[p])

        def work(p):
            copy(p).wait()
            for k in range(PER):
                g = p * PER + k
                low_ref[g] = wide[:R, columns(g)].astype(BF)
                high_ref[g] = wide[R:, columns(g)].astype(BF)

        each(PARTS, lambda p: copy(p).start())
        each(PARTS, work)

    return order.run(
        body,
        "cast_own",
        (policy,),
        [HBM],
        [tiles_out(R)] * 2,
        [VMEM] * 2,
        [pltpu.VMEM((QUARTER, D), F32), pltpu.SemaphoreType.DMA((PARTS,))],
    )


def add_own(order, policy, chunks):
    def body(at, x_ref, low_ref, high_ref, o_ref, wide, sems):
        held = pl.ds(first_row(at, True, True, 0), QUARTER)

        def copy(p):
            return pltpu.make_async_copy(x_ref.at[held, span_of(p)], wide.at[:, span_of(p)], sems.at[p])

        def work(p):
            copy(p).wait()
            for k in range(PER):
                g = p * PER + k
                o_ref[g, :R] = (wide[:R, columns(g)] + low_ref[g].astype(F32)).astype(BF)
                o_ref[g, R:] = (wide[R:, columns(g)] + high_ref[g].astype(F32)).astype(BF)

        each(PARTS, lambda p: copy(p).start())
        each(PARTS, work)

    (out,) = order.run(
        body,
        "add_own",
        (policy, *[in_vmem(tiles) for tiles in chunks]),
        [HBM, VMEM, VMEM],
        [tiles_out(QUARTER)],
        [VMEM],
        [pltpu.VMEM((QUARTER, D), F32), pltpu.SemaphoreType.DMA((PARTS,))],
    )
    return out


def pick_rows(order, anchor):
    def body(at, a_ref, p_ref, held, in_sems, out_sems):
        rows = [member_row(at, (True, True, 0), xh) for xh in range(2)]

        def fetch(p, xh):
            some = pl.ds(4 * p, 4)
            return pltpu.make_async_copy(
                a_ref.at[some, xh, pl.ds(rows[xh], QUARTER), :], held.at[some, xh], in_sems.at[xh, p]
            )

        def store(p, xh):
            some = pl.ds(4 * p, 4)
            return pltpu.make_async_copy(held.at[some, xh], p_ref.at[some, xh], out_sems.at[xh, p])

        def forward(p, xh):
            fetch(p, xh).wait()
            store(p, xh).start()

        for xh in range(2):
            each(4, lambda p, xh=xh: fetch(p, xh).start())
        for xh in range(2):
            each(4, lambda p, xh=xh: forward(p, xh))
        for xh in range(2):
            each(4, lambda p, xh=xh: store(p, xh).wait())

    (picked,) = order.run(
        body,
        "pick_rows",
        (anchor,),
        [HBM],
        [pltpu.HBM((16, 2, QUARTER, WIDTH), BF)],
        [HBM],
        [
            pltpu.VMEM((16, 2, QUARTER, WIDTH), BF),
            pltpu.SemaphoreType.DMA((2, 4)),
            pltpu.SemaphoreType.DMA((2, 4)),
        ],
    )
    return picked.reshape(SHARDS, QUARTER, WIDTH)


def blend_rows(order, own, other, anchor):
    def body(at, x_ref, t_ref, a_ref, o_ref, held, sems):
        def store(p):
            some = pl.ds(p * PER, PER)
            return pltpu.make_async_copy(held.at[some], o_ref.at[some], sems.at[p])

        def work(p):
            for k in range(PER):
                g = p * PER + k
                average = (x_ref[g].astype(F32) + t_ref[g].astype(F32)) / 4
                held[g] = ((1.0 - blend_rate) * a_ref[g].astype(F32) + blend_rate * average).astype(BF)
            store(p).start()

        each(PARTS, work)
        each(PARTS, lambda p: store(p).wait())

    (out,) = order.run(
        body,
        "blend_rows",
        [in_vmem(x) for x in (own, other, anchor)],
        [VMEM] * 3,
        [pltpu.HBM((SHARDS, QUARTER, WIDTH), BF)],
        [HBM],
        [pltpu.VMEM((SHARDS, QUARTER, WIDTH), BF), pltpu.SemaphoreType.DMA((PARTS,))],
    )
    return out


def plane(at, same):
    return at[2] if same else 1 - at[2]


def split_planes(order, finished, back):
    def body(at, f_ref, b_ref, first_ref, low_ref, second_ref, high_ref, sems):
        def stores(p):
            some = pl.ds(4 * p, 4)
            ends = ((f_ref, first_ref), (b_ref, low_ref))
            return [
                pltpu.make_async_copy(x.at[some, plane(at, True)], o.at[some], sems.at[i, p])
                for i, (x, o) in enumerate(ends)
            ]

        def start(p):
            for store in stores(p):
                store.start()

        def work(k):
            high_ref[k] = b_ref[k, plane(at, False)]
            second_ref[k] = f_ref[k, plane(at, False)]

        def finish(p):
            for store in stores(p):
                store.wait()

        each(4, start)
        each(16, work)
        each(4, finish)

    half = (16, QUARTER, WIDTH)
    return order.run(
        body,
        "split_planes",
        [in_vmem(x.reshape(16, 2, QUARTER, WIDTH)) for x in (finished, back)],
        [VMEM, VMEM],
        [pltpu.HBM(half, BF), jax.ShapeDtypeStruct(half, BF), pltpu.VMEM(half, BF), pltpu.VMEM(half, BF)],
        [HBM, ANY, VMEM, VMEM],
        [pltpu.SemaphoreType.DMA((2, 4))],
    )


def copy_tiles(order, tiles):
    def body(at, x_ref, o_ref):
        def work(g):
            o_ref[g] = x_ref[g]

        each(tiles.shape[0], work)

    out = pltpu.VMEM(tiles.shape, BF)
    return order.run(body, "copy_tiles", [in_vmem(tiles)], [VMEM], [out], [VMEM], [])[0]


def write_rows(order, wide_pieces, placed_pieces, blended, anchor, size=1024):
    n, m = len(wide_pieces), len(placed_pieces)
    counts = [len(arrays) for arrays, _, _ in wide_pieces]
    flat = [x for arrays, _, _ in wide_pieces for x in arrays]
    late = sum(counts[:-1])
    outs = [pltpu.HBM((ROWS, D), F32)] * (n > 0) + [pltpu.HBM((16, 2, ROWS, WIDTH), BF)] * (m > 0)
    earlier = [x for x, k in ((blended, n), (anchor, m)) if k and x is not None]

    def body(at, *refs):
        flat_refs, refs = list(refs[: len(flat)]), refs[len(flat) :]
        placed, refs = refs[:m], refs[m + len(earlier) :]
        out_refs, (wide, held, sems, placed_sems, held_sem) = refs[: len(outs)], refs[len(outs) :]

        def place(i, p):
            some = pl.ds(4 * p, 4)
            core, chip, same = placed_pieces[i][1:]
            there = pl.ds(first_row(at, core, chip, 0), QUARTER)
            return pltpu.make_async_copy(
                placed[i].at[some], out_refs[-1].at[some, plane(at, same), there, :], placed_sems.at[i, p]
            )

        def copy(i, p):
            there = pl.ds(first_row(at, *wide_pieces[i][1:], 0), QUARTER)
            return pltpu.make_async_copy(
                wide.at[i, :, span_of(p)], out_refs[0].at[there, span_of(p)], sems.at[i, p]
            )

        def work(i, tiles, p):
            if len(tiles) == 1:
                for k in range(PER):
                    g = p * PER + k
                    wide[i, :, columns(g)] = tiles[0][g].astype(F32)
            else:
                for k in range(PER // 2):
                    yz = p * (PER // 2) + k
                    for ref, same in zip(tiles, (True, False)):
                        wide[i, :, columns(2 * yz + plane(at, same))] = ref[yz].astype(F32)
            copy(i, p).start()

        if n:
            last = pltpu.make_async_copy(flat_refs[late], held, held_sem)
            last.start()
            flat_refs[late] = held
        for i in range(m):
            each(4, lambda p, i=i: place(i, p).start())
        for i in range(n):
            if i == n - 1:
                last.wait()
            tiles = flat_refs[sum(counts[:i]) : sum(counts[: i + 1])]
            each(PARTS, lambda p, i=i, tiles=tiles: work(i, tiles, p))
        for i in range(n):
            each(PARTS, lambda p, i=i: copy(i, p).wait())
        for i in range(m):
            each(4, lambda p, i=i: place(i, p).wait())

    in_hbm = lambda x: pltpu.with_memory_space_constraint(x, pltpu.HBM)
    args = [in_hbm(x) if i == late else in_vmem(x) for i, x in enumerate(flat)]
    specs = [HBM if i == late else VMEM for i in range(len(flat))]
    return order.run(
        body,
        "write_rows",
        args + [in_vmem(x) for x, *_ in placed_pieces] + earlier,
        specs + [VMEM] * m + [HBM] * len(earlier),
        outs,
        [HBM] * len(outs),
        [
            pltpu.VMEM((max(n, 1), QUARTER, D if n else 128), F32),
            pltpu.VMEM(flat[late].shape if n else (1, 16, 128), BF),
            pltpu.SemaphoreType.DMA((max(n, 1), PARTS)),
            pltpu.SemaphoreType.DMA((max(m, 1), 4)),
            pltpu.SemaphoreType.DMA,
        ],
        {len(flat) + m + 1 + k: k for k in range(len(earlier))},
        size,
    )


def per_device(policies, anchor):
    policy = pltpu.with_memory_space_constraint(policies[0], pltpu.HBM)
    shards = pltpu.with_memory_space_constraint(anchor.reshape(16, 2, ROWS, WIDTH), pltpu.HBM)
    order = Order(jnp.stack([lax.axis_index(name) for name in ("xl", "c", "xh")]).astype(jnp.int32))
    swap = [(0, 1), (1, 0)]
    groups = exchange_groups()

    def exchange(tiles):
        return lax.all_to_all(
            tiles, AXES, split_axis=0, concat_axis=0, axis_index_groups=groups, tiled=True
        )

    def core(tiles):
        return lax.ppermute(tiles, "c", swap)

    def chip(tiles):
        return lax.ppermute(tiles, "xl", swap)

    theirs = core(cast_rows(order, policy))
    picked = pick_rows(order, shards)
    other = chip(add_theirs(order, policy, theirs))
    fetched = exchange(picked)
    own = add_own(order, policy, [core(tiles) for tiles in cast_own(order, policy)])

    own = blend_rows(order, own, other, fetched)
    finished = chip(own)
    back = exchange(own)
    pieces = [([core(own)], False, True), ([own], True, True)]
    (blended,) = write_rows(order, pieces, [], None, None, WRITE_COST)

    first, low, second, high = split_planes(order, finished, back)
    back_first = lax.all_to_all(first, ("y", "z"), split_axis=0, concat_axis=0, tiled=True)
    back_second = chip(high)
    pieces = [
        (low, True, True, True),
        (core(low), False, True, True),
        (high, True, False, False),
        (core(high), False, False, False),
    ]
    (new_anchor,) = write_rows(order, [], pieces, None, None)
    back_second = copy_tiles(order, back_second)
    wide_pieces = [([core(first), core(second)], False, False), ([first, second], True, False)]
    pieces = [(back_second, True, True, False)]
    blended, new_anchor = write_rows(order, wide_pieces, pieces, blended, new_anchor)
    back_first = copy_tiles(order, back_first)
    pieces = [(back_first, True, False, True), (core(back_second), False, True, False)]
    (new_anchor,) = write_rows(order, [], pieces, None, new_anchor, LAST_COST)
    (new_anchor,) = write_rows(order, [], [(core(back_first), False, False, True)], None, new_anchor)
    return blended, new_anchor.reshape(SHARDS * ROWS, WIDTH)


def solution(mesh):
    fine = Mesh(mesh.devices.reshape(SIZES), AXES)
    shards = ("y", "z", "xh")
    return jax.shard_map(
        per_device,
        mesh=fine,
        in_specs=(P(("xl", "c"), shards, None), P(None, shards)),
        out_specs=(P(shards, None), P(None, shards)),
        check_vma=False,
    )
```

```python
import jax
import jax.numpy as jnp
import numpy as np
from jax import lax
from jax.experimental import pallas as pl
from jax.experimental.pallas import tpu as pltpu
from jax.sharding import Mesh, PartitionSpec as P

blend_rate = 0.3

AXES = ("xl", "c", "y", "z", "xh")
SIZES = (2, 2, 4, 4, 2)
SHARDS = 32
ROWS = 256
WIDTH = 256
D = 8192
HALF = 128
QUARTER = 64
R = 32
BF = jnp.bfloat16
F32 = jnp.float32
VMEM_LIMIT = 10 << 20
PARTS = 8
PER = SHARDS // PARTS
WRITE_COST = 11 << 20
LAST_COST = 37 << 20
ANY = pl.BlockSpec(memory_space=pl.ANY)
HBM = pl.BlockSpec(memory_space=pltpu.HBM)
VMEM = pl.BlockSpec(memory_space=pltpu.VMEM)
TOKEN = jax.ShapeDtypeStruct((8, 128), jnp.int32)


def exchange_groups():
    ids = np.arange(128).reshape(SIZES)
    return [
        [int(ids[flip ^ xh, c, y, z, xh]) for y in range(4) for z in range(4) for xh in range(2)]
        for flip in range(2)
        for c in range(2)
    ]


def in_vmem(x):
    return pltpu.with_memory_space_constraint(x, pltpu.VMEM)


class Order:
    def __init__(self, place):
        self.place = place
        self.token = None

    def run(self, body, name, args, specs, outs, out_specs, scratch, aliases=None, size=1024):
        held = [] if self.token is None else [self.token]

        def ordered(at, *refs):
            ins, rest = refs[: len(args)], refs[len(args) + len(held) :]
            results, others = rest[: len(outs)], rest[len(outs) + 1 :]
            body(at, *ins, *results, *others)

        *results, self.token = pl.pallas_call(
            ordered,
            out_shape=[*outs, TOKEN],
            grid_spec=pltpu.PrefetchScalarGridSpec(
                num_scalar_prefetch=1,
                grid=(),
                in_specs=[*specs, *[ANY] * len(held)],
                out_specs=[*out_specs, ANY],
                scratch_shapes=scratch,
            ),
            input_output_aliases=aliases or {},
            compiler_params=pltpu.CompilerParams(vmem_limit_bytes=VMEM_LIMIT),
            cost_estimate=pl.CostEstimate(flops=0, bytes_accessed=size, transcendentals=0),
            name=name,
        )(self.place, *args, *held)
        return results


def columns(g):
    return pl.ds(pl.multiple_of(g * WIDTH, WIDTH), WIDTH)


def each(count, work):
    pl.loop(0, count)(work)


def first_row(at, core, chip, start, xl=None):
    xl = at[0] if xl is None else xl
    half = at[1] if core else 1 - at[1]
    quarter = xl if chip else 1 - xl
    return pl.multiple_of(half * HALF + quarter * QUARTER + start, 16)


def member_row(at, where, xh):
    differs = at[2] if xh == 0 else 1 - at[2]
    return first_row(at, *where, at[0] + differs - 2 * at[0] * differs)


def tiles_out(rows):
    return pltpu.VMEM((SHARDS, rows, WIDTH), BF)


def span_of(p):
    return pl.ds(pl.multiple_of(p * PER * WIDTH, WIDTH), PER * WIDTH)


def cast_rows(order, policy):
    def body(at, x_ref, o_ref, wide, sems):
        held = pl.ds(first_row(at, False, False, 0), QUARTER)

        def copy(p):
            return pltpu.make_async_copy(x_ref.at[held, span_of(p)], wide.at[:, span_of(p)], sems.at[p])

        def work(p):
            copy(p).wait()
            for k in range(PER):
                g = p * PER + k
                o_ref[g] = wide[:, columns(g)].astype(BF)

        each(PARTS, lambda p: copy(p).start())
        each(PARTS, work)

    (out,) = order.run(
        body,
        "cast_rows",
        (policy,),
        [HBM],
        [tiles_out(QUARTER)],
        [VMEM],
        [pltpu.VMEM((QUARTER, D), F32), pltpu.SemaphoreType.DMA((PARTS,))],
    )
    return out


def add_theirs(order, policy, tiles):
    def body(at, x_ref, t_ref, o_ref, wide, held, in_sems, out_sems):
        rows = pl.ds(first_row(at, True, False, 0), QUARTER)

        def fetch(p):
            return pltpu.make_async_copy(x_ref.at[rows, span_of(p)], wide.at[:, span_of(p)], in_sems.at[p])

        def store(p):
            some = pl.ds(p * PER, PER)
            return pltpu.make_async_copy(held.at[some], o_ref.at[some], out_sems.at[p])

        def work(p):
            fetch(p).wait()
            for k in range(PER):
                g = p * PER + k
                held[g] = (wide[:, columns(g)] + t_ref[g].astype(F32)).astype(BF)
            store(p).start()

        each(PARTS, lambda p: fetch(p).start())
        each(PARTS, work)
        each(PARTS, lambda p: store(p).wait())

    (out,) = order.run(
        body,
        "add_theirs",
        (policy, in_vmem(tiles)),
        [HBM, VMEM],
        [pltpu.HBM((SHARDS, QUARTER, WIDTH), BF)],
        [HBM],
        [
            pltpu.VMEM((QUARTER, D), F32),
            pltpu.VMEM((SHARDS, QUARTER, WIDTH), BF),
            pltpu.SemaphoreType.DMA((PARTS,)),
            pltpu.SemaphoreType.DMA((PARTS,)),
        ],
    )
    return out


def cast_own(order, policy):
    def body(at, x_ref, low_ref, high_ref, wide, sems):
        held = pl.ds(first_row(at, False, True, 0), QUARTER)

        def copy(p):
            return pltpu.make_async_copy(x_ref.at[held, span_of(p)], wide.at[:, span_of(p)], sems.at[p])

        def work(p):
            copy(p).wait()
            for k in range(PER):
                g = p * PER + k
                low_ref[g] = wide[:R, columns(g)].astype(BF)
                high_ref[g] = wide[R:, columns(g)].astype(BF)

        each(PARTS, lambda p: copy(p).start())
        each(PARTS, work)

    return order.run(
        body,
        "cast_own",
        (policy,),
        [HBM],
        [tiles_out(R)] * 2,
        [VMEM] * 2,
        [pltpu.VMEM((QUARTER, D), F32), pltpu.SemaphoreType.DMA((PARTS,))],
    )


def add_own(order, policy, chunks):
    def body(at, x_ref, low_ref, high_ref, o_ref, wide, sems):
        held = pl.ds(first_row(at, True, True, 0), QUARTER)

        def copy(p):
            return pltpu.make_async_copy(x_ref.at[held, span_of(p)], wide.at[:, span_of(p)], sems.at[p])

        def work(p):
            copy(p).wait()
            for k in range(PER):
                g = p * PER + k
                o_ref[g, :R] = (wide[:R, columns(g)] + low_ref[g].astype(F32)).astype(BF)
                o_ref[g, R:] = (wide[R:, columns(g)] + high_ref[g].astype(F32)).astype(BF)

        each(PARTS, lambda p: copy(p).start())
        each(PARTS, work)

    (out,) = order.run(
        body,
        "add_own",
        (policy, *[in_vmem(tiles) for tiles in chunks]),
        [HBM, VMEM, VMEM],
        [tiles_out(QUARTER)],
        [VMEM],
        [pltpu.VMEM((QUARTER, D), F32), pltpu.SemaphoreType.DMA((PARTS,))],
    )
    return out


def pick_rows(order, anchor):
    def body(at, a_ref, p_ref, held, in_sems, out_sems):
        rows = [member_row(at, (True, True, 0), xh) for xh in range(2)]

        def fetch(p, xh):
            some = pl.ds(4 * p, 4)
            return pltpu.make_async_copy(
                a_ref.at[some, xh, pl.ds(rows[xh], QUARTER), :], held.at[some, xh], in_sems.at[xh, p]
            )

        def store(p, xh):
            some = pl.ds(4 * p, 4)
            return pltpu.make_async_copy(held.at[some, xh], p_ref.at[some, xh], out_sems.at[xh, p])

        def forward(p, xh):
            fetch(p, xh).wait()
            store(p, xh).start()

        for xh in range(2):
            each(4, lambda p, xh=xh: fetch(p, xh).start())
        for xh in range(2):
            each(4, lambda p, xh=xh: forward(p, xh))
        for xh in range(2):
            each(4, lambda p, xh=xh: store(p, xh).wait())

    (picked,) = order.run(
        body,
        "pick_rows",
        (anchor,),
        [HBM],
        [pltpu.HBM((16, 2, QUARTER, WIDTH), BF)],
        [HBM],
        [
            pltpu.VMEM((16, 2, QUARTER, WIDTH), BF),
            pltpu.SemaphoreType.DMA((2, 4)),
            pltpu.SemaphoreType.DMA((2, 4)),
        ],
    )
    return picked.reshape(SHARDS, QUARTER, WIDTH)


def blend_rows(order, own, other, anchor):
    def body(at, x_ref, t_ref, a_ref, o_ref, held, sems):
        def store(p):
            some = pl.ds(p * PER, PER)
            return pltpu.make_async_copy(held.at[some], o_ref.at[some], sems.at[p])

        def work(p):
            for k in range(PER):
                g = p * PER + k
                average = (x_ref[g].astype(F32) + t_ref[g].astype(F32)) / 4
                held[g] = ((1.0 - blend_rate) * a_ref[g].astype(F32) + blend_rate * average).astype(BF)
            store(p).start()

        each(PARTS, work)
        each(PARTS, lambda p: store(p).wait())

    (out,) = order.run(
        body,
        "blend_rows",
        [in_vmem(x) for x in (own, other, anchor)],
        [VMEM] * 3,
        [pltpu.HBM((SHARDS, QUARTER, WIDTH), BF)],
        [HBM],
        [pltpu.VMEM((SHARDS, QUARTER, WIDTH), BF), pltpu.SemaphoreType.DMA((PARTS,))],
    )
    return out


def plane(at, same):
    return at[2] if same else 1 - at[2]


def split_planes(order, finished, back):
    def body(at, f_ref, b_ref, first_ref, low_ref, second_ref, high_ref, sems):
        def stores(p):
            some = pl.ds(4 * p, 4)
            ends = ((f_ref, first_ref), (b_ref, low_ref))
            return [
                pltpu.make_async_copy(x.at[some, plane(at, True)], o.at[some], sems.at[i, p])
                for i, (x, o) in enumerate(ends)
            ]

        def start(p):
            for store in stores(p):
                store.start()

        def work(k):
            high_ref[k] = b_ref[k, plane(at, False)]
            second_ref[k] = f_ref[k, plane(at, False)]

        def finish(p):
            for store in stores(p):
                store.wait()

        each(4, start)
        each(16, work)
        each(4, finish)

    half = (16, QUARTER, WIDTH)
    return order.run(
        body,
        "split_planes",
        [in_vmem(x.reshape(16, 2, QUARTER, WIDTH)) for x in (finished, back)],
        [VMEM, VMEM],
        [pltpu.HBM(half, BF), jax.ShapeDtypeStruct(half, BF), pltpu.VMEM(half, BF), pltpu.VMEM(half, BF)],
        [HBM, ANY, VMEM, VMEM],
        [pltpu.SemaphoreType.DMA((2, 4))],
    )


def copy_tiles(order, arrays):
    n = len(arrays)

    def body(at, *refs):
        ins, outs, sems = refs[:n], refs[n : 2 * n], refs[2 * n]

        def copy(i, p):
            some = pl.ds(4 * p, 4)
            return pltpu.make_async_copy(ins[i].at[some], outs[i].at[some], sems.at[i, p])

        for i in range(n):
            each(4, lambda p, i=i: copy(i, p).start())
        for i in range(n):
            each(4, lambda p, i=i: copy(i, p).wait())

    return order.run(
        body,
        "copy_tiles",
        arrays,
        [ANY] * n,
        [pltpu.VMEM(x.shape, BF) for x in arrays],
        [VMEM] * n,
        [pltpu.SemaphoreType.DMA((n, 4))],
    )


def write_rows(order, wide_pieces, placed_pieces, blended, anchor, size=1024):
    n, m = len(wide_pieces), len(placed_pieces)
    counts = [len(arrays) for arrays, _, _ in wide_pieces]
    flat = [x for arrays, _, _ in wide_pieces for x in arrays]
    late = sum(counts[:-1])
    outs = [pltpu.HBM((ROWS, D), F32)] * (n > 0) + [pltpu.HBM((16, 2, ROWS, WIDTH), BF)] * (m > 0)
    earlier = [x for x, k in ((blended, n), (anchor, m)) if k and x is not None]

    def body(at, *refs):
        flat_refs, refs = list(refs[: len(flat)]), refs[len(flat) :]
        placed, refs = refs[:m], refs[m + len(earlier) :]
        out_refs, (wide, held, sems, placed_sems, held_sem) = refs[: len(outs)], refs[len(outs) :]

        def place(i, p):
            some = pl.ds(4 * p, 4)
            core, chip, same = placed_pieces[i][1:]
            there = pl.ds(first_row(at, core, chip, 0), QUARTER)
            return pltpu.make_async_copy(
                placed[i].at[some], out_refs[-1].at[some, plane(at, same), there, :], placed_sems.at[i, p]
            )

        def copy(i, p):
            there = pl.ds(first_row(at, *wide_pieces[i][1:], 0), QUARTER)
            return pltpu.make_async_copy(
                wide.at[i, :, span_of(p)], out_refs[0].at[there, span_of(p)], sems.at[i, p]
            )

        def work(i, tiles, p):
            if len(tiles) == 1:
                for k in range(PER):
                    g = p * PER + k
                    wide[i, :, columns(g)] = tiles[0][g].astype(F32)
            else:
                for k in range(PER // 2):
                    yz = p * (PER // 2) + k
                    for ref, same in zip(tiles, (True, False)):
                        wide[i, :, columns(2 * yz + plane(at, same))] = ref[yz].astype(F32)
            copy(i, p).start()

        if n:
            last = pltpu.make_async_copy(flat_refs[late], held, held_sem)
            last.start()
            flat_refs[late] = held
        for i in range(m):
            each(4, lambda p, i=i: place(i, p).start())
        for i in range(n):
            if i == n - 1:
                last.wait()
            tiles = flat_refs[sum(counts[:i]) : sum(counts[: i + 1])]
            each(PARTS, lambda p, i=i, tiles=tiles: work(i, tiles, p))
        for i in range(n):
            each(PARTS, lambda p, i=i: copy(i, p).wait())
        for i in range(m):
            each(4, lambda p, i=i: place(i, p).wait())

    in_hbm = lambda x: pltpu.with_memory_space_constraint(x, pltpu.HBM)
    args = [in_hbm(x) if i == late else in_vmem(x) for i, x in enumerate(flat)]
    specs = [HBM if i == late else VMEM for i in range(len(flat))]
    return order.run(
        body,
        "write_rows",
        args + [in_vmem(x) for x, *_ in placed_pieces] + earlier,
        specs + [VMEM] * m + [HBM] * len(earlier),
        outs,
        [HBM] * len(outs),
        [
            pltpu.VMEM((max(n, 1), QUARTER, D if n else 128), F32),
            pltpu.VMEM(flat[late].shape if n else (1, 16, 128), BF),
            pltpu.SemaphoreType.DMA((max(n, 1), PARTS)),
            pltpu.SemaphoreType.DMA((max(m, 1), 4)),
            pltpu.SemaphoreType.DMA,
        ],
        {len(flat) + m + 1 + k: k for k in range(len(earlier))},
        size,
    )


def per_device(policies, anchor):
    policy = pltpu.with_memory_space_constraint(policies[0], pltpu.HBM)
    shards = pltpu.with_memory_space_constraint(anchor.reshape(16, 2, ROWS, WIDTH), pltpu.HBM)
    order = Order(jnp.stack([lax.axis_index(name) for name in ("xl", "c", "xh")]).astype(jnp.int32))
    swap = [(0, 1), (1, 0)]
    groups = exchange_groups()

    def exchange(tiles):
        return lax.all_to_all(
            tiles, AXES, split_axis=0, concat_axis=0, axis_index_groups=groups, tiled=True
        )

    def core(tiles):
        return lax.ppermute(tiles, "c", swap)

    def chip(tiles):
        return lax.ppermute(tiles, "xl", swap)

    theirs = core(cast_rows(order, policy))
    picked = pick_rows(order, shards)
    other = chip(add_theirs(order, policy, theirs))
    fetched = exchange(picked)
    own = add_own(order, policy, [core(tiles) for tiles in cast_own(order, policy)])

    own = blend_rows(order, own, other, fetched)
    finished = chip(own)
    back = exchange(own)
    pieces = [([core(own)], False, True), ([own], True, True)]
    (blended,) = write_rows(order, pieces, [], None, None, WRITE_COST)

    first, low, second, high = split_planes(order, finished, back)
    back_first = lax.all_to_all(first, ("y", "z"), split_axis=0, concat_axis=0, tiled=True)
    back_second = chip(high)
    pieces = [
        (low, True, True, True),
        (core(low), False, True, True),
        (high, True, False, False),
        (core(high), False, False, False),
    ]
    (new_anchor,) = write_rows(order, [], pieces, None, None)
    pieces = [([core(first), core(second)], False, False), ([first, second], True, False)]
    (blended,) = write_rows(order, pieces, [], blended, None)
    back_first, back_second = copy_tiles(order, [back_first, back_second])
    pieces = [(back_first, True, False, True), (back_second, True, True, False)]
    (new_anchor,) = write_rows(order, [], pieces, None, new_anchor, LAST_COST)
    pieces = [(core(back_first), False, False, True), (core(back_second), False, True, False)]
    (new_anchor,) = write_rows(order, [], pieces, None, new_anchor)
    return blended, new_anchor.reshape(SHARDS * ROWS, WIDTH)


def solution(mesh):
    fine = Mesh(mesh.devices.reshape(SIZES), AXES)
    shards = ("y", "z", "xh")
    return jax.shard_map(
        per_device,
        mesh=fine,
        in_specs=(P(("xl", "c"), shards, None), P(None, shards)),
        out_specs=(P(shards, None), P(None, shards)),
        check_vma=False,
    )
```

```python
import jax
import jax.numpy as jnp
import numpy as np
from jax import lax
from jax.experimental import pallas as pl
from jax.experimental.pallas import tpu as pltpu
from jax.sharding import Mesh, PartitionSpec as P

blend_rate = 0.3

AXES = ("xl", "c", "y", "z", "xh")
SIZES = (2, 2, 4, 4, 2)
SHARDS = 32
ROWS = 256
WIDTH = 256
D = 8192
HALF = 128
QUARTER = 64
R = 32
BF = jnp.bfloat16
F32 = jnp.float32
VMEM_LIMIT = 10 << 20
PARTS = 8
PER = SHARDS // PARTS
WRITE_COST = 11 << 20
LAST_COST = 37 << 20
ANY = pl.BlockSpec(memory_space=pl.ANY)
HBM = pl.BlockSpec(memory_space=pltpu.HBM)
VMEM = pl.BlockSpec(memory_space=pltpu.VMEM)
TOKEN = jax.ShapeDtypeStruct((8, 128), jnp.int32)


def exchange_groups():
    ids = np.arange(128).reshape(SIZES)
    return [
        [int(ids[flip ^ xh, c, y, z, xh]) for y in range(4) for z in range(4) for xh in range(2)]
        for flip in range(2)
        for c in range(2)
    ]


def in_vmem(x):
    return pltpu.with_memory_space_constraint(x, pltpu.VMEM)


class Order:
    def __init__(self, place):
        self.place = place
        self.token = None

    def behind(self, x):
        x, self.token = lax.optimization_barrier((x, self.token))
        return x

    def run(self, body, name, args, specs, outs, out_specs, scratch, aliases=None, size=1024):
        held = [] if self.token is None else [self.token]

        def ordered(at, *refs):
            ins, rest = refs[: len(args)], refs[len(args) + len(held) :]
            results, others = rest[: len(outs)], rest[len(outs) + 1 :]
            body(at, *ins, *results, *others)

        *results, self.token = pl.pallas_call(
            ordered,
            out_shape=[*outs, TOKEN],
            grid_spec=pltpu.PrefetchScalarGridSpec(
                num_scalar_prefetch=1,
                grid=(),
                in_specs=[*specs, *[ANY] * len(held)],
                out_specs=[*out_specs, ANY],
                scratch_shapes=scratch,
            ),
            input_output_aliases=aliases or {},
            compiler_params=pltpu.CompilerParams(vmem_limit_bytes=VMEM_LIMIT),
            cost_estimate=pl.CostEstimate(flops=0, bytes_accessed=size, transcendentals=0),
            name=name,
        )(self.place, *args, *held)
        return results


def columns(g):
    return pl.ds(pl.multiple_of(g * WIDTH, WIDTH), WIDTH)


def each(count, work):
    pl.loop(0, count)(work)


def first_row(at, core, chip, start, xl=None):
    xl = at[0] if xl is None else xl
    half = at[1] if core else 1 - at[1]
    quarter = xl if chip else 1 - xl
    return pl.multiple_of(half * HALF + quarter * QUARTER + start, 16)


def member_row(at, where, xh):
    differs = at[2] if xh == 0 else 1 - at[2]
    return first_row(at, *where, at[0] + differs - 2 * at[0] * differs)


def tiles_out(rows):
    return pltpu.VMEM((SHARDS, rows, WIDTH), BF)


def span_of(p):
    return pl.ds(pl.multiple_of(p * PER * WIDTH, WIDTH), PER * WIDTH)


def cast_rows(order, policy):
    def body(at, x_ref, o_ref, wide, sems):
        held = pl.ds(first_row(at, False, False, 0), QUARTER)

        def copy(p):
            return pltpu.make_async_copy(x_ref.at[held, span_of(p)], wide.at[:, span_of(p)], sems.at[p])

        def work(p):
            copy(p).wait()
            for k in range(PER):
                g = p * PER + k
                o_ref[g] = wide[:, columns(g)].astype(BF)

        each(PARTS, lambda p: copy(p).start())
        each(PARTS, work)

    (out,) = order.run(
        body,
        "cast_rows",
        (policy,),
        [HBM],
        [tiles_out(QUARTER)],
        [VMEM],
        [pltpu.VMEM((QUARTER, D), F32), pltpu.SemaphoreType.DMA((PARTS,))],
    )
    return out


def add_theirs(order, policy, tiles):
    def body(at, x_ref, t_ref, o_ref, wide, held, in_sems, out_sems):
        rows = pl.ds(first_row(at, True, False, 0), QUARTER)

        def fetch(p):
            return pltpu.make_async_copy(x_ref.at[rows, span_of(p)], wide.at[:, span_of(p)], in_sems.at[p])

        def store(p):
            some = pl.ds(p * PER, PER)
            return pltpu.make_async_copy(held.at[some], o_ref.at[some], out_sems.at[p])

        def work(p):
            fetch(p).wait()
            for k in range(PER):
                g = p * PER + k
                held[g] = (wide[:, columns(g)] + t_ref[g].astype(F32)).astype(BF)
            store(p).start()

        each(PARTS, lambda p: fetch(p).start())
        each(PARTS, work)
        each(PARTS, lambda p: store(p).wait())

    (out,) = order.run(
        body,
        "add_theirs",
        (policy, in_vmem(tiles)),
        [HBM, VMEM],
        [pltpu.HBM((SHARDS, QUARTER, WIDTH), BF)],
        [HBM],
        [
            pltpu.VMEM((QUARTER, D), F32),
            pltpu.VMEM((SHARDS, QUARTER, WIDTH), BF),
            pltpu.SemaphoreType.DMA((PARTS,)),
            pltpu.SemaphoreType.DMA((PARTS,)),
        ],
    )
    return out


def cast_own(order, policy):
    def body(at, x_ref, low_ref, high_ref, wide, sems):
        held = pl.ds(first_row(at, False, True, 0), QUARTER)

        def copy(p):
            return pltpu.make_async_copy(x_ref.at[held, span_of(p)], wide.at[:, span_of(p)], sems.at[p])

        def work(p):
            copy(p).wait()
            for k in range(PER):
                g = p * PER + k
                low_ref[g] = wide[:R, columns(g)].astype(BF)
                high_ref[g] = wide[R:, columns(g)].astype(BF)

        each(PARTS, lambda p: copy(p).start())
        each(PARTS, work)

    return order.run(
        body,
        "cast_own",
        (policy,),
        [HBM],
        [tiles_out(R)] * 2,
        [VMEM] * 2,
        [pltpu.VMEM((QUARTER, D), F32), pltpu.SemaphoreType.DMA((PARTS,))],
    )


def add_own(order, policy, chunks):
    def body(at, x_ref, low_ref, high_ref, o_ref, wide, sems):
        held = pl.ds(first_row(at, True, True, 0), QUARTER)

        def copy(p):
            return pltpu.make_async_copy(x_ref.at[held, span_of(p)], wide.at[:, span_of(p)], sems.at[p])

        def work(p):
            copy(p).wait()
            for k in range(PER):
                g = p * PER + k
                o_ref[g, :R] = (wide[:R, columns(g)] + low_ref[g].astype(F32)).astype(BF)
                o_ref[g, R:] = (wide[R:, columns(g)] + high_ref[g].astype(F32)).astype(BF)

        each(PARTS, lambda p: copy(p).start())
        each(PARTS, work)

    (out,) = order.run(
        body,
        "add_own",
        (policy, *[in_vmem(tiles) for tiles in chunks]),
        [HBM, VMEM, VMEM],
        [tiles_out(QUARTER)],
        [VMEM],
        [pltpu.VMEM((QUARTER, D), F32), pltpu.SemaphoreType.DMA((PARTS,))],
    )
    return out


def pick_rows(order, anchor):
    def body(at, a_ref, p_ref, held, in_sems, out_sems):
        rows = [member_row(at, (True, True, 0), xh) for xh in range(2)]

        def fetch(p, xh):
            some = pl.ds(4 * p, 4)
            return pltpu.make_async_copy(
                a_ref.at[some, xh, pl.ds(rows[xh], QUARTER), :], held.at[some, xh], in_sems.at[xh, p]
            )

        def store(p, xh):
            some = pl.ds(4 * p, 4)
            return pltpu.make_async_copy(held.at[some, xh], p_ref.at[some, xh], out_sems.at[xh, p])

        def forward(p, xh):
            fetch(p, xh).wait()
            store(p, xh).start()

        for xh in range(2):
            each(4, lambda p, xh=xh: fetch(p, xh).start())
        for xh in range(2):
            each(4, lambda p, xh=xh: forward(p, xh))
        for xh in range(2):
            each(4, lambda p, xh=xh: store(p, xh).wait())

    (picked,) = order.run(
        body,
        "pick_rows",
        (anchor,),
        [HBM],
        [pltpu.HBM((16, 2, QUARTER, WIDTH), BF)],
        [HBM],
        [
            pltpu.VMEM((16, 2, QUARTER, WIDTH), BF),
            pltpu.SemaphoreType.DMA((2, 4)),
            pltpu.SemaphoreType.DMA((2, 4)),
        ],
    )
    return picked.reshape(SHARDS, QUARTER, WIDTH)


def blend_rows(order, own, other, anchor):
    def body(at, x_ref, t_ref, a_ref, o_ref, held, sems):
        def store(p):
            some = pl.ds(p * PER, PER)
            return pltpu.make_async_copy(held.at[some], o_ref.at[some], sems.at[p])

        def work(p):
            for k in range(PER):
                g = p * PER + k
                average = (x_ref[g].astype(F32) + t_ref[g].astype(F32)) / 4
                held[g] = ((1.0 - blend_rate) * a_ref[g].astype(F32) + blend_rate * average).astype(BF)
            store(p).start()

        each(PARTS, work)
        each(PARTS, lambda p: store(p).wait())

    (out,) = order.run(
        body,
        "blend_rows",
        [in_vmem(x) for x in (own, other, anchor)],
        [VMEM] * 3,
        [pltpu.HBM((SHARDS, QUARTER, WIDTH), BF)],
        [HBM],
        [pltpu.VMEM((SHARDS, QUARTER, WIDTH), BF), pltpu.SemaphoreType.DMA((PARTS,))],
    )
    return out


def plane(at, same):
    return at[2] if same else 1 - at[2]


def split_planes(order, finished, back):
    def body(at, f_ref, b_ref, first_ref, low_ref, second_ref, high_ref, sems):
        def stores(p):
            some = pl.ds(4 * p, 4)
            ends = ((f_ref, first_ref), (b_ref, low_ref))
            return [
                pltpu.make_async_copy(x.at[some, plane(at, True)], o.at[some], sems.at[i, p])
                for i, (x, o) in enumerate(ends)
            ]

        def start(p):
            for store in stores(p):
                store.start()

        def work(k):
            high_ref[k] = b_ref[k, plane(at, False)]
            second_ref[k] = f_ref[k, plane(at, False)]

        def finish(p):
            for store in stores(p):
                store.wait()

        each(4, start)
        each(16, work)
        each(4, finish)

    half = (16, QUARTER, WIDTH)
    return order.run(
        body,
        "split_planes",
        [in_vmem(x.reshape(16, 2, QUARTER, WIDTH)) for x in (finished, back)],
        [VMEM, VMEM],
        [pltpu.HBM(half, BF), jax.ShapeDtypeStruct(half, BF), pltpu.VMEM(half, BF), pltpu.VMEM(half, BF)],
        [HBM, ANY, VMEM, VMEM],
        [pltpu.SemaphoreType.DMA((2, 4))],
    )


def write_rows(order, wide_pieces, placed_pieces, blended, anchor, size=1024):
    n, m = len(wide_pieces), len(placed_pieces)
    counts = [len(arrays) for arrays, _, _ in wide_pieces]
    flat = [x for arrays, _, _ in wide_pieces for x in arrays]
    late = sum(counts[:-1])
    outs = [pltpu.HBM((ROWS, D), F32)] * (n > 0) + [pltpu.HBM((16, 2, ROWS, WIDTH), BF)] * (m > 0)
    earlier = [x for x, k in ((blended, n), (anchor, m)) if k and x is not None]

    def body(at, *refs):
        flat_refs, refs = list(refs[: len(flat)]), refs[len(flat) :]
        placed, refs = refs[:m], refs[m + len(earlier) :]
        out_refs, (wide, held, sems, placed_sems, held_sem) = refs[: len(outs)], refs[len(outs) :]

        def place(i, p):
            some = pl.ds(4 * p, 4)
            core, chip, same = placed_pieces[i][1:]
            there = pl.ds(first_row(at, core, chip, 0), QUARTER)
            return pltpu.make_async_copy(
                placed[i].at[some], out_refs[-1].at[some, plane(at, same), there, :], placed_sems.at[i, p]
            )

        def copy(i, p):
            there = pl.ds(first_row(at, *wide_pieces[i][1:], 0), QUARTER)
            return pltpu.make_async_copy(
                wide.at[i, :, span_of(p)], out_refs[0].at[there, span_of(p)], sems.at[i, p]
            )

        def work(i, tiles, p):
            if len(tiles) == 1:
                for k in range(PER):
                    g = p * PER + k
                    wide[i, :, columns(g)] = tiles[0][g].astype(F32)
            else:
                for k in range(PER // 2):
                    yz = p * (PER // 2) + k
                    for ref, same in zip(tiles, (True, False)):
                        wide[i, :, columns(2 * yz + plane(at, same))] = ref[yz].astype(F32)
            copy(i, p).start()

        if n:
            last = pltpu.make_async_copy(flat_refs[late], held, held_sem)
            last.start()
            flat_refs[late] = held
        for i in range(m):
            each(4, lambda p, i=i: place(i, p).start())
        for i in range(n):
            if i == n - 1:
                last.wait()
            tiles = flat_refs[sum(counts[:i]) : sum(counts[: i + 1])]
            each(PARTS, lambda p, i=i, tiles=tiles: work(i, tiles, p))
        for i in range(n):
            each(PARTS, lambda p, i=i: copy(i, p).wait())
        for i in range(m):
            each(4, lambda p, i=i: place(i, p).wait())

    in_hbm = lambda x: pltpu.with_memory_space_constraint(x, pltpu.HBM)
    args = [in_hbm(x) if i == late else in_vmem(x) for i, x in enumerate(flat)]
    specs = [HBM if i == late else VMEM for i in range(len(flat))]
    return order.run(
        body,
        "write_rows",
        args + [in_vmem(x) for x, *_ in placed_pieces] + earlier,
        specs + [VMEM] * m + [HBM] * len(earlier),
        outs,
        [HBM] * len(outs),
        [
            pltpu.VMEM((max(n, 1), QUARTER, D if n else 128), F32),
            pltpu.VMEM(flat[late].shape if n else (1, 16, 128), BF),
            pltpu.SemaphoreType.DMA((max(n, 1), PARTS)),
            pltpu.SemaphoreType.DMA((max(m, 1), 4)),
            pltpu.SemaphoreType.DMA,
        ],
        {len(flat) + m + 1 + k: k for k in range(len(earlier))},
        size,
    )


def per_device(policies, anchor):
    policy = pltpu.with_memory_space_constraint(policies[0], pltpu.HBM)
    shards = pltpu.with_memory_space_constraint(anchor.reshape(16, 2, ROWS, WIDTH), pltpu.HBM)
    order = Order(jnp.stack([lax.axis_index(name) for name in ("xl", "c", "xh")]).astype(jnp.int32))
    swap = [(0, 1), (1, 0)]
    groups = exchange_groups()

    def exchange(tiles):
        return lax.all_to_all(
            tiles, AXES, split_axis=0, concat_axis=0, axis_index_groups=groups, tiled=True
        )

    def core(tiles):
        return lax.ppermute(tiles, "c", swap)

    def chip(tiles):
        return lax.ppermute(tiles, "xl", swap)

    theirs = core(cast_rows(order, policy))
    picked = pick_rows(order, shards)
    other = chip(add_theirs(order, policy, theirs))
    fetched = exchange(picked)
    own = add_own(order, policy, [core(tiles) for tiles in cast_own(order, policy)])

    own = blend_rows(order, own, other, fetched)
    finished = chip(own)
    back = exchange(own)
    pieces = [([core(own)], False, True), ([own], True, True)]
    (blended,) = write_rows(order, pieces, [], None, None, WRITE_COST)

    first, low, second, high = split_planes(order, finished, back)
    back_first = lax.all_to_all(first, ("y", "z"), split_axis=0, concat_axis=0, tiled=True)
    back_second = chip(high)
    pieces = [
        (low, True, True, True),
        (core(low), False, True, True),
        (high, True, False, False),
        (core(high), False, False, False),
    ]
    (new_anchor,) = write_rows(order, [], pieces, None, None)
    pieces = [([core(first), core(second)], False, False), ([first, second], True, False)]
    (blended,) = write_rows(order, pieces, [], blended, None)
    back_second = order.behind(back_second)
    back_first = order.behind(back_first)
    pieces = [(back_first, True, False, True), (back_second, True, True, False)]
    (new_anchor,) = write_rows(order, [], pieces, None, new_anchor, LAST_COST)
    pieces = [(core(back_first), False, False, True), (core(back_second), False, True, False)]
    (new_anchor,) = write_rows(order, [], pieces, None, new_anchor)
    return blended, new_anchor.reshape(SHARDS * ROWS, WIDTH)


def solution(mesh):
    fine = Mesh(mesh.devices.reshape(SIZES), AXES)
    shards = ("y", "z", "xh")
    return jax.shard_map(
        per_device,
        mesh=fine,
        in_specs=(P(("xl", "c"), shards, None), P(None, shards)),
        out_specs=(P(shards, None), P(None, shards)),
        check_vma=False,
    )
```

```python
import jax
import jax.numpy as jnp
import numpy as np
from jax import lax
from jax.experimental import pallas as pl
from jax.experimental.pallas import tpu as pltpu
from jax.sharding import Mesh, PartitionSpec as P

blend_rate = 0.3
GROUPS = 4

AXES = ("xl", "c", "y", "z", "xh")
SIZES = (2, 2, 4, 4, 2)
SHARDS = 32
ROWS = 256
WIDTH = 256
D = 8192
HALF = 128
QUARTER = 64
R = 32
BF = jnp.bfloat16
F32 = jnp.float32
VMEM_LIMIT = 10 << 20
PARTS = 8
PER = SHARDS // PARTS
WRITE_COST = 11 << 20
LAST_COST = 37 << 20
ANY = pl.BlockSpec(memory_space=pl.ANY)
HBM = pl.BlockSpec(memory_space=pltpu.HBM)
VMEM = pl.BlockSpec(memory_space=pltpu.VMEM)
TOKEN = jax.ShapeDtypeStruct((8, 128), jnp.int32)


def exchange_groups():
    ids = np.arange(128).reshape(SIZES)
    return [
        [int(ids[flip ^ xh, c, y, z, xh]) for y in range(4) for z in range(4) for xh in range(2)]
        for flip in range(2)
        for c in range(2)
    ]


def in_vmem(x):
    return pltpu.with_memory_space_constraint(x, pltpu.VMEM)


class Order:
    def __init__(self, place):
        self.place = place
        self.token = None

    def behind(self, x):
        x, self.token = lax.optimization_barrier((x, self.token))
        return x

    def run(self, body, name, args, specs, outs, out_specs, scratch, aliases=None, size=1024):
        held = [] if self.token is None else [self.token]

        def ordered(at, *refs):
            ins, rest = refs[: len(args)], refs[len(args) + len(held) :]
            results, others = rest[: len(outs)], rest[len(outs) + 1 :]
            body(at, *ins, *results, *others)

        *results, self.token = pl.pallas_call(
            ordered,
            out_shape=[*outs, TOKEN],
            grid_spec=pltpu.PrefetchScalarGridSpec(
                num_scalar_prefetch=1,
                grid=(),
                in_specs=[*specs, *[ANY] * len(held)],
                out_specs=[*out_specs, ANY],
                scratch_shapes=scratch,
            ),
            input_output_aliases=aliases or {},
            compiler_params=pltpu.CompilerParams(vmem_limit_bytes=VMEM_LIMIT),
            cost_estimate=pl.CostEstimate(flops=0, bytes_accessed=size, transcendentals=0),
            name=name,
        )(self.place, *args, *held)
        return results


def columns(g):
    return pl.ds(pl.multiple_of(g * WIDTH, WIDTH), WIDTH)


def each(count, work):
    pl.loop(0, count)(work)


def first_row(at, core, chip, start, xl=None):
    xl = at[0] if xl is None else xl
    half = at[1] if core else 1 - at[1]
    quarter = xl if chip else 1 - xl
    return pl.multiple_of(half * HALF + quarter * QUARTER + start, 16)


def member_row(at, where, xh):
    differs = at[2] if xh == 0 else 1 - at[2]
    return first_row(at, *where, at[0] + differs - 2 * at[0] * differs)


def tiles_out(rows):
    return pltpu.VMEM((SHARDS, rows, WIDTH), BF)


def span_of(p):
    return pl.ds(pl.multiple_of(p * PER * WIDTH, WIDTH), PER * WIDTH)


def cast_rows(order, policy):
    def body(at, x_ref, o_ref, wide, sems):
        held = pl.ds(first_row(at, False, False, 0), QUARTER)

        def copy(p):
            return pltpu.make_async_copy(x_ref.at[held, span_of(p)], wide.at[:, span_of(p)], sems.at[p])

        def work(p):
            copy(p).wait()
            for k in range(PER):
                g = p * PER + k
                o_ref[g] = wide[:, columns(g)].astype(BF)

        each(PARTS, lambda p: copy(p).start())
        each(PARTS, work)

    (out,) = order.run(
        body,
        "cast_rows",
        (policy,),
        [HBM],
        [tiles_out(QUARTER)],
        [VMEM],
        [pltpu.VMEM((QUARTER, D), F32), pltpu.SemaphoreType.DMA((PARTS,))],
    )
    return out


def add_theirs(order, rows, tiles):
    def body(at, x_ref, t_ref, o_ref, held, sems):
        def store(p):
            some = pl.ds(p * PER, PER)
            return pltpu.make_async_copy(held.at[some], o_ref.at[some], sems.at[p])

        def work(p):
            for k in range(PER):
                g = p * PER + k
                held[g] = (x_ref[:, columns(g)] + t_ref[g].astype(F32)).astype(BF)
            store(p).start()

        each(PARTS, work)
        each(PARTS, lambda p: store(p).wait())

    (out,) = order.run(
        body,
        "add_theirs",
        (in_vmem(rows), in_vmem(tiles)),
        [VMEM, VMEM],
        [pltpu.HBM((SHARDS, QUARTER, WIDTH), BF)],
        [HBM],
        [pltpu.VMEM((SHARDS, QUARTER, WIDTH), BF), pltpu.SemaphoreType.DMA((PARTS,))],
    )
    return out


def cast_own(order, policy):
    def body(at, x_ref, low_ref, high_ref, wide, sems):
        held = pl.ds(first_row(at, False, True, 0), QUARTER)

        def copy(p):
            return pltpu.make_async_copy(x_ref.at[held, span_of(p)], wide.at[:, span_of(p)], sems.at[p])

        def work(p):
            copy(p).wait()
            for k in range(PER):
                g = p * PER + k
                low_ref[g] = wide[:R, columns(g)].astype(BF)
                high_ref[g] = wide[R:, columns(g)].astype(BF)

        each(PARTS, lambda p: copy(p).start())
        each(PARTS, work)

    return order.run(
        body,
        "cast_own",
        (policy,),
        [HBM],
        [tiles_out(R)] * 2,
        [VMEM] * 2,
        [pltpu.VMEM((QUARTER, D), F32), pltpu.SemaphoreType.DMA((PARTS,))],
    )


def add_own(order, policy, chunks):
    def body(at, x_ref, low_ref, high_ref, o_ref, wide, sems):
        held = pl.ds(first_row(at, True, True, 0), QUARTER)

        def copy(p):
            return pltpu.make_async_copy(x_ref.at[held, span_of(p)], wide.at[:, span_of(p)], sems.at[p])

        def work(p):
            copy(p).wait()
            for k in range(PER):
                g = p * PER + k
                o_ref[g, :R] = (wide[:R, columns(g)] + low_ref[g].astype(F32)).astype(BF)
                o_ref[g, R:] = (wide[R:, columns(g)] + high_ref[g].astype(F32)).astype(BF)

        each(PARTS, lambda p: copy(p).start())
        each(PARTS, work)

    (out,) = order.run(
        body,
        "add_own",
        (policy, *[in_vmem(tiles) for tiles in chunks]),
        [HBM, VMEM, VMEM],
        [tiles_out(QUARTER)],
        [VMEM],
        [pltpu.VMEM((QUARTER, D), F32), pltpu.SemaphoreType.DMA((PARTS,))],
    )
    return out


def pick_rows(order, anchor, policy):
    def body(at, a_ref, x_ref, p_ref, rows_ref, held, in_sems, out_sems, x_sems):
        rows = [member_row(at, (True, True, 0), xh) for xh in range(2)]
        theirs = pl.ds(first_row(at, True, False, 0), QUARTER)

        def fetch(p, xh):
            some = pl.ds(4 * p, 4)
            return pltpu.make_async_copy(
                a_ref.at[some, xh, pl.ds(rows[xh], QUARTER), :], held.at[some, xh], in_sems.at[xh, p]
            )

        def store(p, xh):
            some = pl.ds(4 * p, 4)
            return pltpu.make_async_copy(held.at[some, xh], p_ref.at[some, xh], out_sems.at[xh, p])

        def copy(p):
            return pltpu.make_async_copy(
                x_ref.at[theirs, span_of(p)], rows_ref.at[:, span_of(p)], x_sems.at[p]
            )

        def forward(p, xh):
            fetch(p, xh).wait()
            store(p, xh).start()

        for xh in range(2):
            each(4, lambda p, xh=xh: fetch(p, xh).start())
        each(PARTS, lambda p: copy(p).start())
        for xh in range(2):
            each(4, lambda p, xh=xh: forward(p, xh))
        each(PARTS, lambda p: copy(p).wait())
        for xh in range(2):
            each(4, lambda p, xh=xh: store(p, xh).wait())

    picked, rows = order.run(
        body,
        "pick_rows",
        (anchor, policy),
        [HBM, HBM],
        [pltpu.HBM((16, 2, QUARTER, WIDTH), BF), pltpu.VMEM((QUARTER, D), F32)],
        [HBM, VMEM],
        [
            pltpu.VMEM((16, 2, QUARTER, WIDTH), BF),
            pltpu.SemaphoreType.DMA((2, 4)),
            pltpu.SemaphoreType.DMA((2, 4)),
            pltpu.SemaphoreType.DMA((PARTS,)),
        ],
    )
    return picked.reshape(SHARDS, QUARTER, WIDTH), rows


def blend_rows(order, own, other, anchor):
    def body(at, x_ref, t_ref, a_ref, o_ref, held, sems):
        def store(p):
            some = pl.ds(p * PER, PER)
            return pltpu.make_async_copy(held.at[some], o_ref.at[some], sems.at[p])

        def work(p):
            for k in range(PER):
                g = p * PER + k
                total = x_ref[g].astype(F32) + t_ref[g].astype(F32)
                new = (1.0 - blend_rate) * a_ref[g].astype(F32) + (blend_rate / GROUPS) * total
                held[g] = new.astype(BF)
            store(p).start()

        each(PARTS, work)
        each(PARTS, lambda p: store(p).wait())

    (out,) = order.run(
        body,
        "blend_rows",
        [in_vmem(x) for x in (own, other, anchor)],
        [VMEM] * 3,
        [pltpu.HBM((SHARDS, QUARTER, WIDTH), BF)],
        [HBM],
        [pltpu.VMEM((SHARDS, QUARTER, WIDTH), BF), pltpu.SemaphoreType.DMA((PARTS,))],
    )
    return out


def plane(at, same):
    return at[2] if same else 1 - at[2]


def split_planes(order, finished, back):
    def body(at, f_ref, b_ref, first_ref, low_ref, second_ref, high_ref, sems):
        def stores(p):
            some = pl.ds(4 * p, 4)
            ends = ((f_ref, first_ref), (b_ref, low_ref))
            return [
                pltpu.make_async_copy(x.at[some, plane(at, True)], o.at[some], sems.at[i, p])
                for i, (x, o) in enumerate(ends)
            ]

        def start(p):
            for store in stores(p):
                store.start()

        def work(k):
            high_ref[k] = b_ref[k, plane(at, False)]
            second_ref[k] = f_ref[k, plane(at, False)]

        def finish(p):
            for store in stores(p):
                store.wait()

        each(4, start)
        each(16, work)
        each(4, finish)

    half = (16, QUARTER, WIDTH)
    return order.run(
        body,
        "split_planes",
        [in_vmem(x.reshape(16, 2, QUARTER, WIDTH)) for x in (finished, back)],
        [VMEM, VMEM],
        [pltpu.HBM(half, BF), jax.ShapeDtypeStruct(half, BF), pltpu.VMEM(half, BF), pltpu.VMEM(half, BF)],
        [HBM, ANY, VMEM, VMEM],
        [pltpu.SemaphoreType.DMA((2, 4))],
    )


def write_rows(order, wide_pieces, placed_pieces, blended, anchor, size=1024):
    n, m = len(wide_pieces), len(placed_pieces)
    counts = [len(arrays) for arrays, _, _ in wide_pieces]
    flat = [x for arrays, _, _ in wide_pieces for x in arrays]
    late = sum(counts[:-1])
    outs = [pltpu.HBM((ROWS, D), F32)] * (n > 0) + [pltpu.HBM((16, 2, ROWS, WIDTH), BF)] * (m > 0)
    earlier = [x for x, k in ((blended, n), (anchor, m)) if k and x is not None]

    def body(at, *refs):
        flat_refs, refs = list(refs[: len(flat)]), refs[len(flat) :]
        placed, refs = refs[:m], refs[m + len(earlier) :]
        out_refs, (wide, held, sems, placed_sems, held_sem) = refs[: len(outs)], refs[len(outs) :]

        def place(i, p):
            some = pl.ds(4 * p, 4)
            core, chip, same = placed_pieces[i][1:]
            there = pl.ds(first_row(at, core, chip, 0), QUARTER)
            return pltpu.make_async_copy(
                placed[i].at[some], out_refs[-1].at[some, plane(at, same), there, :], placed_sems.at[i, p]
            )

        def copy(i, p):
            there = pl.ds(first_row(at, *wide_pieces[i][1:], 0), QUARTER)
            return pltpu.make_async_copy(
                wide.at[i, :, span_of(p)], out_refs[0].at[there, span_of(p)], sems.at[i, p]
            )

        def work(i, tiles, p):
            if len(tiles) == 1:
                for k in range(PER):
                    g = p * PER + k
                    wide[i, :, columns(g)] = tiles[0][g].astype(F32)
            else:
                for k in range(PER // 2):
                    yz = p * (PER // 2) + k
                    for ref, same in zip(tiles, (True, False)):
                        wide[i, :, columns(2 * yz + plane(at, same))] = ref[yz].astype(F32)
            copy(i, p).start()

        if n:
            last = pltpu.make_async_copy(flat_refs[late], held, held_sem)
            last.start()
            flat_refs[late] = held
        for i in range(m):
            each(4, lambda p, i=i: place(i, p).start())
        for i in range(n):
            if i == n - 1:
                last.wait()
            tiles = flat_refs[sum(counts[:i]) : sum(counts[: i + 1])]
            each(PARTS, lambda p, i=i, tiles=tiles: work(i, tiles, p))
        for i in range(n):
            each(PARTS, lambda p, i=i: copy(i, p).wait())
        for i in range(m):
            each(4, lambda p, i=i: place(i, p).wait())

    in_hbm = lambda x: pltpu.with_memory_space_constraint(x, pltpu.HBM)
    args = [in_hbm(x) if i == late else in_vmem(x) for i, x in enumerate(flat)]
    specs = [HBM if i == late else VMEM for i in range(len(flat))]
    return order.run(
        body,
        "write_rows",
        args + [in_vmem(x) for x, *_ in placed_pieces] + earlier,
        specs + [VMEM] * m + [HBM] * len(earlier),
        outs,
        [HBM] * len(outs),
        [
            pltpu.VMEM((max(n, 1), QUARTER, D if n else 128), F32),
            pltpu.VMEM(flat[late].shape if n else (1, 16, 128), BF),
            pltpu.SemaphoreType.DMA((max(n, 1), PARTS)),
            pltpu.SemaphoreType.DMA((max(m, 1), 4)),
            pltpu.SemaphoreType.DMA,
        ],
        {len(flat) + m + 1 + k: k for k in range(len(earlier))},
        size,
    )


def per_device(policies, anchor):
    policy = pltpu.with_memory_space_constraint(policies[0], pltpu.HBM)
    shards = pltpu.with_memory_space_constraint(anchor.reshape(16, 2, ROWS, WIDTH), pltpu.HBM)
    order = Order(jnp.stack([lax.axis_index(name) for name in ("xl", "c", "xh")]).astype(jnp.int32))
    swap = [(0, 1), (1, 0)]
    groups = exchange_groups()

    def exchange(tiles):
        return lax.all_to_all(
            tiles, AXES, split_axis=0, concat_axis=0, axis_index_groups=groups, tiled=True
        )

    def core(tiles):
        return lax.ppermute(tiles, "c", swap)

    def chip(tiles):
        return lax.ppermute(tiles, "xl", swap)

    theirs = core(cast_rows(order, policy))
    picked, rows = pick_rows(order, shards, policy)
    other = chip(add_theirs(order, rows, theirs))
    fetched = exchange(picked)
    own = add_own(order, policy, [core(tiles) for tiles in cast_own(order, policy)])

    own = blend_rows(order, own, other, fetched)
    finished = chip(own)
    back = exchange(own)
    pieces = [([core(own)], False, True), ([own], True, True)]
    (blended,) = write_rows(order, pieces, [], None, None, WRITE_COST)

    first, low, second, high = split_planes(order, finished, back)
    back_first = lax.all_to_all(first, ("y", "z"), split_axis=0, concat_axis=0, tiled=True)
    back_second = chip(high)
    pieces = [
        (low, True, True, True),
        (core(low), False, True, True),
        (high, True, False, False),
        (core(high), False, False, False),
    ]
    (new_anchor,) = write_rows(order, [], pieces, None, None)
    pieces = [([core(first), core(second)], False, False), ([first, second], True, False)]
    (blended,) = write_rows(order, pieces, [], blended, None)
    back_second = order.behind(back_second)
    back_first = order.behind(back_first)
    pieces = [(back_first, True, False, True), (back_second, True, True, False)]
    (new_anchor,) = write_rows(order, [], pieces, None, new_anchor, LAST_COST)
    pieces = [(core(back_first), False, False, True), (core(back_second), False, True, False)]
    (new_anchor,) = write_rows(order, [], pieces, None, new_anchor)
    return blended, new_anchor.reshape(SHARDS * ROWS, WIDTH)


def solution(mesh):
    fine = Mesh(mesh.devices.reshape(SIZES), AXES)
    shards = ("y", "z", "xh")
    return jax.shard_map(
        per_device,
        mesh=fine,
        in_specs=(P(("xl", "c"), shards, None), P(None, shards)),
        out_specs=(P(shards, None), P(None, shards)),
        check_vma=False,
    )
```

```python
import jax
import jax.numpy as jnp
import numpy as np
from jax import lax
from jax.experimental import pallas as pl
from jax.experimental.pallas import tpu as pltpu
from jax.sharding import Mesh, PartitionSpec as P

blend_rate = 0.3
GROUPS = 4

AXES = ("xl", "c", "y", "z", "xh")
SIZES = (2, 2, 4, 4, 2)
SHARDS = 32
ROWS = 256
WIDTH = 256
D = 8192
HALF = 128
QUARTER = 64
R = 32
BF = jnp.bfloat16
F32 = jnp.float32
VMEM_LIMIT = 10 << 20
PARTS = 8
PER = SHARDS // PARTS
WRITE_COST = 11 << 20
LAST_COST = 37 << 20
ANY = pl.BlockSpec(memory_space=pl.ANY)
HBM = pl.BlockSpec(memory_space=pltpu.HBM)
VMEM = pl.BlockSpec(memory_space=pltpu.VMEM)
TOKEN = jax.ShapeDtypeStruct((8, 128), jnp.int32)


def exchange_groups():
    ids = np.arange(128).reshape(SIZES)
    return [
        [int(ids[flip ^ xh, c, y, z, xh]) for y in range(4) for z in range(4) for xh in range(2)]
        for flip in range(2)
        for c in range(2)
    ]


def in_vmem(x):
    return pltpu.with_memory_space_constraint(x, pltpu.VMEM)


class Order:
    def __init__(self, place):
        self.place = place
        self.token = None

    def behind(self, x):
        x, self.token = lax.optimization_barrier((x, self.token))
        return x

    def run(self, body, name, args, specs, outs, out_specs, scratch, aliases=None, size=1024):
        held = [] if self.token is None else [self.token]

        def ordered(at, *refs):
            ins, rest = refs[: len(args)], refs[len(args) + len(held) :]
            results, others = rest[: len(outs)], rest[len(outs) + 1 :]
            body(at, *ins, *results, *others)

        *results, self.token = pl.pallas_call(
            ordered,
            out_shape=[*outs, TOKEN],
            grid_spec=pltpu.PrefetchScalarGridSpec(
                num_scalar_prefetch=1,
                grid=(),
                in_specs=[*specs, *[ANY] * len(held)],
                out_specs=[*out_specs, ANY],
                scratch_shapes=scratch,
            ),
            input_output_aliases=aliases or {},
            compiler_params=pltpu.CompilerParams(vmem_limit_bytes=VMEM_LIMIT),
            cost_estimate=pl.CostEstimate(flops=0, bytes_accessed=size, transcendentals=0),
            name=name,
        )(self.place, *args, *held)
        return results


def columns(g):
    return pl.ds(pl.multiple_of(g * WIDTH, WIDTH), WIDTH)


def each(count, work):
    pl.loop(0, count)(work)


def first_row(at, core, chip, start, xl=None):
    xl = at[0] if xl is None else xl
    half = at[1] if core else 1 - at[1]
    quarter = xl if chip else 1 - xl
    return pl.multiple_of(half * HALF + quarter * QUARTER + start, 16)


def member_row(at, where, xh):
    differs = at[2] if xh == 0 else 1 - at[2]
    return first_row(at, *where, at[0] + differs - 2 * at[0] * differs)


def tiles_out(rows):
    return pltpu.VMEM((SHARDS, rows, WIDTH), BF)


def span_of(p):
    return pl.ds(pl.multiple_of(p * PER * WIDTH, WIDTH), PER * WIDTH)


def cast_rows(order, policy):
    def body(at, x_ref, o_ref, wide, sems):
        held = pl.ds(first_row(at, False, False, 0), QUARTER)

        def copy(p):
            return pltpu.make_async_copy(x_ref.at[held, span_of(p)], wide.at[:, span_of(p)], sems.at[p])

        def work(p):
            copy(p).wait()
            for k in range(PER):
                g = p * PER + k
                o_ref[g] = wide[:, columns(g)].astype(BF)

        each(PARTS, lambda p: copy(p).start())
        each(PARTS, work)

    (out,) = order.run(
        body,
        "cast_rows",
        (policy,),
        [HBM],
        [tiles_out(QUARTER)],
        [VMEM],
        [pltpu.VMEM((QUARTER, D), F32), pltpu.SemaphoreType.DMA((PARTS,))],
    )
    return out


def add_theirs(order, rows, tiles):
    def body(at, x_ref, t_ref, o_ref, held, sems):
        def store(p):
            some = pl.ds(p * PER, PER)
            return pltpu.make_async_copy(held.at[some], o_ref.at[some], sems.at[p])

        def work(p):
            for k in range(PER):
                g = p * PER + k
                held[g] = (x_ref[:, columns(g)] + t_ref[g].astype(F32)).astype(BF)
            store(p).start()

        each(PARTS, work)
        each(PARTS, lambda p: store(p).wait())

    (out,) = order.run(
        body,
        "add_theirs",
        (in_vmem(rows), in_vmem(tiles)),
        [VMEM, VMEM],
        [pltpu.HBM((SHARDS, QUARTER, WIDTH), BF)],
        [HBM],
        [pltpu.VMEM((SHARDS, QUARTER, WIDTH), BF), pltpu.SemaphoreType.DMA((PARTS,))],
    )
    return out


def cast_own(order, policy):
    def body(at, x_ref, low_ref, high_ref, wide, sems):
        held = pl.ds(first_row(at, False, True, 0), QUARTER)

        def copy(p):
            return pltpu.make_async_copy(x_ref.at[held, span_of(p)], wide.at[:, span_of(p)], sems.at[p])

        def work(p):
            copy(p).wait()
            for k in range(PER):
                g = p * PER + k
                low_ref[g] = wide[:R, columns(g)].astype(BF)
                high_ref[g] = wide[R:, columns(g)].astype(BF)

        each(PARTS, lambda p: copy(p).start())
        each(PARTS, work)

    return order.run(
        body,
        "cast_own",
        (policy,),
        [HBM],
        [tiles_out(R)] * 2,
        [VMEM] * 2,
        [pltpu.VMEM((QUARTER, D), F32), pltpu.SemaphoreType.DMA((PARTS,))],
    )


def add_own(order, policy, chunks):
    def body(at, x_ref, low_ref, high_ref, o_ref, wide, sems):
        held = pl.ds(first_row(at, True, True, 0), QUARTER)

        def copy(p):
            return pltpu.make_async_copy(x_ref.at[held, span_of(p)], wide.at[:, span_of(p)], sems.at[p])

        def work(p):
            copy(p).wait()
            for k in range(PER):
                g = p * PER + k
                o_ref[g, :R] = (wide[:R, columns(g)] + low_ref[g].astype(F32)).astype(BF)
                o_ref[g, R:] = (wide[R:, columns(g)] + high_ref[g].astype(F32)).astype(BF)

        each(PARTS, lambda p: copy(p).start())
        each(PARTS, work)

    (out,) = order.run(
        body,
        "add_own",
        (policy, *[in_vmem(tiles) for tiles in chunks]),
        [HBM, VMEM, VMEM],
        [tiles_out(QUARTER)],
        [VMEM],
        [pltpu.VMEM((QUARTER, D), F32), pltpu.SemaphoreType.DMA((PARTS,))],
    )
    return out


def pick_rows(order, anchor, policy):
    def body(at, a_ref, x_ref, p_ref, rows_ref, held, in_sems, out_sems, x_sems):
        rows = [member_row(at, (True, True, 0), xh) for xh in range(2)]
        theirs = pl.ds(first_row(at, True, False, 0), QUARTER)

        def fetch(p, xh):
            some = pl.ds(4 * p, 4)
            return pltpu.make_async_copy(
                a_ref.at[some, xh, pl.ds(rows[xh], QUARTER), :], held.at[some, xh], in_sems.at[xh, p]
            )

        def store(p, xh):
            some = pl.ds(4 * p, 4)
            return pltpu.make_async_copy(held.at[some, xh], p_ref.at[some, xh], out_sems.at[xh, p])

        def copy(p):
            return pltpu.make_async_copy(
                x_ref.at[theirs, span_of(p)], rows_ref.at[:, span_of(p)], x_sems.at[p]
            )

        def forward(p, xh):
            fetch(p, xh).wait()
            store(p, xh).start()

        for xh in range(2):
            each(4, lambda p, xh=xh: fetch(p, xh).start())
        each(PARTS, lambda p: copy(p).start())
        for xh in range(2):
            each(4, lambda p, xh=xh: forward(p, xh))
        each(PARTS, lambda p: copy(p).wait())
        for xh in range(2):
            each(4, lambda p, xh=xh: store(p, xh).wait())

    picked, rows = order.run(
        body,
        "pick_rows",
        (anchor, policy),
        [HBM, HBM],
        [pltpu.HBM((16, 2, QUARTER, WIDTH), BF), pltpu.VMEM((QUARTER, D), F32)],
        [HBM, VMEM],
        [
            pltpu.VMEM((16, 2, QUARTER, WIDTH), BF),
            pltpu.SemaphoreType.DMA((2, 4)),
            pltpu.SemaphoreType.DMA((2, 4)),
            pltpu.SemaphoreType.DMA((PARTS,)),
        ],
    )
    return picked.reshape(SHARDS, QUARTER, WIDTH), rows


def blend_rows(order, own, other, anchor):
    def body(at, x_ref, t_ref, a_ref, o_ref, held, sems):
        def store(p):
            some = pl.ds(p * PER, PER)
            return pltpu.make_async_copy(held.at[some], o_ref.at[some], sems.at[p])

        def work(p):
            for k in range(PER):
                g = p * PER + k
                total = x_ref[g].astype(F32) + t_ref[g].astype(F32)
                new = (1.0 - blend_rate) * a_ref[g].astype(F32) + (blend_rate / GROUPS) * total
                held[g] = new.astype(BF)
            store(p).start()

        each(PARTS, work)
        each(PARTS, lambda p: store(p).wait())

    (out,) = order.run(
        body,
        "blend_rows",
        [in_vmem(x) for x in (own, other, anchor)],
        [VMEM] * 3,
        [pltpu.HBM((SHARDS, QUARTER, WIDTH), BF)],
        [HBM],
        [pltpu.VMEM((SHARDS, QUARTER, WIDTH), BF), pltpu.SemaphoreType.DMA((PARTS,))],
    )
    return out


def plane(at, same):
    return at[2] if same else 1 - at[2]


def split_planes(order, finished, back):
    def body(at, f_ref, b_ref, first_ref, high_ref, sems):
        def store(p):
            some = pl.ds(4 * p, 4)
            return pltpu.make_async_copy(f_ref.at[some, plane(at, True)], first_ref.at[some], sems.at[p])

        def work(k):
            high_ref[k] = b_ref[k, plane(at, False)]

        each(4, lambda p: store(p).start())
        each(16, work)
        each(4, lambda p: store(p).wait())

    half = (16, QUARTER, WIDTH)
    return order.run(
        body,
        "split_planes",
        [in_vmem(x.reshape(16, 2, QUARTER, WIDTH)) for x in (finished, back)],
        [VMEM, VMEM],
        [pltpu.HBM(half, BF), pltpu.VMEM(half, BF)],
        [HBM, VMEM],
        [pltpu.SemaphoreType.DMA((4,))],
    )


def place_back(order, own, other):
    def body(at, own_ref, other_ref, out_ref, held, sems, held_sems):
        def there(core, same, p):
            row = first_row(at, core, same, 0)
            return out_ref.at[pl.ds(4 * p, 4), plane(at, same), pl.ds(row, QUARTER), :]

        def place(ref, core, same, p):
            return pltpu.make_async_copy(
                ref.at[pl.ds(4 * p, 4), plane(at, same)],
                there(core, same, p),
                sems.at[int(core), int(same), p],
            )

        def fetch(p):
            some = pl.ds(4 * p, 4)
            return pltpu.make_async_copy(other_ref.at[some], held.at[some], held_sems.at[p])

        def forward(p):
            fetch(p).wait()
            for same in (True, False):
                place(held, False, same, p).start()

        each(4, lambda p: fetch(p).start())
        for same in (True, False):
            each(4, lambda p, same=same: place(own_ref, True, same, p).start())
        each(4, forward)
        for ref, core in ((own_ref, True), (held, False)):
            for same in (True, False):
                each(4, lambda p, ref=ref, core=core, same=same: place(ref, core, same, p).wait())

    shape = (16, 2, QUARTER, WIDTH)
    return order.run(
        body,
        "place_back",
        [in_vmem(own.reshape(shape)), other.reshape(shape)],
        [VMEM, ANY],
        [pltpu.HBM((16, 2, ROWS, WIDTH), BF)],
        [HBM],
        [
            pltpu.VMEM(shape, BF),
            pltpu.SemaphoreType.DMA((2, 2, 4)),
            pltpu.SemaphoreType.DMA((4,)),
        ],
    )[0]


def write_rows(order, wide_pieces, placed_pieces, blended, anchor, size=1024, late_in_hbm=False):
    n, m = len(wide_pieces), len(placed_pieces)
    counts = [len(arrays) for arrays, _, _ in wide_pieces]
    flat = [x for arrays, _, _ in wide_pieces for x in arrays]
    late = sum(counts[:-1])
    outs = [pltpu.HBM((ROWS, D), F32)] * (n > 0) + [pltpu.HBM((16, 2, ROWS, WIDTH), BF)] * (m > 0)
    earlier = [x for x, k in ((blended, n), (anchor, m)) if k and x is not None]

    def body(at, *refs):
        flat_refs, refs = list(refs[: len(flat)]), refs[len(flat) :]
        placed, refs = refs[:m], refs[m + len(earlier) :]
        out_refs, (wide, held, sems, placed_sems, held_sem) = refs[: len(outs)], refs[len(outs) :]

        def place(i, p):
            some = pl.ds(4 * p, 4)
            core, chip, same = placed_pieces[i][1:]
            there = pl.ds(first_row(at, core, chip, 0), QUARTER)
            return pltpu.make_async_copy(
                placed[i].at[some], out_refs[-1].at[some, plane(at, same), there, :], placed_sems.at[i, p]
            )

        def copy(i, p):
            there = pl.ds(first_row(at, *wide_pieces[i][1:], 0), QUARTER)
            return pltpu.make_async_copy(
                wide.at[i, :, span_of(p)], out_refs[0].at[there, span_of(p)], sems.at[i, p]
            )

        def work(i, tiles, p):
            if len(tiles) == 1:
                for k in range(PER):
                    g = p * PER + k
                    wide[i, :, columns(g)] = tiles[0][g].astype(F32)
            else:
                for k in range(PER // 2):
                    yz = p * (PER // 2) + k
                    for ref, same in zip(tiles, (True, False)):
                        wide[i, :, columns(2 * yz + plane(at, same))] = ref[yz].astype(F32)
            copy(i, p).start()

        if n:
            last = pltpu.make_async_copy(flat_refs[late], held, held_sem)
            last.start()
            flat_refs[late] = held
        for i in range(m):
            each(4, lambda p, i=i: place(i, p).start())
        for i in range(n):
            if i == n - 1:
                last.wait()
            tiles = flat_refs[sum(counts[:i]) : sum(counts[: i + 1])]
            each(PARTS, lambda p, i=i, tiles=tiles: work(i, tiles, p))
        for i in range(n):
            each(PARTS, lambda p, i=i: copy(i, p).wait())
        for i in range(m):
            each(4, lambda p, i=i: place(i, p).wait())

    args = [x if i == late else in_vmem(x) for i, x in enumerate(flat)]
    specs = [ANY if i == late else VMEM for i in range(len(flat))]
    if late_in_hbm:
        args[late] = pltpu.with_memory_space_constraint(args[late], pltpu.HBM)
        specs[late] = HBM
    return order.run(
        body,
        "write_rows",
        args + [in_vmem(x) for x, *_ in placed_pieces] + earlier,
        specs + [VMEM] * m + [HBM] * len(earlier),
        outs,
        [HBM] * len(outs),
        [
            pltpu.VMEM((max(n, 1), QUARTER, D if n else 128), F32),
            pltpu.VMEM(flat[late].shape if n else (1, 16, 128), BF),
            pltpu.SemaphoreType.DMA((max(n, 1), PARTS)),
            pltpu.SemaphoreType.DMA((max(m, 1), 4)),
            pltpu.SemaphoreType.DMA,
        ],
        {len(flat) + m + 1 + k: k for k in range(len(earlier))},
        size,
    )


def per_device(policies, anchor):
    policy = pltpu.with_memory_space_constraint(policies[0], pltpu.HBM)
    shards = pltpu.with_memory_space_constraint(anchor.reshape(16, 2, ROWS, WIDTH), pltpu.HBM)
    order = Order(jnp.stack([lax.axis_index(name) for name in ("xl", "c", "xh")]).astype(jnp.int32))
    swap = [(0, 1), (1, 0)]
    groups = exchange_groups()

    def exchange(tiles):
        return lax.all_to_all(
            tiles, AXES, split_axis=0, concat_axis=0, axis_index_groups=groups, tiled=True
        )

    def core(tiles):
        return lax.ppermute(tiles, "c", swap)

    def chip(tiles):
        return lax.ppermute(tiles, "xl", swap)

    theirs = core(cast_rows(order, policy))
    picked, rows = pick_rows(order, shards, policy)
    other = chip(add_theirs(order, rows, theirs))
    fetched = exchange(picked)
    own = add_own(order, policy, [core(tiles) for tiles in cast_own(order, policy)])

    own = blend_rows(order, own, other, fetched)
    finished = chip(own)
    back = exchange(own)
    pieces = [([core(own)], False, True), ([own], True, True)]
    (blended,) = write_rows(order, pieces, [], None, None, WRITE_COST, late_in_hbm=True)

    first, high = split_planes(order, finished, back)
    back_first = lax.all_to_all(first, ("y", "z"), split_axis=0, concat_axis=0, tiled=True)
    back_second = chip(high)
    finished, back = order.behind(finished), order.behind(back)
    new_anchor = place_back(order, back, core(back))
    pieces = [([finished], True, False), ([core(finished)], False, False)]
    (blended,) = write_rows(order, pieces, [], blended, None)
    back_second = order.behind(back_second)
    back_first = order.behind(back_first)
    pieces = [(back_first, True, False, True), (back_second, True, True, False)]
    (new_anchor,) = write_rows(order, [], pieces, None, new_anchor, LAST_COST)
    pieces = [(core(back_first), False, False, True), (core(back_second), False, True, False)]
    (new_anchor,) = write_rows(order, [], pieces, None, new_anchor)
    return blended, new_anchor.reshape(SHARDS * ROWS, WIDTH)


def solution(mesh):
    fine = Mesh(mesh.devices.reshape(SIZES), AXES)
    shards = ("y", "z", "xh")
    return jax.shard_map(
        per_device,
        mesh=fine,
        in_specs=(P(("xl", "c"), shards, None), P(None, shards)),
        out_specs=(P(shards, None), P(None, shards)),
        check_vma=False,
    )
```

```python
import jax
import jax.numpy as jnp
import numpy as np
from jax import lax
from jax.experimental import pallas as pl
from jax.experimental.pallas import tpu as pltpu
from jax.sharding import Mesh, PartitionSpec as P

blend_rate = 0.3
GROUPS = 4

AXES = ("xl", "c", "y", "z", "xh")
SIZES = (2, 2, 4, 4, 2)
SHARDS = 32
ROWS = 256
WIDTH = 256
D = 8192
HALF = 128
QUARTER = 64
R = 32
BF = jnp.bfloat16
F32 = jnp.float32
VMEM_LIMIT = 10 << 20
PARTS = 8
PER = SHARDS // PARTS
WRITE_COST = 11 << 20
LAST_COST = 37 << 20
ANY = pl.BlockSpec(memory_space=pl.ANY)
HBM = pl.BlockSpec(memory_space=pltpu.HBM)
VMEM = pl.BlockSpec(memory_space=pltpu.VMEM)
TOKEN = jax.ShapeDtypeStruct((8, 128), jnp.int32)


def exchange_groups():
    ids = np.arange(128).reshape(SIZES)
    return [
        [int(ids[flip ^ xh, c, y, z, xh]) for y in range(4) for z in range(4) for xh in range(2)]
        for flip in range(2)
        for c in range(2)
    ]


def in_vmem(x):
    return pltpu.with_memory_space_constraint(x, pltpu.VMEM)


class Order:
    def __init__(self, place):
        self.place = place
        self.token = None

    def behind(self, x):
        x, self.token = lax.optimization_barrier((x, self.token))
        return x

    def run(self, body, name, args, specs, outs, out_specs, scratch, aliases=None, size=1024):
        held = [] if self.token is None else [self.token]

        def ordered(at, *refs):
            ins, rest = refs[: len(args)], refs[len(args) + len(held) :]
            results, others = rest[: len(outs)], rest[len(outs) + 1 :]
            body(at, *ins, *results, *others)

        *results, self.token = pl.pallas_call(
            ordered,
            out_shape=[*outs, TOKEN],
            grid_spec=pltpu.PrefetchScalarGridSpec(
                num_scalar_prefetch=1,
                grid=(),
                in_specs=[*specs, *[ANY] * len(held)],
                out_specs=[*out_specs, ANY],
                scratch_shapes=scratch,
            ),
            input_output_aliases=aliases or {},
            compiler_params=pltpu.CompilerParams(vmem_limit_bytes=VMEM_LIMIT),
            cost_estimate=pl.CostEstimate(flops=0, bytes_accessed=size, transcendentals=0),
            name=name,
        )(self.place, *args, *held)
        return results


def columns(g):
    return pl.ds(pl.multiple_of(g * WIDTH, WIDTH), WIDTH)


def each(count, work):
    pl.loop(0, count)(work)


def first_row(at, core, chip, start, xl=None):
    xl = at[0] if xl is None else xl
    half = at[1] if core else 1 - at[1]
    quarter = xl if chip else 1 - xl
    return pl.multiple_of(half * HALF + quarter * QUARTER + start, 16)


def member_row(at, where, xh):
    differs = at[2] if xh == 0 else 1 - at[2]
    return first_row(at, *where, at[0] + differs - 2 * at[0] * differs)


def tiles_out(rows):
    return pltpu.VMEM((SHARDS, rows, WIDTH), BF)


def span_of(p):
    return pl.ds(pl.multiple_of(p * PER * WIDTH, WIDTH), PER * WIDTH)


def cast_rows(order, policy):
    def body(at, x_ref, o_ref, wide, sems):
        held = pl.ds(first_row(at, False, False, 0), QUARTER)

        def copy(p):
            return pltpu.make_async_copy(x_ref.at[held, span_of(p)], wide.at[:, span_of(p)], sems.at[p])

        def work(p):
            copy(p).wait()
            for k in range(PER):
                g = p * PER + k
                o_ref[g] = wide[:, columns(g)].astype(BF)

        each(PARTS, lambda p: copy(p).start())
        each(PARTS, work)

    (out,) = order.run(
        body,
        "cast_rows",
        (policy,),
        [HBM],
        [tiles_out(QUARTER)],
        [VMEM],
        [pltpu.VMEM((QUARTER, D), F32), pltpu.SemaphoreType.DMA((PARTS,))],
    )
    return out


def add_theirs(order, rows, tiles, picked):
    def body(at, x_ref, t_ref, p_ref, o_ref, q_ref, held, sems, picked_sems):
        def store(p):
            some = pl.ds(p * PER, PER)
            return pltpu.make_async_copy(held.at[some], o_ref.at[some], sems.at[p])

        def copy(p):
            some = pl.ds(p * PER, PER)
            return pltpu.make_async_copy(p_ref.at[some], q_ref.at[some], picked_sems.at[p])

        def work(p):
            for k in range(PER):
                g = p * PER + k
                held[g] = (x_ref[:, columns(g)] + t_ref[g].astype(F32)).astype(BF)
            store(p).start()

        each(PARTS, lambda p: copy(p).start())
        each(PARTS, work)
        each(PARTS, lambda p: copy(p).wait())
        each(PARTS, lambda p: store(p).wait())

    return order.run(
        body,
        "add_theirs",
        [in_vmem(x) for x in (rows, tiles, picked)],
        [VMEM] * 3,
        [pltpu.HBM((SHARDS, QUARTER, WIDTH), BF)] * 2,
        [HBM] * 2,
        [
            pltpu.VMEM((SHARDS, QUARTER, WIDTH), BF),
            pltpu.SemaphoreType.DMA((PARTS,)),
            pltpu.SemaphoreType.DMA((PARTS,)),
        ],
    )


def cast_own(order, policy):
    def body(at, x_ref, low_ref, high_ref, wide, sems):
        held = pl.ds(first_row(at, False, True, 0), QUARTER)

        def copy(p):
            return pltpu.make_async_copy(x_ref.at[held, span_of(p)], wide.at[:, span_of(p)], sems.at[p])

        def work(p):
            copy(p).wait()
            for k in range(PER):
                g = p * PER + k
                low_ref[g] = wide[:R, columns(g)].astype(BF)
                high_ref[g] = wide[R:, columns(g)].astype(BF)

        each(PARTS, lambda p: copy(p).start())
        each(PARTS, work)

    return order.run(
        body,
        "cast_own",
        (policy,),
        [HBM],
        [tiles_out(R)] * 2,
        [VMEM] * 2,
        [pltpu.VMEM((QUARTER, D), F32), pltpu.SemaphoreType.DMA((PARTS,))],
    )


def add_own(order, policy, chunks):
    def body(at, x_ref, low_ref, high_ref, o_ref, wide, sems):
        held = pl.ds(first_row(at, True, True, 0), QUARTER)

        def copy(p):
            return pltpu.make_async_copy(x_ref.at[held, span_of(p)], wide.at[:, span_of(p)], sems.at[p])

        def work(p):
            copy(p).wait()
            for k in range(PER):
                g = p * PER + k
                o_ref[g, :R] = (wide[:R, columns(g)] + low_ref[g].astype(F32)).astype(BF)
                o_ref[g, R:] = (wide[R:, columns(g)] + high_ref[g].astype(F32)).astype(BF)

        each(PARTS, lambda p: copy(p).start())
        each(PARTS, work)

    (out,) = order.run(
        body,
        "add_own",
        (policy, *[in_vmem(tiles) for tiles in chunks]),
        [HBM, VMEM, VMEM],
        [tiles_out(QUARTER)],
        [VMEM],
        [pltpu.VMEM((QUARTER, D), F32), pltpu.SemaphoreType.DMA((PARTS,))],
    )
    return out


def pick_rows(order, anchor, policy):
    def body(at, a_ref, x_ref, p_ref, rows_ref, a_sems, x_sems):
        rows = [member_row(at, (True, True, 0), xh) for xh in range(2)]
        theirs = pl.ds(first_row(at, True, False, 0), QUARTER)

        def fetch(p, xh):
            some = pl.ds(4 * p, 4)
            return pltpu.make_async_copy(
                a_ref.at[some, xh, pl.ds(rows[xh], QUARTER), :], p_ref.at[some, xh], a_sems.at[xh, p]
            )

        def copy(p):
            return pltpu.make_async_copy(
                x_ref.at[theirs, span_of(p)], rows_ref.at[:, span_of(p)], x_sems.at[p]
            )

        each(PARTS, lambda p: copy(p).start())
        for xh in range(2):
            each(4, lambda p, xh=xh: fetch(p, xh).start())
        each(PARTS, lambda p: copy(p).wait())
        for xh in range(2):
            each(4, lambda p, xh=xh: fetch(p, xh).wait())

    picked, rows = order.run(
        body,
        "pick_rows",
        (anchor, policy),
        [HBM, HBM],
        [pltpu.VMEM((16, 2, QUARTER, WIDTH), BF), pltpu.VMEM((QUARTER, D), F32)],
        [VMEM, VMEM],
        [pltpu.SemaphoreType.DMA((2, 4)), pltpu.SemaphoreType.DMA((PARTS,))],
    )
    return picked.reshape(SHARDS, QUARTER, WIDTH), rows


def blend_rows(order, own, other, anchor):
    def body(at, x_ref, t_ref, a_ref, o_ref, held, sems):
        def store(p):
            some = pl.ds(p * PER, PER)
            return pltpu.make_async_copy(held.at[some], o_ref.at[some], sems.at[p])

        def work(p):
            for k in range(PER):
                g = p * PER + k
                total = x_ref[g].astype(F32) + t_ref[g].astype(F32)
                new = (1.0 - blend_rate) * a_ref[g].astype(F32) + (blend_rate / GROUPS) * total
                held[g] = new.astype(BF)
            store(p).start()

        each(PARTS, work)
        each(PARTS, lambda p: store(p).wait())

    (out,) = order.run(
        body,
        "blend_rows",
        [in_vmem(x) for x in (own, other, anchor)],
        [VMEM] * 3,
        [pltpu.HBM((SHARDS, QUARTER, WIDTH), BF)],
        [HBM],
        [pltpu.VMEM((SHARDS, QUARTER, WIDTH), BF), pltpu.SemaphoreType.DMA((PARTS,))],
    )
    return out


def plane(at, same):
    return at[2] if same else 1 - at[2]


def split_planes(order, finished, back):
    def body(at, f_ref, b_ref, first_ref, high_ref, sems):
        def stores(p):
            some = pl.ds(4 * p, 4)
            ends = ((f_ref, True, first_ref), (b_ref, False, high_ref))
            return [
                pltpu.make_async_copy(x.at[some, plane(at, same)], o.at[some], sems.at[i, p])
                for i, (x, same, o) in enumerate(ends)
            ]

        def start(p):
            for store in stores(p):
                store.start()

        def finish(p):
            for store in stores(p):
                store.wait()

        each(4, start)
        each(4, finish)

    half = (16, QUARTER, WIDTH)
    return order.run(
        body,
        "split_planes",
        [in_vmem(x.reshape(16, 2, QUARTER, WIDTH)) for x in (finished, back)],
        [VMEM, VMEM],
        [pltpu.HBM(half, BF)] * 2,
        [HBM] * 2,
        [pltpu.SemaphoreType.DMA((2, 4))],
    )


def place_back(order, own, other):
    def body(at, own_ref, other_ref, out_ref, held, sems, held_sems):
        def there(core, same, p):
            row = first_row(at, core, same, 0)
            return out_ref.at[pl.ds(4 * p, 4), plane(at, same), pl.ds(row, QUARTER), :]

        def place(ref, core, same, p):
            return pltpu.make_async_copy(
                ref.at[pl.ds(4 * p, 4), plane(at, same)],
                there(core, same, p),
                sems.at[int(core), int(same), p],
            )

        def fetch(p):
            some = pl.ds(4 * p, 4)
            return pltpu.make_async_copy(other_ref.at[some], held.at[some], held_sems.at[p])

        def forward(p):
            fetch(p).wait()
            for same in (True, False):
                place(held, False, same, p).start()

        each(4, lambda p: fetch(p).start())
        for same in (True, False):
            each(4, lambda p, same=same: place(own_ref, True, same, p).start())
        each(4, forward)
        for ref, core in ((own_ref, True), (held, False)):
            for same in (True, False):
                each(4, lambda p, ref=ref, core=core, same=same: place(ref, core, same, p).wait())

    shape = (16, 2, QUARTER, WIDTH)
    return order.run(
        body,
        "place_back",
        [in_vmem(own.reshape(shape)), other.reshape(shape)],
        [VMEM, ANY],
        [pltpu.HBM((16, 2, ROWS, WIDTH), BF)],
        [HBM],
        [
            pltpu.VMEM(shape, BF),
            pltpu.SemaphoreType.DMA((2, 2, 4)),
            pltpu.SemaphoreType.DMA((4,)),
        ],
    )[0]


def write_rows(order, wide_pieces, placed_pieces, blended, anchor, size=1024, late_in_hbm=False):
    n, m = len(wide_pieces), len(placed_pieces)
    counts = [len(arrays) for arrays, _, _ in wide_pieces]
    flat = [x for arrays, _, _ in wide_pieces for x in arrays]
    late = sum(counts[:-1])
    outs = [pltpu.HBM((ROWS, D), F32)] * (n > 0) + [pltpu.HBM((16, 2, ROWS, WIDTH), BF)] * (m > 0)
    earlier = [x for x, k in ((blended, n), (anchor, m)) if k and x is not None]

    def body(at, *refs):
        flat_refs, refs = list(refs[: len(flat)]), refs[len(flat) :]
        placed, refs = refs[:m], refs[m + len(earlier) :]
        out_refs, (wide, held, sems, placed_sems, held_sem) = refs[: len(outs)], refs[len(outs) :]

        def place(i, p):
            some = pl.ds(4 * p, 4)
            core, chip, same = placed_pieces[i][1:]
            there = pl.ds(first_row(at, core, chip, 0), QUARTER)
            return pltpu.make_async_copy(
                placed[i].at[some], out_refs[-1].at[some, plane(at, same), there, :], placed_sems.at[i, p]
            )

        def copy(i, p):
            there = pl.ds(first_row(at, *wide_pieces[i][1:], 0), QUARTER)
            return pltpu.make_async_copy(
                wide.at[i, :, span_of(p)], out_refs[0].at[there, span_of(p)], sems.at[i, p]
            )

        def work(i, tiles, p):
            if len(tiles) == 1:
                for k in range(PER):
                    g = p * PER + k
                    wide[i, :, columns(g)] = tiles[0][g].astype(F32)
            else:
                for k in range(PER // 2):
                    yz = p * (PER // 2) + k
                    for ref, same in zip(tiles, (True, False)):
                        wide[i, :, columns(2 * yz + plane(at, same))] = ref[yz].astype(F32)
            copy(i, p).start()

        if n:
            last = pltpu.make_async_copy(flat_refs[late], held, held_sem)
            last.start()
            flat_refs[late] = held
        for i in range(m):
            each(4, lambda p, i=i: place(i, p).start())
        for i in range(n):
            if i == n - 1:
                last.wait()
            tiles = flat_refs[sum(counts[:i]) : sum(counts[: i + 1])]
            each(PARTS, lambda p, i=i, tiles=tiles: work(i, tiles, p))
        for i in range(n):
            each(PARTS, lambda p, i=i: copy(i, p).wait())
        for i in range(m):
            each(4, lambda p, i=i: place(i, p).wait())

    args = [x if i == late else in_vmem(x) for i, x in enumerate(flat)]
    specs = [ANY if i == late else VMEM for i in range(len(flat))]
    if late_in_hbm:
        args[late] = pltpu.with_memory_space_constraint(args[late], pltpu.HBM)
        specs[late] = HBM
    return order.run(
        body,
        "write_rows",
        args + [in_vmem(x) for x, *_ in placed_pieces] + earlier,
        specs + [VMEM] * m + [HBM] * len(earlier),
        outs,
        [HBM] * len(outs),
        [
            pltpu.VMEM((max(n, 1), QUARTER, D if n else 128), F32),
            pltpu.VMEM(flat[late].shape if n else (1, 16, 128), BF),
            pltpu.SemaphoreType.DMA((max(n, 1), PARTS)),
            pltpu.SemaphoreType.DMA((max(m, 1), 4)),
            pltpu.SemaphoreType.DMA,
        ],
        {len(flat) + m + 1 + k: k for k in range(len(earlier))},
        size,
    )


def per_device(policies, anchor):
    policy = pltpu.with_memory_space_constraint(policies[0], pltpu.HBM)
    shards = pltpu.with_memory_space_constraint(anchor.reshape(16, 2, ROWS, WIDTH), pltpu.HBM)
    order = Order(jnp.stack([lax.axis_index(name) for name in ("xl", "c", "xh")]).astype(jnp.int32))
    swap = [(0, 1), (1, 0)]
    groups = exchange_groups()

    def exchange(tiles):
        return lax.all_to_all(
            tiles, AXES, split_axis=0, concat_axis=0, axis_index_groups=groups, tiled=True
        )

    def core(tiles):
        return lax.ppermute(tiles, "c", swap)

    def chip(tiles):
        return lax.ppermute(tiles, "xl", swap)

    theirs = core(cast_rows(order, policy))
    picked, rows = pick_rows(order, shards, policy)
    theirs, picked = add_theirs(order, rows, theirs, picked)
    other = chip(theirs)
    fetched = exchange(picked)
    own = add_own(order, policy, [core(tiles) for tiles in cast_own(order, policy)])

    own = blend_rows(order, own, other, fetched)
    finished = chip(own)
    back = exchange(own)
    pieces = [([core(own)], False, True), ([own], True, True)]
    (blended,) = write_rows(order, pieces, [], None, None, WRITE_COST, late_in_hbm=True)

    first, high = split_planes(order, finished, back)
    back_first = lax.all_to_all(first, ("y", "z"), split_axis=0, concat_axis=0, tiled=True)
    back_second = chip(high)
    finished, back = order.behind(finished), order.behind(back)
    new_anchor = place_back(order, back, core(back))
    pieces = [([finished], True, False), ([core(finished)], False, False)]
    (blended,) = write_rows(order, pieces, [], blended, None)
    back_second = order.behind(back_second)
    back_first = order.behind(back_first)
    pieces = [(back_first, True, False, True), (back_second, True, True, False)]
    (new_anchor,) = write_rows(order, [], pieces, None, new_anchor, LAST_COST)
    pieces = [(core(back_first), False, False, True), (core(back_second), False, True, False)]
    (new_anchor,) = write_rows(order, [], pieces, None, new_anchor)
    return blended, new_anchor.reshape(SHARDS * ROWS, WIDTH)


def solution(mesh):
    fine = Mesh(mesh.devices.reshape(SIZES), AXES)
    shards = ("y", "z", "xh")
    return jax.shard_map(
        per_device,
        mesh=fine,
        in_specs=(P(("xl", "c"), shards, None), P(None, shards)),
        out_specs=(P(shards, None), P(None, shards)),
        check_vma=False,
    )
```

```python
import jax
import jax.numpy as jnp
import numpy as np
from jax import lax
from jax.experimental import pallas as pl
from jax.experimental.pallas import tpu as pltpu
from jax.sharding import Mesh, PartitionSpec as P

blend_rate = 0.3
GROUPS = 4

AXES = ("xl", "c", "y", "z", "xh")
SIZES = (2, 2, 4, 4, 2)
SHARDS = 32
ROWS = 256
WIDTH = 256
D = 8192
HALF = 128
QUARTER = 64
R = 32
BF = jnp.bfloat16
F32 = jnp.float32
VMEM_LIMIT = 10 << 20
PARTS = 8
PER = SHARDS // PARTS
WRITE_COST = 11 << 20
LAST_COST = 37 << 20
ANY = pl.BlockSpec(memory_space=pl.ANY)
HBM = pl.BlockSpec(memory_space=pltpu.HBM)
VMEM = pl.BlockSpec(memory_space=pltpu.VMEM)
TOKEN = jax.ShapeDtypeStruct((8, 128), jnp.int32)


def exchange_groups():
    ids = np.arange(128).reshape(SIZES)
    return [
        [int(ids[flip ^ xh, c, y, z, xh]) for xh in range(2) for y in range(4) for z in range(4)]
        for flip in range(2)
        for c in range(2)
    ]


def in_vmem(x):
    return pltpu.with_memory_space_constraint(x, pltpu.VMEM)


class Order:
    def __init__(self, place):
        self.place = place
        self.token = None

    def behind(self, x):
        x, self.token = lax.optimization_barrier((x, self.token))
        return x

    def run(self, body, name, args, specs, outs, out_specs, scratch, aliases=None, size=1024):
        held = [] if self.token is None else [self.token]

        def ordered(at, *refs):
            ins, rest = refs[: len(args)], refs[len(args) + len(held) :]
            results, others = rest[: len(outs)], rest[len(outs) + 1 :]
            body(at, *ins, *results, *others)

        *results, self.token = pl.pallas_call(
            ordered,
            out_shape=[*outs, TOKEN],
            grid_spec=pltpu.PrefetchScalarGridSpec(
                num_scalar_prefetch=1,
                grid=(),
                in_specs=[*specs, *[ANY] * len(held)],
                out_specs=[*out_specs, ANY],
                scratch_shapes=scratch,
            ),
            input_output_aliases=aliases or {},
            compiler_params=pltpu.CompilerParams(vmem_limit_bytes=VMEM_LIMIT),
            cost_estimate=pl.CostEstimate(flops=0, bytes_accessed=size, transcendentals=0),
            name=name,
        )(self.place, *args, *held)
        return results


def columns(g):
    return pl.ds(pl.multiple_of(g * WIDTH, WIDTH), WIDTH)


def slot(p, k):
    return (k % 2) * 16 + p * (PER // 2) + k // 2


def each(count, work):
    pl.loop(0, count)(work)


def first_row(at, core, chip, start, xl=None):
    xl = at[0] if xl is None else xl
    half = at[1] if core else 1 - at[1]
    quarter = xl if chip else 1 - xl
    return pl.multiple_of(half * HALF + quarter * QUARTER + start, 16)


def member_row(at, where, xh):
    differs = at[2] if xh == 0 else 1 - at[2]
    return first_row(at, *where, at[0] + differs - 2 * at[0] * differs)


def tiles_out(rows):
    return pltpu.VMEM((SHARDS, rows, WIDTH), BF)


def span_of(p):
    return pl.ds(pl.multiple_of(p * PER * WIDTH, WIDTH), PER * WIDTH)


def cast_rows(order, policy):
    def body(at, x_ref, o_ref, wide, sems):
        held = pl.ds(first_row(at, False, False, 0), QUARTER)

        def copy(p):
            return pltpu.make_async_copy(x_ref.at[held, span_of(p)], wide.at[:, span_of(p)], sems.at[p])

        def work(p):
            copy(p).wait()
            for k in range(PER):
                g = p * PER + k
                o_ref[slot(p, k)] = wide[:, columns(g)].astype(BF)

        each(PARTS, lambda p: copy(p).start())
        each(PARTS, work)

    (out,) = order.run(
        body,
        "cast_rows",
        (policy,),
        [HBM],
        [tiles_out(QUARTER)],
        [VMEM],
        [pltpu.VMEM((QUARTER, D), F32), pltpu.SemaphoreType.DMA((PARTS,))],
    )
    return out


def add_theirs(order, rows, tiles, picked):
    def body(at, x_ref, t_ref, p_ref, o_ref, q_ref, held, sems, picked_sems):
        def store(p):
            some = pl.ds(p * PER, PER)
            return pltpu.make_async_copy(held.at[some], o_ref.at[some], sems.at[p])

        def copy(p):
            some = pl.ds(p * PER, PER)
            return pltpu.make_async_copy(p_ref.at[some], q_ref.at[some], picked_sems.at[p])

        def work(p):
            for k in range(PER):
                at_slot = p * PER + k
                g = 2 * ((p & 3) * PER + k) + (p >> 2)
                held[at_slot] = (x_ref[:, columns(g)] + t_ref[at_slot].astype(F32)).astype(BF)
            store(p).start()

        each(PARTS, lambda p: copy(p).start())
        each(PARTS, work)
        each(PARTS, lambda p: copy(p).wait())
        each(PARTS, lambda p: store(p).wait())

    return order.run(
        body,
        "add_theirs",
        [in_vmem(x) for x in (rows, tiles, picked)],
        [VMEM] * 3,
        [pltpu.HBM((SHARDS, QUARTER, WIDTH), BF)] * 2,
        [HBM] * 2,
        [
            pltpu.VMEM((SHARDS, QUARTER, WIDTH), BF),
            pltpu.SemaphoreType.DMA((PARTS,)),
            pltpu.SemaphoreType.DMA((PARTS,)),
        ],
    )


def cast_own(order, policy):
    def body(at, x_ref, low_ref, high_ref, wide, sems):
        held = pl.ds(first_row(at, False, True, 0), QUARTER)

        def copy(p):
            return pltpu.make_async_copy(x_ref.at[held, span_of(p)], wide.at[:, span_of(p)], sems.at[p])

        def work(p):
            copy(p).wait()
            for k in range(PER):
                g = p * PER + k
                low_ref[slot(p, k)] = wide[:R, columns(g)].astype(BF)
                high_ref[slot(p, k)] = wide[R:, columns(g)].astype(BF)

        each(PARTS, lambda p: copy(p).start())
        each(PARTS, work)

    return order.run(
        body,
        "cast_own",
        (policy,),
        [HBM],
        [tiles_out(R)] * 2,
        [VMEM] * 2,
        [pltpu.VMEM((QUARTER, D), F32), pltpu.SemaphoreType.DMA((PARTS,))],
    )


def add_own(order, policy, chunks):
    def body(at, x_ref, low_ref, high_ref, o_ref, wide, sems):
        held = pl.ds(first_row(at, True, True, 0), QUARTER)

        def copy(p):
            return pltpu.make_async_copy(x_ref.at[held, span_of(p)], wide.at[:, span_of(p)], sems.at[p])

        def work(p):
            copy(p).wait()
            for k in range(PER):
                g = p * PER + k
                o_ref[slot(p, k), :R] = (wide[:R, columns(g)] + low_ref[slot(p, k)].astype(F32)).astype(BF)
                o_ref[slot(p, k), R:] = (wide[R:, columns(g)] + high_ref[slot(p, k)].astype(F32)).astype(BF)

        each(PARTS, lambda p: copy(p).start())
        each(PARTS, work)

    (out,) = order.run(
        body,
        "add_own",
        (policy, *[in_vmem(tiles) for tiles in chunks]),
        [HBM, VMEM, VMEM],
        [tiles_out(QUARTER)],
        [VMEM],
        [pltpu.VMEM((QUARTER, D), F32), pltpu.SemaphoreType.DMA((PARTS,))],
    )
    return out


def pick_rows(order, anchor, policy):
    def body(at, a_ref, x_ref, p_ref, rows_ref, a_sems, x_sems):
        rows = [member_row(at, (True, True, 0), xh) for xh in range(2)]
        theirs = pl.ds(first_row(at, True, False, 0), QUARTER)

        def fetch(p, xh):
            some = pl.ds(4 * p, 4)
            return pltpu.make_async_copy(
                a_ref.at[some, xh, pl.ds(rows[xh], QUARTER), :], p_ref.at[xh, some], a_sems.at[xh, p]
            )

        def copy(p):
            return pltpu.make_async_copy(
                x_ref.at[theirs, span_of(p)], rows_ref.at[:, span_of(p)], x_sems.at[p]
            )

        each(PARTS, lambda p: copy(p).start())
        for xh in range(2):
            each(4, lambda p, xh=xh: fetch(p, xh).start())
        each(PARTS, lambda p: copy(p).wait())
        for xh in range(2):
            each(4, lambda p, xh=xh: fetch(p, xh).wait())

    picked, rows = order.run(
        body,
        "pick_rows",
        (anchor, policy),
        [HBM, HBM],
        [pltpu.VMEM((2, 16, QUARTER, WIDTH), BF), pltpu.VMEM((QUARTER, D), F32)],
        [VMEM, VMEM],
        [pltpu.SemaphoreType.DMA((2, 4)), pltpu.SemaphoreType.DMA((PARTS,))],
    )
    return picked.reshape(SHARDS, QUARTER, WIDTH), rows


def blend_rows(order, own, other, anchor):
    def body(at, x_ref, t_ref, a_ref, o_ref, held, sems):
        def store(p):
            some = pl.ds(p * PER, PER)
            return pltpu.make_async_copy(held.at[some], o_ref.at[some], sems.at[p])

        def work(p):
            for k in range(PER):
                g = p * PER + k
                total = x_ref[g].astype(F32) + t_ref[g].astype(F32)
                new = (1.0 - blend_rate) * a_ref[g].astype(F32) + (blend_rate / GROUPS) * total
                held[g] = new.astype(BF)
            store(p).start()

        each(PARTS, work)
        each(PARTS, lambda p: store(p).wait())

    (out,) = order.run(
        body,
        "blend_rows",
        [in_vmem(x) for x in (own, other, anchor)],
        [VMEM] * 3,
        [pltpu.HBM((SHARDS, QUARTER, WIDTH), BF)],
        [HBM],
        [pltpu.VMEM((SHARDS, QUARTER, WIDTH), BF), pltpu.SemaphoreType.DMA((PARTS,))],
    )
    return out


def plane(at, same):
    return at[2] if same else 1 - at[2]


def split_planes(order, finished, back):
    def body(at, f_ref, b_ref, first_ref, high_ref, sems):
        def stores(p):
            some = pl.ds(4 * p, 4)
            ends = ((f_ref, True, first_ref), (b_ref, False, high_ref))
            return [
                pltpu.make_async_copy(x.at[plane(at, same), some], o.at[some], sems.at[i, p])
                for i, (x, same, o) in enumerate(ends)
            ]

        def start(p):
            for store in stores(p):
                store.start()

        def finish(p):
            for store in stores(p):
                store.wait()

        each(4, start)
        each(4, finish)

    half = (16, QUARTER, WIDTH)
    return order.run(
        body,
        "split_planes",
        [in_vmem(x.reshape(2, 16, QUARTER, WIDTH)) for x in (finished, back)],
        [VMEM, VMEM],
        [pltpu.HBM(half, BF)] * 2,
        [HBM] * 2,
        [pltpu.SemaphoreType.DMA((2, 4))],
    )


def place_back(order, own, other):
    def body(at, own_ref, other_ref, out_ref, held, sems, held_sems):
        def there(core, same, p):
            row = first_row(at, core, same, 0)
            return out_ref.at[pl.ds(4 * p, 4), plane(at, same), pl.ds(row, QUARTER), :]

        def place(ref, core, same, p):
            return pltpu.make_async_copy(
                ref.at[plane(at, same), pl.ds(4 * p, 4)],
                there(core, same, p),
                sems.at[int(core), int(same), p],
            )

        def fetch(xh, p):
            some = pl.ds(4 * p, 4)
            return pltpu.make_async_copy(other_ref.at[xh, some], held.at[xh, some], held_sems.at[xh, p])

        def forward(p):
            for xh in range(2):
                fetch(xh, p).wait()
            for same in (True, False):
                place(held, False, same, p).start()

        for xh in range(2):
            each(4, lambda p, xh=xh: fetch(xh, p).start())
        for same in (True, False):
            each(4, lambda p, same=same: place(own_ref, True, same, p).start())
        each(4, forward)
        for ref, core in ((own_ref, True), (held, False)):
            for same in (True, False):
                each(4, lambda p, ref=ref, core=core, same=same: place(ref, core, same, p).wait())

    shape = (2, 16, QUARTER, WIDTH)
    return order.run(
        body,
        "place_back",
        [in_vmem(own.reshape(shape)), other.reshape(shape)],
        [VMEM, ANY],
        [pltpu.HBM((16, 2, ROWS, WIDTH), BF)],
        [HBM],
        [
            pltpu.VMEM(shape, BF),
            pltpu.SemaphoreType.DMA((2, 2, 4)),
            pltpu.SemaphoreType.DMA((2, 4)),
        ],
    )[0]


def write_rows(order, wide_pieces, placed_pieces, blended, anchor, size=1024, late_in_hbm=False):
    n, m = len(wide_pieces), len(placed_pieces)
    flat = [tiles for tiles, _, _ in wide_pieces]
    late = n - 1
    outs = [pltpu.HBM((ROWS, D), F32)] * (n > 0) + [pltpu.HBM((16, 2, ROWS, WIDTH), BF)] * (m > 0)
    earlier = [x for x, k in ((blended, n), (anchor, m)) if k and x is not None]

    def body(at, *refs):
        flat_refs, refs = list(refs[: len(flat)]), refs[len(flat) :]
        placed, refs = refs[:m], refs[m + len(earlier) :]
        out_refs, (wide, held, sems, placed_sems, held_sem) = refs[: len(outs)], refs[len(outs) :]

        def place(i, p):
            some = pl.ds(4 * p, 4)
            core, chip, same = placed_pieces[i][1:]
            there = pl.ds(first_row(at, core, chip, 0), QUARTER)
            return pltpu.make_async_copy(
                placed[i].at[some], out_refs[-1].at[some, plane(at, same), there, :], placed_sems.at[i, p]
            )

        def copy(i, p):
            there = pl.ds(first_row(at, *wide_pieces[i][1:], 0), QUARTER)
            return pltpu.make_async_copy(
                wide.at[i, :, span_of(p)], out_refs[0].at[there, span_of(p)], sems.at[i, p]
            )

        def work(i, tiles, p):
            for k in range(PER):
                wide[i, :, columns(p * PER + k)] = tiles[slot(p, k)].astype(F32)
            copy(i, p).start()

        if n:
            last = pltpu.make_async_copy(flat_refs[late], held, held_sem)
            last.start()
            flat_refs[late] = held
        for i in range(m):
            each(4, lambda p, i=i: place(i, p).start())
        for i in range(n):
            if i == n - 1:
                last.wait()
            each(PARTS, lambda p, i=i, tiles=flat_refs[i]: work(i, tiles, p))
        for i in range(n):
            each(PARTS, lambda p, i=i: copy(i, p).wait())
        for i in range(m):
            each(4, lambda p, i=i: place(i, p).wait())

    args = [x if i == late else in_vmem(x) for i, x in enumerate(flat)]
    specs = [ANY if i == late else VMEM for i in range(len(flat))]
    if late_in_hbm:
        args[late] = pltpu.with_memory_space_constraint(args[late], pltpu.HBM)
        specs[late] = HBM
    return order.run(
        body,
        "write_rows",
        args + [in_vmem(x) for x, *_ in placed_pieces] + earlier,
        specs + [VMEM] * m + [HBM] * len(earlier),
        outs,
        [HBM] * len(outs),
        [
            pltpu.VMEM((max(n, 1), QUARTER, D if n else 128), F32),
            pltpu.VMEM(flat[late].shape if n else (1, 16, 128), BF),
            pltpu.SemaphoreType.DMA((max(n, 1), PARTS)),
            pltpu.SemaphoreType.DMA((max(m, 1), 4)),
            pltpu.SemaphoreType.DMA,
        ],
        {len(flat) + m + 1 + k: k for k in range(len(earlier))},
        size,
    )


def per_device(policies, anchor):
    policy = pltpu.with_memory_space_constraint(policies[0], pltpu.HBM)
    shards = pltpu.with_memory_space_constraint(anchor.reshape(16, 2, ROWS, WIDTH), pltpu.HBM)
    order = Order(jnp.stack([lax.axis_index(name) for name in ("xl", "c", "xh")]).astype(jnp.int32))
    swap = [(0, 1), (1, 0)]
    groups = exchange_groups()

    def exchange(tiles):
        return lax.all_to_all(
            tiles, AXES, split_axis=0, concat_axis=0, axis_index_groups=groups, tiled=True
        )

    def core(tiles):
        return lax.ppermute(tiles, "c", swap)

    def chip(tiles):
        return lax.ppermute(tiles, "xl", swap)

    theirs = core(cast_rows(order, policy))
    picked, rows = pick_rows(order, shards, policy)
    theirs, picked = add_theirs(order, rows, theirs, picked)
    other = chip(theirs)
    fetched = exchange(picked)
    own = add_own(order, policy, [core(tiles) for tiles in cast_own(order, policy)])

    own = blend_rows(order, own, other, fetched)
    finished = chip(own)
    back = exchange(own)
    pieces = [(core(own), False, True), (own, True, True)]
    (blended,) = write_rows(order, pieces, [], None, None, WRITE_COST, late_in_hbm=True)

    first, high = split_planes(order, finished, back)
    back_first = lax.all_to_all(first, ("y", "z"), split_axis=0, concat_axis=0, tiled=True)
    back_second = chip(high)
    finished, back = order.behind(finished), order.behind(back)
    new_anchor = place_back(order, back, core(back))
    pieces = [(finished, True, False), (core(finished), False, False)]
    (blended,) = write_rows(order, pieces, [], blended, None)
    back_second = order.behind(back_second)
    back_first = order.behind(back_first)
    pieces = [(back_first, True, False, True), (back_second, True, True, False)]
    (new_anchor,) = write_rows(order, [], pieces, None, new_anchor, LAST_COST)
    pieces = [(core(back_first), False, False, True), (core(back_second), False, True, False)]
    (new_anchor,) = write_rows(order, [], pieces, None, new_anchor)
    return blended, new_anchor.reshape(SHARDS * ROWS, WIDTH)


def solution(mesh):
    fine = Mesh(mesh.devices.reshape(SIZES), AXES)
    shards = ("y", "z", "xh")
    return jax.shard_map(
        per_device,
        mesh=fine,
        in_specs=(P(("xl", "c"), shards, None), P(None, shards)),
        out_specs=(P(shards, None), P(None, shards)),
        check_vma=False,
    )
```

```python
import jax
import jax.numpy as jnp
import numpy as np
from jax import lax
from jax.experimental import pallas as pl
from jax.experimental.pallas import tpu as pltpu
from jax.sharding import Mesh, PartitionSpec as P

blend_rate = 0.3
GROUPS = 4

AXES = ("xl", "c", "y", "z", "xh")
SIZES = (2, 2, 4, 4, 2)
SHARDS = 32
ROWS = 256
WIDTH = 256
D = 8192
HALF = 128
QUARTER = 64
R = 32
BF = jnp.bfloat16
F32 = jnp.float32
VMEM_LIMIT = 10 << 20
PARTS = 8
PER = SHARDS // PARTS
WRITE_COST = 11 << 20
LAST_COST = 37 << 20
ANY = pl.BlockSpec(memory_space=pl.ANY)
HBM = pl.BlockSpec(memory_space=pltpu.HBM)
VMEM = pl.BlockSpec(memory_space=pltpu.VMEM)
TOKEN = jax.ShapeDtypeStruct((8, 128), jnp.int32)


def exchange_groups():
    ids = np.arange(128).reshape(SIZES)
    return [
        [int(ids[flip ^ xh, c, y, z, xh]) for xh in range(2) for y in range(4) for z in range(4)]
        for flip in range(2)
        for c in range(2)
    ]


def in_vmem(x):
    return pltpu.with_memory_space_constraint(x, pltpu.VMEM)


class Order:
    def __init__(self, place):
        self.place = place
        self.token = None

    def behind(self, x):
        x, self.token = lax.optimization_barrier((x, self.token))
        return x

    def run(self, body, name, args, specs, outs, out_specs, scratch, aliases=None, size=1024):
        held = [] if self.token is None else [self.token]

        def ordered(at, *refs):
            ins, rest = refs[: len(args)], refs[len(args) + len(held) :]
            results, others = rest[: len(outs)], rest[len(outs) + 1 :]
            body(at, *ins, *results, *others)

        *results, self.token = pl.pallas_call(
            ordered,
            out_shape=[*outs, TOKEN],
            grid_spec=pltpu.PrefetchScalarGridSpec(
                num_scalar_prefetch=1,
                grid=(),
                in_specs=[*specs, *[ANY] * len(held)],
                out_specs=[*out_specs, ANY],
                scratch_shapes=scratch,
            ),
            input_output_aliases=aliases or {},
            compiler_params=pltpu.CompilerParams(vmem_limit_bytes=VMEM_LIMIT),
            cost_estimate=pl.CostEstimate(flops=0, bytes_accessed=size, transcendentals=0),
            name=name,
        )(self.place, *args, *held)
        return results


def columns(g):
    return pl.ds(pl.multiple_of(g * WIDTH, WIDTH), WIDTH)


def slot(p, k):
    return (k % 2) * 16 + p * (PER // 2) + k // 2


def each(count, work):
    pl.loop(0, count)(work)


def first_row(at, core, chip, start, xl=None):
    xl = at[0] if xl is None else xl
    half = at[1] if core else 1 - at[1]
    quarter = xl if chip else 1 - xl
    return pl.multiple_of(half * HALF + quarter * QUARTER + start, 16)


def member_row(at, where, xh):
    differs = at[2] if xh == 0 else 1 - at[2]
    return first_row(at, *where, at[0] + differs - 2 * at[0] * differs)


def tiles_out(rows):
    return pltpu.VMEM((SHARDS, rows, WIDTH), BF)


def span_of(p):
    return pl.ds(pl.multiple_of(p * PER * WIDTH, WIDTH), PER * WIDTH)


def cast_rows(order, policy):
    def body(at, x_ref, o_ref, wide, sems):
        held = pl.ds(first_row(at, False, False, 0), QUARTER)

        def copy(p):
            return pltpu.make_async_copy(x_ref.at[held, span_of(p)], wide.at[:, span_of(p)], sems.at[p])

        def work(p):
            copy(p).wait()
            for k in range(PER):
                g = p * PER + k
                o_ref[slot(p, k)] = wide[:, columns(g)].astype(BF)

        each(PARTS, lambda p: copy(p).start())
        each(PARTS, work)

    (out,) = order.run(
        body,
        "cast_rows",
        (policy,),
        [HBM],
        [tiles_out(QUARTER)],
        [VMEM],
        [pltpu.VMEM((QUARTER, D), F32), pltpu.SemaphoreType.DMA((PARTS,))],
    )
    return out


def add_theirs(order, rows, tiles):
    def body(at, x_ref, t_ref, o_ref, held, sems):
        def store(p):
            some = pl.ds(p * PER, PER)
            return pltpu.make_async_copy(held.at[some], o_ref.at[some], sems.at[p])

        def work(p):
            for k in range(PER):
                at_slot = p * PER + k
                g = 2 * ((p & 3) * PER + k) + (p >> 2)
                held[at_slot] = (x_ref[:, columns(g)] + t_ref[at_slot].astype(F32)).astype(BF)
            store(p).start()

        each(PARTS, work)
        each(PARTS, lambda p: store(p).wait())

    return order.run(
        body,
        "add_theirs",
        [in_vmem(x) for x in (rows, tiles)],
        [VMEM] * 2,
        [pltpu.HBM((SHARDS, QUARTER, WIDTH), BF)],
        [HBM],
        [pltpu.VMEM((SHARDS, QUARTER, WIDTH), BF), pltpu.SemaphoreType.DMA((PARTS,))],
    )[0]


def store_tiles(order, tiles):
    def body(at, x_ref, o_ref, sems):
        def copy(p):
            some = pl.ds(p * PER, PER)
            return pltpu.make_async_copy(x_ref.at[some], o_ref.at[some], sems.at[p])

        each(PARTS, lambda p: copy(p).start())
        each(PARTS, lambda p: copy(p).wait())

    return order.run(
        body,
        "store_tiles",
        [in_vmem(tiles)],
        [VMEM],
        [pltpu.HBM(tiles.shape, BF)],
        [HBM],
        [pltpu.SemaphoreType.DMA((PARTS,))],
    )[0]


def cast_own(order, policy):
    def body(at, x_ref, low_ref, high_ref, wide, sems):
        held = pl.ds(first_row(at, False, True, 0), QUARTER)

        def copy(p):
            return pltpu.make_async_copy(x_ref.at[held, span_of(p)], wide.at[:, span_of(p)], sems.at[p])

        def work(p):
            copy(p).wait()
            for k in range(PER):
                g = p * PER + k
                low_ref[slot(p, k)] = wide[:R, columns(g)].astype(BF)
                high_ref[slot(p, k)] = wide[R:, columns(g)].astype(BF)

        each(PARTS, lambda p: copy(p).start())
        each(PARTS, work)

    return order.run(
        body,
        "cast_own",
        (policy,),
        [HBM],
        [tiles_out(R)] * 2,
        [VMEM] * 2,
        [pltpu.VMEM((QUARTER, D), F32), pltpu.SemaphoreType.DMA((PARTS,))],
    )


def add_own(order, policy, chunks):
    def body(at, x_ref, low_ref, high_ref, o_ref, wide, sems):
        held = pl.ds(first_row(at, True, True, 0), QUARTER)

        def copy(p):
            return pltpu.make_async_copy(x_ref.at[held, span_of(p)], wide.at[:, span_of(p)], sems.at[p])

        def work(p):
            copy(p).wait()
            for k in range(PER):
                g = p * PER + k
                o_ref[slot(p, k), :R] = (wide[:R, columns(g)] + low_ref[slot(p, k)].astype(F32)).astype(BF)
                o_ref[slot(p, k), R:] = (wide[R:, columns(g)] + high_ref[slot(p, k)].astype(F32)).astype(BF)

        each(PARTS, lambda p: copy(p).start())
        each(PARTS, work)

    (out,) = order.run(
        body,
        "add_own",
        (policy, *[in_vmem(tiles) for tiles in chunks]),
        [HBM, VMEM, VMEM],
        [tiles_out(QUARTER)],
        [VMEM],
        [pltpu.VMEM((QUARTER, D), F32), pltpu.SemaphoreType.DMA((PARTS,))],
    )
    return out


def pick_rows(order, anchor, policy):
    def body(at, a_ref, x_ref, p_ref, rows_ref, a_sems, x_sems):
        rows = [member_row(at, (True, True, 0), xh) for xh in range(2)]
        theirs = pl.ds(first_row(at, True, False, 0), QUARTER)

        def fetch(p, xh):
            some = pl.ds(4 * p, 4)
            return pltpu.make_async_copy(
                a_ref.at[some, xh, pl.ds(rows[xh], QUARTER), :], p_ref.at[xh, some], a_sems.at[xh, p]
            )

        def copy(p):
            return pltpu.make_async_copy(
                x_ref.at[theirs, span_of(p)], rows_ref.at[:, span_of(p)], x_sems.at[p]
            )

        each(PARTS, lambda p: copy(p).start())
        for xh in range(2):
            each(4, lambda p, xh=xh: fetch(p, xh).start())
        each(PARTS, lambda p: copy(p).wait())
        for xh in range(2):
            each(4, lambda p, xh=xh: fetch(p, xh).wait())

    picked, rows = order.run(
        body,
        "pick_rows",
        (anchor, policy),
        [HBM, HBM],
        [pltpu.VMEM((2, 16, QUARTER, WIDTH), BF), pltpu.VMEM((QUARTER, D), F32)],
        [VMEM, VMEM],
        [pltpu.SemaphoreType.DMA((2, 4)), pltpu.SemaphoreType.DMA((PARTS,))],
    )
    return picked.reshape(SHARDS, QUARTER, WIDTH), rows


def blend_rows(order, own, other, anchor):
    def body(at, x_ref, t_ref, a_ref, o_ref, *rest):
        planes, held, sems = rest[:2], rest[2], rest[3]

        def stores(xh, p):
            some = pl.ds(p * PER, PER)
            all_some = pl.ds(xh * 16 + p * PER, PER)
            ends = (o_ref.at[all_some], planes[xh].at[some])
            return [
                pltpu.make_async_copy(held.at[all_some], end, sems.at[i, xh, p])
                for i, end in enumerate(ends)
            ]

        def work(xh, p):
            for k in range(PER):
                g = xh * 16 + p * PER + k
                total = x_ref[g].astype(F32) + t_ref[g].astype(F32)
                new = (1.0 - blend_rate) * a_ref[g].astype(F32) + (blend_rate / GROUPS) * total
                held[g] = new.astype(BF)
            for store in stores(xh, p):
                store.start()

        def finish(xh, p):
            for store in stores(xh, p):
                store.wait()

        for xh in range(2):
            each(4, lambda p, xh=xh: work(xh, p))
        for xh in range(2):
            each(4, lambda p, xh=xh: finish(xh, p))

    return order.run(
        body,
        "blend_rows",
        [in_vmem(x) for x in (own, other, anchor)],
        [VMEM] * 3,
        [pltpu.HBM((n, QUARTER, WIDTH), BF) for n in (SHARDS, 16, 16)],
        [HBM] * 3,
        [pltpu.VMEM((SHARDS, QUARTER, WIDTH), BF), pltpu.SemaphoreType.DMA((2, 2, 4))],
    )


def plane(at, same):
    return at[2] if same else 1 - at[2]


def split_planes(order, finished, back):
    def body(at, f_ref, b_ref, first_ref, high_ref, sems):
        def stores(p):
            some = pl.ds(4 * p, 4)
            ends = ((f_ref, True, first_ref), (b_ref, False, high_ref))
            return [
                pltpu.make_async_copy(x.at[plane(at, same), some], o.at[some], sems.at[i, p])
                for i, (x, same, o) in enumerate(ends)
            ]

        def start(p):
            for store in stores(p):
                store.start()

        def finish(p):
            for store in stores(p):
                store.wait()

        each(4, start)
        each(4, finish)

    half = (16, QUARTER, WIDTH)
    return order.run(
        body,
        "split_planes",
        [in_vmem(x.reshape(2, 16, QUARTER, WIDTH)) for x in (finished, back)],
        [VMEM, VMEM],
        [pltpu.HBM(half, BF)] * 2,
        [HBM] * 2,
        [pltpu.SemaphoreType.DMA((2, 4))],
    )


def place_back(order, own, other):
    def body(at, own_ref, other_ref, out_ref, held, sems, held_sems):
        def there(core, same, p):
            row = first_row(at, core, same, 0)
            return out_ref.at[pl.ds(4 * p, 4), plane(at, same), pl.ds(row, QUARTER), :]

        def place(ref, core, same, p):
            return pltpu.make_async_copy(
                ref.at[plane(at, same), pl.ds(4 * p, 4)],
                there(core, same, p),
                sems.at[int(core), int(same), p],
            )

        def fetch(xh, p):
            some = pl.ds(4 * p, 4)
            return pltpu.make_async_copy(other_ref.at[xh, some], held.at[xh, some], held_sems.at[xh, p])

        def forward(p):
            for xh in range(2):
                fetch(xh, p).wait()
            for same in (True, False):
                place(held, False, same, p).start()

        for xh in range(2):
            each(4, lambda p, xh=xh: fetch(xh, p).start())
        for same in (True, False):
            each(4, lambda p, same=same: place(own_ref, True, same, p).start())
        each(4, forward)
        for ref, core in ((own_ref, True), (held, False)):
            for same in (True, False):
                each(4, lambda p, ref=ref, core=core, same=same: place(ref, core, same, p).wait())

    shape = (2, 16, QUARTER, WIDTH)
    return order.run(
        body,
        "place_back",
        [in_vmem(own.reshape(shape)), other.reshape(shape)],
        [VMEM, ANY],
        [pltpu.HBM((16, 2, ROWS, WIDTH), BF)],
        [HBM],
        [
            pltpu.VMEM(shape, BF),
            pltpu.SemaphoreType.DMA((2, 2, 4)),
            pltpu.SemaphoreType.DMA((2, 4)),
        ],
    )[0]


def write_rows(order, wide_pieces, placed_pieces, blended, anchor, size=1024, late_in_hbm=False):
    n, m = len(wide_pieces), len(placed_pieces)
    counts = [len(arrays) for arrays, _, _ in wide_pieces]
    flat = [x for arrays, _, _ in wide_pieces for x in arrays]
    late = len(flat) - 1
    outs = [pltpu.HBM((ROWS, D), F32)] * (n > 0) + [pltpu.HBM((16, 2, ROWS, WIDTH), BF)] * (m > 0)
    earlier = [x for x, k in ((blended, n), (anchor, m)) if k and x is not None]

    def body(at, *refs):
        flat_refs, refs = list(refs[: len(flat)]), refs[len(flat) :]
        placed, refs = refs[:m], refs[m + len(earlier) :]
        out_refs, (wide, held, sems, placed_sems, held_sem) = refs[: len(outs)], refs[len(outs) :]

        def place(i, p):
            some = pl.ds(4 * p, 4)
            core, chip, same = placed_pieces[i][1:]
            there = pl.ds(first_row(at, core, chip, 0), QUARTER)
            return pltpu.make_async_copy(
                placed[i].at[some], out_refs[-1].at[some, plane(at, same), there, :], placed_sems.at[i, p]
            )

        def copy(i, p):
            there = pl.ds(first_row(at, *wide_pieces[i][1:], 0), QUARTER)
            return pltpu.make_async_copy(
                wide.at[i, :, span_of(p)], out_refs[0].at[there, span_of(p)], sems.at[i, p]
            )

        def work(i, tiles, p):
            for k in range(PER):
                if len(tiles) == 1:
                    tile = tiles[0][slot(p, k)]
                else:
                    tile = tiles[k % 2][p * (PER // 2) + k // 2]
                wide[i, :, columns(p * PER + k)] = tile.astype(F32)
            copy(i, p).start()

        if n:
            last = pltpu.make_async_copy(flat_refs[late], held, held_sem)
            last.start()
            flat_refs[late] = held
        for i in range(m):
            each(4, lambda p, i=i: place(i, p).start())
        for i in range(n):
            if i == n - 1:
                last.wait()
            tiles = flat_refs[sum(counts[:i]) : sum(counts[: i + 1])]
            each(PARTS, lambda p, i=i, tiles=tiles: work(i, tiles, p))
        for i in range(n):
            each(PARTS, lambda p, i=i: copy(i, p).wait())
        for i in range(m):
            each(4, lambda p, i=i: place(i, p).wait())

    args = [x if i == late else in_vmem(x) for i, x in enumerate(flat)]
    specs = [ANY if i == late else VMEM for i in range(len(flat))]
    if late_in_hbm:
        args[late] = pltpu.with_memory_space_constraint(args[late], pltpu.HBM)
        specs[late] = HBM
    return order.run(
        body,
        "write_rows",
        args + [in_vmem(x) for x, *_ in placed_pieces] + earlier,
        specs + [VMEM] * m + [HBM] * len(earlier),
        outs,
        [HBM] * len(outs),
        [
            pltpu.VMEM((max(n, 1), QUARTER, D if n else 128), F32),
            pltpu.VMEM(flat[late].shape if n else (1, 16, 128), BF),
            pltpu.SemaphoreType.DMA((max(n, 1), PARTS)),
            pltpu.SemaphoreType.DMA((max(m, 1), 4)),
            pltpu.SemaphoreType.DMA,
        ],
        {len(flat) + m + 1 + k: k for k in range(len(earlier))},
        size,
    )


def per_device(policies, anchor):
    policy = pltpu.with_memory_space_constraint(policies[0], pltpu.HBM)
    shards = pltpu.with_memory_space_constraint(anchor.reshape(16, 2, ROWS, WIDTH), pltpu.HBM)
    order = Order(jnp.stack([lax.axis_index(name) for name in ("xl", "c", "xh")]).astype(jnp.int32))
    swap = [(0, 1), (1, 0)]
    groups = exchange_groups()

    def exchange(tiles):
        return lax.all_to_all(
            tiles, AXES, split_axis=0, concat_axis=0, axis_index_groups=groups, tiled=True
        )

    def core(tiles):
        return lax.ppermute(tiles, "c", swap)

    def chip(tiles):
        return lax.ppermute(tiles, "xl", swap)

    theirs = core(cast_rows(order, policy))
    picked, rows = pick_rows(order, shards, policy)
    other = chip(add_theirs(order, rows, theirs))
    fetched = exchange(store_tiles(order, picked))
    own = add_own(order, policy, [core(tiles) for tiles in cast_own(order, policy)])

    own, *planes = blend_rows(order, own, other, fetched)
    finished = chip(own)
    back = exchange(own)
    pieces = [([core(tiles) for tiles in planes], False, True), ([own], True, True)]
    (blended,) = write_rows(order, pieces, [], None, None, WRITE_COST, late_in_hbm=True)

    first, high = split_planes(order, finished, back)
    back_first = lax.all_to_all(first, ("y", "z"), split_axis=0, concat_axis=0, tiled=True)
    back_second = chip(high)
    finished, back = order.behind(finished), order.behind(back)
    new_anchor = place_back(order, back, core(back))
    pieces = [([finished], True, False), ([core(finished)], False, False)]
    (blended,) = write_rows(order, pieces, [], blended, None)
    back_second = order.behind(back_second)
    back_first = order.behind(back_first)
    pieces = [(back_first, True, False, True), (back_second, True, True, False)]
    (new_anchor,) = write_rows(order, [], pieces, None, new_anchor, LAST_COST)
    pieces = [(core(back_first), False, False, True), (core(back_second), False, True, False)]
    (new_anchor,) = write_rows(order, [], pieces, None, new_anchor)
    return blended, new_anchor.reshape(SHARDS * ROWS, WIDTH)


def solution(mesh):
    fine = Mesh(mesh.devices.reshape(SIZES), AXES)
    shards = ("y", "z", "xh")
    return jax.shard_map(
        per_device,
        mesh=fine,
        in_specs=(P(("xl", "c"), shards, None), P(None, shards)),
        out_specs=(P(shards, None), P(None, shards)),
        check_vma=False,
    )
```

```python
import jax
import jax.numpy as jnp
import numpy as np
from jax import lax
from jax.experimental import pallas as pl
from jax.experimental.pallas import tpu as pltpu
from jax.sharding import Mesh, PartitionSpec as P

blend_rate = 0.3
GROUPS = 4

AXES = ("xl", "c", "y", "z", "xh")
SIZES = (2, 2, 4, 4, 2)
SHARDS = 32
ROWS = 256
WIDTH = 256
D = 8192
HALF = 128
QUARTER = 64
R = 32
BF = jnp.bfloat16
F32 = jnp.float32
VMEM_LIMIT = 10 << 20
PARTS = 8
PER = SHARDS // PARTS
WRITE_COST = 11 << 20
LAST_COST = 37 << 20
ANY = pl.BlockSpec(memory_space=pl.ANY)
HBM = pl.BlockSpec(memory_space=pltpu.HBM)
VMEM = pl.BlockSpec(memory_space=pltpu.VMEM)
TOKEN = jax.ShapeDtypeStruct((8, 128), jnp.int32)


def exchange_groups():
    ids = np.arange(128).reshape(SIZES)
    return [
        [int(ids[flip ^ xh, c, y, z, xh]) for xh in range(2) for y in range(4) for z in range(4)]
        for flip in range(2)
        for c in range(2)
    ]


def in_vmem(x):
    return pltpu.with_memory_space_constraint(x, pltpu.VMEM)


class Order:
    def __init__(self, place):
        self.place = place
        self.token = None

    def behind(self, x):
        x, self.token = lax.optimization_barrier((x, self.token))
        return x

    def run(self, body, name, args, specs, outs, out_specs, scratch, aliases=None, size=1024):
        held = [] if self.token is None else [self.token]

        def ordered(at, *refs):
            ins, rest = refs[: len(args)], refs[len(args) + len(held) :]
            results, others = rest[: len(outs)], rest[len(outs) + 1 :]
            body(at, *ins, *results, *others)

        *results, self.token = pl.pallas_call(
            ordered,
            out_shape=[*outs, TOKEN],
            grid_spec=pltpu.PrefetchScalarGridSpec(
                num_scalar_prefetch=1,
                grid=(),
                in_specs=[*specs, *[ANY] * len(held)],
                out_specs=[*out_specs, ANY],
                scratch_shapes=scratch,
            ),
            input_output_aliases=aliases or {},
            compiler_params=pltpu.CompilerParams(vmem_limit_bytes=VMEM_LIMIT),
            cost_estimate=pl.CostEstimate(flops=0, bytes_accessed=size, transcendentals=0),
            name=name,
        )(self.place, *args, *held)
        return results


def columns(g):
    return pl.ds(pl.multiple_of(g * WIDTH, WIDTH), WIDTH)


def slot(p, k):
    return (k % 2) * 16 + p * (PER // 2) + k // 2


def each(count, work):
    pl.loop(0, count)(work)


def first_row(at, core, chip, start, xl=None):
    xl = at[0] if xl is None else xl
    half = at[1] if core else 1 - at[1]
    quarter = xl if chip else 1 - xl
    return pl.multiple_of(half * HALF + quarter * QUARTER + start, 16)


def member_row(at, where, xh):
    differs = at[2] if xh == 0 else 1 - at[2]
    return first_row(at, *where, at[0] + differs - 2 * at[0] * differs)


def tiles_out(rows):
    return pltpu.VMEM((SHARDS, rows, WIDTH), BF)


def span_of(p):
    return pl.ds(pl.multiple_of(p * PER * WIDTH, WIDTH), PER * WIDTH)


def cast_rows(order, policy):
    def body(at, x_ref, o_ref, wide, sems):
        held = pl.ds(first_row(at, False, False, 0), QUARTER)

        def copy(p):
            return pltpu.make_async_copy(x_ref.at[held, span_of(p)], wide.at[:, span_of(p)], sems.at[p])

        def work(p):
            copy(p).wait()
            for k in range(PER):
                g = p * PER + k
                o_ref[slot(p, k)] = wide[:, columns(g)].astype(BF)

        each(PARTS, lambda p: copy(p).start())
        each(PARTS, work)

    (out,) = order.run(
        body,
        "cast_rows",
        (policy,),
        [HBM],
        [tiles_out(QUARTER)],
        [VMEM],
        [pltpu.VMEM((QUARTER, D), F32), pltpu.SemaphoreType.DMA((PARTS,))],
    )
    return out


def add_theirs(order, rows, tiles, picked):
    def body(at, x_ref, t_ref, p_ref, o_ref, q_ref, held, sems, picked_sems):
        def store(p):
            some = pl.ds(p * PER, PER)
            return pltpu.make_async_copy(held.at[some], o_ref.at[some], sems.at[p])

        def copy(p):
            some = pl.ds(p * PER, PER)
            return pltpu.make_async_copy(p_ref.at[some], q_ref.at[some], picked_sems.at[p])

        def work(p):
            for k in range(PER):
                at_slot = p * PER + k
                g = 2 * ((p & 3) * PER + k) + (p >> 2)
                held[at_slot] = (x_ref[:, columns(g)] + t_ref[at_slot].astype(F32)).astype(BF)
            store(p).start()

        each(PARTS, lambda p: copy(p).start())
        each(PARTS, work)
        each(PARTS, lambda p: copy(p).wait())
        each(PARTS, lambda p: store(p).wait())

    return order.run(
        body,
        "add_theirs",
        [in_vmem(x) for x in (rows, tiles, picked)],
        [VMEM] * 3,
        [pltpu.HBM((SHARDS, QUARTER, WIDTH), BF)] * 2,
        [HBM] * 2,
        [
            pltpu.VMEM((SHARDS, QUARTER, WIDTH), BF),
            pltpu.SemaphoreType.DMA((PARTS,)),
            pltpu.SemaphoreType.DMA((PARTS,)),
        ],
    )


def cast_own(order, policy):
    def body(at, x_ref, low_ref, high_ref, wide, sems):
        held = pl.ds(first_row(at, False, True, 0), QUARTER)

        def copy(p):
            return pltpu.make_async_copy(x_ref.at[held, span_of(p)], wide.at[:, span_of(p)], sems.at[p])

        def work(p):
            copy(p).wait()
            for k in range(PER):
                g = p * PER + k
                low_ref[slot(p, k)] = wide[:R, columns(g)].astype(BF)
                high_ref[slot(p, k)] = wide[R:, columns(g)].astype(BF)

        each(PARTS, lambda p: copy(p).start())
        each(PARTS, work)

    return order.run(
        body,
        "cast_own",
        (policy,),
        [HBM],
        [tiles_out(R)] * 2,
        [VMEM] * 2,
        [pltpu.VMEM((QUARTER, D), F32), pltpu.SemaphoreType.DMA((PARTS,))],
    )


def add_own(order, policy, chunks):
    def body(at, x_ref, low_ref, high_ref, o_ref, wide, sems):
        held = pl.ds(first_row(at, True, True, 0), QUARTER)

        def copy(p):
            return pltpu.make_async_copy(x_ref.at[held, span_of(p)], wide.at[:, span_of(p)], sems.at[p])

        def work(p):
            copy(p).wait()
            for k in range(PER):
                g = p * PER + k
                o_ref[slot(p, k), :R] = (wide[:R, columns(g)] + low_ref[slot(p, k)].astype(F32)).astype(BF)
                o_ref[slot(p, k), R:] = (wide[R:, columns(g)] + high_ref[slot(p, k)].astype(F32)).astype(BF)

        each(PARTS, lambda p: copy(p).start())
        each(PARTS, work)

    (out,) = order.run(
        body,
        "add_own",
        (policy, *[in_vmem(tiles) for tiles in chunks]),
        [HBM, VMEM, VMEM],
        [tiles_out(QUARTER)],
        [VMEM],
        [pltpu.VMEM((QUARTER, D), F32), pltpu.SemaphoreType.DMA((PARTS,))],
    )
    return out


def pick_rows(order, anchor, policy):
    def body(at, a_ref, x_ref, p_ref, rows_ref, a_sems, x_sems):
        rows = [member_row(at, (True, True, 0), xh) for xh in range(2)]
        theirs = pl.ds(first_row(at, True, False, 0), QUARTER)

        def fetch(p, xh):
            some = pl.ds(4 * p, 4)
            return pltpu.make_async_copy(
                a_ref.at[some, xh, pl.ds(rows[xh], QUARTER), :], p_ref.at[xh, some], a_sems.at[xh, p]
            )

        def copy(p):
            return pltpu.make_async_copy(
                x_ref.at[theirs, span_of(p)], rows_ref.at[:, span_of(p)], x_sems.at[p]
            )

        each(PARTS, lambda p: copy(p).start())
        for xh in range(2):
            each(4, lambda p, xh=xh: fetch(p, xh).start())
        each(PARTS, lambda p: copy(p).wait())
        for xh in range(2):
            each(4, lambda p, xh=xh: fetch(p, xh).wait())

    picked, rows = order.run(
        body,
        "pick_rows",
        (anchor, policy),
        [HBM, HBM],
        [pltpu.VMEM((2, 16, QUARTER, WIDTH), BF), pltpu.VMEM((QUARTER, D), F32)],
        [VMEM, VMEM],
        [pltpu.SemaphoreType.DMA((2, 4)), pltpu.SemaphoreType.DMA((PARTS,))],
    )
    return picked.reshape(SHARDS, QUARTER, WIDTH), rows


def blend_rows(order, own, other, anchor):
    def body(at, x_ref, t_ref, a_ref, o_ref, *rest):
        planes, held, sems = rest[:2], rest[2], rest[3]

        def stores(xh, p):
            some = pl.ds(p * PER, PER)
            all_some = pl.ds(xh * 16 + p * PER, PER)
            ends = (o_ref.at[all_some], planes[xh].at[some])
            return [
                pltpu.make_async_copy(held.at[all_some], end, sems.at[i, xh, p])
                for i, end in enumerate(ends)
            ]

        def work(xh, p):
            for k in range(PER):
                g = xh * 16 + p * PER + k
                total = x_ref[g].astype(F32) + t_ref[g].astype(F32)
                new = (1.0 - blend_rate) * a_ref[g].astype(F32) + (blend_rate / GROUPS) * total
                held[g] = new.astype(BF)
            for store in stores(xh, p):
                store.start()

        def finish(xh, p):
            for store in stores(xh, p):
                store.wait()

        for xh in range(2):
            each(4, lambda p, xh=xh: work(xh, p))
        for xh in range(2):
            each(4, lambda p, xh=xh: finish(xh, p))

    return order.run(
        body,
        "blend_rows",
        [in_vmem(x) for x in (own, other, anchor)],
        [VMEM] * 3,
        [pltpu.HBM((n, QUARTER, WIDTH), BF) for n in (SHARDS, 16, 16)],
        [HBM] * 3,
        [pltpu.VMEM((SHARDS, QUARTER, WIDTH), BF), pltpu.SemaphoreType.DMA((2, 2, 4))],
    )


def plane(at, same):
    return at[2] if same else 1 - at[2]


def split_planes(order, finished, back):
    def body(at, f_ref, b_ref, first_ref, high_ref, sems):
        def stores(p):
            some = pl.ds(4 * p, 4)
            ends = ((f_ref, True, first_ref), (b_ref, False, high_ref))
            return [
                pltpu.make_async_copy(x.at[plane(at, same), some], o.at[some], sems.at[i, p])
                for i, (x, same, o) in enumerate(ends)
            ]

        def start(p):
            for store in stores(p):
                store.start()

        def finish(p):
            for store in stores(p):
                store.wait()

        each(4, start)
        each(4, finish)

    half = (16, QUARTER, WIDTH)
    return order.run(
        body,
        "split_planes",
        [in_vmem(x.reshape(2, 16, QUARTER, WIDTH)) for x in (finished, back)],
        [VMEM, VMEM],
        [pltpu.HBM(half, BF)] * 2,
        [HBM] * 2,
        [pltpu.SemaphoreType.DMA((2, 4))],
    )


def place_back(order, own, other):
    def body(at, own_ref, other_ref, out_ref, held, sems, held_sems):
        def there(core, same, p):
            row = first_row(at, core, same, 0)
            return out_ref.at[pl.ds(4 * p, 4), plane(at, same), pl.ds(row, QUARTER), :]

        def place(ref, core, same, p):
            return pltpu.make_async_copy(
                ref.at[plane(at, same), pl.ds(4 * p, 4)],
                there(core, same, p),
                sems.at[int(core), int(same), p],
            )

        def fetch(xh, p):
            some = pl.ds(4 * p, 4)
            return pltpu.make_async_copy(other_ref.at[xh, some], held.at[xh, some], held_sems.at[xh, p])

        def forward(p):
            for xh in range(2):
                fetch(xh, p).wait()
            for same in (True, False):
                place(held, False, same, p).start()

        for xh in range(2):
            each(4, lambda p, xh=xh: fetch(xh, p).start())
        for same in (True, False):
            each(4, lambda p, same=same: place(own_ref, True, same, p).start())
        each(4, forward)
        for ref, core in ((own_ref, True), (held, False)):
            for same in (True, False):
                each(4, lambda p, ref=ref, core=core, same=same: place(ref, core, same, p).wait())

    shape = (2, 16, QUARTER, WIDTH)
    return order.run(
        body,
        "place_back",
        [in_vmem(own.reshape(shape)), other.reshape(shape)],
        [VMEM, ANY],
        [pltpu.HBM((16, 2, ROWS, WIDTH), BF)],
        [HBM],
        [
            pltpu.VMEM(shape, BF),
            pltpu.SemaphoreType.DMA((2, 2, 4)),
            pltpu.SemaphoreType.DMA((2, 4)),
        ],
    )[0]


def write_rows(order, wide_pieces, placed_pieces, blended, anchor, size=1024, late_in_hbm=False):
    n, m = len(wide_pieces), len(placed_pieces)
    counts = [len(arrays) for arrays, _, _ in wide_pieces]
    flat = [x for arrays, _, _ in wide_pieces for x in arrays]
    late = len(flat) - 1
    outs = [pltpu.HBM((ROWS, D), F32)] * (n > 0) + [pltpu.HBM((16, 2, ROWS, WIDTH), BF)] * (m > 0)
    earlier = [x for x, k in ((blended, n), (anchor, m)) if k and x is not None]

    def body(at, *refs):
        flat_refs, refs = list(refs[: len(flat)]), refs[len(flat) :]
        placed, refs = refs[:m], refs[m + len(earlier) :]
        out_refs, (wide, held, sems, placed_sems, held_sem) = refs[: len(outs)], refs[len(outs) :]

        def place(i, p):
            some = pl.ds(4 * p, 4)
            core, chip, same = placed_pieces[i][1:]
            there = pl.ds(first_row(at, core, chip, 0), QUARTER)
            return pltpu.make_async_copy(
                placed[i].at[some], out_refs[-1].at[some, plane(at, same), there, :], placed_sems.at[i, p]
            )

        def copy(i, p):
            there = pl.ds(first_row(at, *wide_pieces[i][1:], 0), QUARTER)
            return pltpu.make_async_copy(
                wide.at[i, :, span_of(p)], out_refs[0].at[there, span_of(p)], sems.at[i, p]
            )

        def work(i, tiles, p):
            for k in range(PER):
                if len(tiles) == 1:
                    tile = tiles[0][slot(p, k)]
                else:
                    tile = tiles[k % 2][p * (PER // 2) + k // 2]
                wide[i, :, columns(p * PER + k)] = tile.astype(F32)
            copy(i, p).start()

        if n:
            last = pltpu.make_async_copy(flat_refs[late], held, held_sem)
            last.start()
            flat_refs[late] = held
        for i in range(m):
            each(4, lambda p, i=i: place(i, p).start())
        for i in range(n):
            if i == n - 1:
                last.wait()
            tiles = flat_refs[sum(counts[:i]) : sum(counts[: i + 1])]
            each(PARTS, lambda p, i=i, tiles=tiles: work(i, tiles, p))
        for i in range(n):
            each(PARTS, lambda p, i=i: copy(i, p).wait())
        for i in range(m):
            each(4, lambda p, i=i: place(i, p).wait())

    args = [x if i == late else in_vmem(x) for i, x in enumerate(flat)]
    specs = [ANY if i == late else VMEM for i in range(len(flat))]
    if late_in_hbm:
        args[late] = pltpu.with_memory_space_constraint(args[late], pltpu.HBM)
        specs[late] = HBM
    return order.run(
        body,
        "write_rows",
        args + [in_vmem(x) for x, *_ in placed_pieces] + earlier,
        specs + [VMEM] * m + [HBM] * len(earlier),
        outs,
        [HBM] * len(outs),
        [
            pltpu.VMEM((max(n, 1), QUARTER, D if n else 128), F32),
            pltpu.VMEM(flat[late].shape if n else (1, 16, 128), BF),
            pltpu.SemaphoreType.DMA((max(n, 1), PARTS)),
            pltpu.SemaphoreType.DMA((max(m, 1), 4)),
            pltpu.SemaphoreType.DMA,
        ],
        {len(flat) + m + 1 + k: k for k in range(len(earlier))},
        size,
    )


def per_device(policies, anchor):
    policy = pltpu.with_memory_space_constraint(policies[0], pltpu.HBM)
    shards = pltpu.with_memory_space_constraint(anchor.reshape(16, 2, ROWS, WIDTH), pltpu.HBM)
    order = Order(jnp.stack([lax.axis_index(name) for name in ("xl", "c", "xh")]).astype(jnp.int32))
    swap = [(0, 1), (1, 0)]
    groups = exchange_groups()

    def exchange(tiles):
        return lax.all_to_all(
            tiles, AXES, split_axis=0, concat_axis=0, axis_index_groups=groups, tiled=True
        )

    def core(tiles):
        return lax.ppermute(tiles, "c", swap)

    def chip(tiles):
        return lax.ppermute(tiles, "xl", swap)

    theirs = core(cast_rows(order, policy))
    picked, rows = pick_rows(order, shards, policy)
    theirs, picked = add_theirs(order, rows, theirs, picked)
    other = chip(theirs)
    fetched = exchange(picked)
    own = add_own(order, policy, [core(tiles) for tiles in cast_own(order, policy)])

    own, *planes = blend_rows(order, own, other, fetched)
    finished = chip(own)
    back = exchange(own)
    pieces = [([core(tiles) for tiles in planes], False, True), ([own], True, True)]
    (blended,) = write_rows(order, pieces, [], None, None, WRITE_COST, late_in_hbm=True)

    first, high = split_planes(order, finished, back)
    back_first = lax.all_to_all(first, ("y", "z"), split_axis=0, concat_axis=0, tiled=True)
    back_second = chip(high)
    finished, back = order.behind(finished), order.behind(back)
    new_anchor = place_back(order, back, core(back))
    pieces = [([finished], True, False), ([core(finished)], False, False)]
    (blended,) = write_rows(order, pieces, [], blended, None)
    back_second = order.behind(back_second)
    back_first = order.behind(back_first)
    pieces = [(back_first, True, False, True), (back_second, True, True, False)]
    (new_anchor,) = write_rows(order, [], pieces, None, new_anchor, LAST_COST)
    pieces = [(core(back_first), False, False, True), (core(back_second), False, True, False)]
    (new_anchor,) = write_rows(order, [], pieces, None, new_anchor)
    return blended, new_anchor.reshape(SHARDS * ROWS, WIDTH)


def solution(mesh):
    fine = Mesh(mesh.devices.reshape(SIZES), AXES)
    shards = ("y", "z", "xh")
    return jax.shard_map(
        per_device,
        mesh=fine,
        in_specs=(P(("xl", "c"), shards, None), P(None, shards)),
        out_specs=(P(shards, None), P(None, shards)),
        check_vma=False,
    )
```

```python
import jax
import jax.numpy as jnp
import numpy as np
from jax import lax
from jax.experimental import pallas as pl
from jax.experimental.pallas import tpu as pltpu
from jax.sharding import Mesh, PartitionSpec as P

blend_rate = 0.3
GROUPS = 4

AXES = ("xl", "c", "y", "z", "xh")
SIZES = (2, 2, 4, 4, 2)
SHARDS = 32
ROWS = 256
WIDTH = 256
D = 8192
HALF = 128
QUARTER = 64
R = 32
BF = jnp.bfloat16
F32 = jnp.float32
VMEM_LIMIT = 10 << 20
PARTS = 8
PER = SHARDS // PARTS
WRITE_COST = 11 << 20
LAST_COST = 37 << 20
ANY = pl.BlockSpec(memory_space=pl.ANY)
HBM = pl.BlockSpec(memory_space=pltpu.HBM)
VMEM = pl.BlockSpec(memory_space=pltpu.VMEM)
TOKEN = jax.ShapeDtypeStruct((8, 128), jnp.int32)


def exchange_groups():
    ids = np.arange(128).reshape(SIZES)
    return [
        [int(ids[flip ^ xh, c, y, z, xh]) for xh in range(2) for y in range(4) for z in range(4)]
        for flip in range(2)
        for c in range(2)
    ]


def in_vmem(x):
    return pltpu.with_memory_space_constraint(x, pltpu.VMEM)


class Order:
    def __init__(self, place):
        self.place = place
        self.token = None

    def behind(self, x):
        x, self.token = lax.optimization_barrier((x, self.token))
        return x

    def run(self, body, name, args, specs, outs, out_specs, scratch, aliases=None, size=1024):
        held = [] if self.token is None else [self.token]

        def ordered(at, *refs):
            ins, rest = refs[: len(args)], refs[len(args) + len(held) :]
            results, others = rest[: len(outs)], rest[len(outs) + 1 :]
            body(at, *ins, *results, *others)

        *results, self.token = pl.pallas_call(
            ordered,
            out_shape=[*outs, TOKEN],
            grid_spec=pltpu.PrefetchScalarGridSpec(
                num_scalar_prefetch=1,
                grid=(),
                in_specs=[*specs, *[ANY] * len(held)],
                out_specs=[*out_specs, ANY],
                scratch_shapes=scratch,
            ),
            input_output_aliases=aliases or {},
            compiler_params=pltpu.CompilerParams(vmem_limit_bytes=VMEM_LIMIT),
            cost_estimate=pl.CostEstimate(flops=0, bytes_accessed=size, transcendentals=0),
            name=name,
        )(self.place, *args, *held)
        return results


def columns(g):
    return pl.ds(pl.multiple_of(g * WIDTH, WIDTH), WIDTH)


def slot(p, k):
    return (k % 2) * 16 + p * (PER // 2) + k // 2


def each(count, work):
    pl.loop(0, count)(work)


def first_row(at, core, chip, start, xl=None):
    xl = at[0] if xl is None else xl
    half = at[1] if core else 1 - at[1]
    quarter = xl if chip else 1 - xl
    return pl.multiple_of(half * HALF + quarter * QUARTER + start, 16)


def member_row(at, where, xh):
    differs = at[2] if xh == 0 else 1 - at[2]
    return first_row(at, *where, at[0] + differs - 2 * at[0] * differs)


def tiles_out(rows):
    return pltpu.VMEM((SHARDS, rows, WIDTH), BF)


def span_of(p):
    return pl.ds(pl.multiple_of(p * PER * WIDTH, WIDTH), PER * WIDTH)


def cast_rows(order, policy):
    def body(at, x_ref, o_ref, wide, sems):
        held = pl.ds(first_row(at, False, False, 0), QUARTER)

        def copy(p):
            return pltpu.make_async_copy(x_ref.at[held, span_of(p)], wide.at[:, span_of(p)], sems.at[p])

        def work(p):
            copy(p).wait()
            for k in range(PER):
                g = p * PER + k
                o_ref[slot(p, k)] = wide[:, columns(g)].astype(BF)

        each(PARTS, lambda p: copy(p).start())
        each(PARTS, work)

    (out,) = order.run(
        body,
        "cast_rows",
        (policy,),
        [HBM],
        [tiles_out(QUARTER)],
        [VMEM],
        [pltpu.VMEM((QUARTER, D), F32), pltpu.SemaphoreType.DMA((PARTS,))],
    )
    return out


def add_theirs(order, rows, tiles, picked):
    def body(at, x_ref, t_ref, p_ref, o_ref, q_ref, held, sems, picked_sems):
        def store(p):
            some = pl.ds(p * PER, PER)
            return pltpu.make_async_copy(held.at[some], o_ref.at[some], sems.at[p])

        def copy(p):
            some = pl.ds(p * PER, PER)
            return pltpu.make_async_copy(p_ref.at[some], q_ref.at[some], picked_sems.at[p])

        def work(p):
            for k in range(PER):
                at_slot = p * PER + k
                g = 2 * ((p & 3) * PER + k) + (p >> 2)
                held[at_slot] = (x_ref[:, columns(g)] + t_ref[at_slot].astype(F32)).astype(BF)
            store(p).start()

        each(PARTS, lambda p: copy(p).start())
        each(PARTS, work)
        each(PARTS, lambda p: copy(p).wait())
        each(PARTS, lambda p: store(p).wait())

    return order.run(
        body,
        "add_theirs",
        [in_vmem(x) for x in (rows, tiles, picked)],
        [VMEM] * 3,
        [pltpu.HBM((SHARDS, QUARTER, WIDTH), BF)] * 2,
        [HBM] * 2,
        [
            pltpu.VMEM((SHARDS, QUARTER, WIDTH), BF),
            pltpu.SemaphoreType.DMA((PARTS,)),
            pltpu.SemaphoreType.DMA((PARTS,)),
        ],
    )


def cast_own(order, policy):
    def body(at, x_ref, low_ref, high_ref, wide, sems):
        held = pl.ds(first_row(at, False, True, 0), QUARTER)

        def copy(p):
            return pltpu.make_async_copy(x_ref.at[held, span_of(p)], wide.at[:, span_of(p)], sems.at[p])

        def work(p):
            copy(p).wait()
            for k in range(PER):
                g = p * PER + k
                low_ref[slot(p, k)] = wide[:R, columns(g)].astype(BF)
                high_ref[slot(p, k)] = wide[R:, columns(g)].astype(BF)

        each(PARTS, lambda p: copy(p).start())
        each(PARTS, work)

    return order.run(
        body,
        "cast_own",
        (policy,),
        [HBM],
        [tiles_out(R)] * 2,
        [VMEM] * 2,
        [pltpu.VMEM((QUARTER, D), F32), pltpu.SemaphoreType.DMA((PARTS,))],
    )


def add_own(order, policy, chunks):
    def body(at, x_ref, low_ref, high_ref, o_ref, wide, sems):
        held = pl.ds(first_row(at, True, True, 0), QUARTER)

        def copy(p):
            return pltpu.make_async_copy(x_ref.at[held, span_of(p)], wide.at[:, span_of(p)], sems.at[p])

        def work(p):
            copy(p).wait()
            for k in range(PER):
                g = p * PER + k
                o_ref[slot(p, k), :R] = (wide[:R, columns(g)] + low_ref[slot(p, k)].astype(F32)).astype(BF)
                o_ref[slot(p, k), R:] = (wide[R:, columns(g)] + high_ref[slot(p, k)].astype(F32)).astype(BF)

        each(PARTS, lambda p: copy(p).start())
        each(PARTS, work)

    (out,) = order.run(
        body,
        "add_own",
        (policy, *[in_vmem(tiles) for tiles in chunks]),
        [HBM, VMEM, VMEM],
        [tiles_out(QUARTER)],
        [VMEM],
        [pltpu.VMEM((QUARTER, D), F32), pltpu.SemaphoreType.DMA((PARTS,))],
    )
    return out


def pick_rows(order, anchor, policy):
    def body(at, a_ref, x_ref, p_ref, rows_ref, a_sems, x_sems):
        rows = [member_row(at, (True, True, 0), xh) for xh in range(2)]
        theirs = pl.ds(first_row(at, True, False, 0), QUARTER)

        def fetch(p, xh):
            some = pl.ds(4 * p, 4)
            return pltpu.make_async_copy(
                a_ref.at[some, xh, pl.ds(rows[xh], QUARTER), :], p_ref.at[xh, some], a_sems.at[xh, p]
            )

        def copy(p):
            return pltpu.make_async_copy(
                x_ref.at[theirs, span_of(p)], rows_ref.at[:, span_of(p)], x_sems.at[p]
            )

        each(PARTS, lambda p: copy(p).start())
        for xh in range(2):
            each(4, lambda p, xh=xh: fetch(p, xh).start())
        each(PARTS, lambda p: copy(p).wait())
        for xh in range(2):
            each(4, lambda p, xh=xh: fetch(p, xh).wait())

    picked, rows = order.run(
        body,
        "pick_rows",
        (anchor, policy),
        [HBM, HBM],
        [pltpu.VMEM((2, 16, QUARTER, WIDTH), BF), pltpu.VMEM((QUARTER, D), F32)],
        [VMEM, VMEM],
        [pltpu.SemaphoreType.DMA((2, 4)), pltpu.SemaphoreType.DMA((PARTS,))],
    )
    return picked.reshape(SHARDS, QUARTER, WIDTH), rows


def blend_rows(order, own, other, anchor):
    def body(at, x_ref, t_ref, a_ref, o_ref, *rest):
        planes, held, sems = rest[:2], rest[2], rest[3]

        def stores(xh, p):
            some = pl.ds(p * PER, PER)
            all_some = pl.ds(xh * 16 + p * PER, PER)
            ends = (o_ref.at[all_some], planes[xh].at[some])
            return [
                pltpu.make_async_copy(held.at[all_some], end, sems.at[i, xh, p])
                for i, end in enumerate(ends)
            ]

        def work(xh, p):
            for k in range(PER):
                g = xh * 16 + p * PER + k
                total = x_ref[g].astype(F32) + t_ref[g].astype(F32)
                new = (1.0 - blend_rate) * a_ref[g].astype(F32) + (blend_rate / GROUPS) * total
                held[g] = new.astype(BF)
            for store in stores(xh, p):
                store.start()

        def finish(xh, p):
            for store in stores(xh, p):
                store.wait()

        for xh in range(2):
            each(4, lambda p, xh=xh: work(xh, p))
        for xh in range(2):
            each(4, lambda p, xh=xh: finish(xh, p))

    return order.run(
        body,
        "blend_rows",
        [in_vmem(x) for x in (own, other, anchor)],
        [VMEM] * 3,
        [pltpu.HBM((n, QUARTER, WIDTH), BF) for n in (SHARDS, 16, 16)],
        [HBM] * 3,
        [pltpu.VMEM((SHARDS, QUARTER, WIDTH), BF), pltpu.SemaphoreType.DMA((2, 2, 4))],
    )


def plane(at, same):
    return at[2] if same else 1 - at[2]


def split_planes(order, finished, back):
    def body(at, f_ref, b_ref, first_ref, high_ref, sems):
        def stores(p):
            some = pl.ds(4 * p, 4)
            ends = ((f_ref, True, first_ref), (b_ref, False, high_ref))
            return [
                pltpu.make_async_copy(x.at[plane(at, same), some], o.at[some], sems.at[i, p])
                for i, (x, same, o) in enumerate(ends)
            ]

        def start(p):
            for store in stores(p):
                store.start()

        def finish(p):
            for store in stores(p):
                store.wait()

        each(4, start)
        each(4, finish)

    half = (16, QUARTER, WIDTH)
    return order.run(
        body,
        "split_planes",
        [in_vmem(x.reshape(2, 16, QUARTER, WIDTH)) for x in (finished, back)],
        [VMEM, VMEM],
        [pltpu.HBM(half, BF)] * 2,
        [HBM] * 2,
        [pltpu.SemaphoreType.DMA((2, 4))],
    )


def place_back(order, own, other):
    def body(at, own_ref, other_ref, out_ref, held, sems, held_sems):
        def there(core, same, p):
            row = first_row(at, core, same, 0)
            return out_ref.at[pl.ds(4 * p, 4), plane(at, same), pl.ds(row, QUARTER), :]

        def place(ref, core, same, p):
            return pltpu.make_async_copy(
                ref.at[plane(at, same), pl.ds(4 * p, 4)],
                there(core, same, p),
                sems.at[int(core), int(same), p],
            )

        def fetch(xh, p):
            some = pl.ds(4 * p, 4)
            return pltpu.make_async_copy(other_ref.at[xh, some], held.at[xh, some], held_sems.at[xh, p])

        def forward(p):
            for xh in range(2):
                fetch(xh, p).wait()
            for same in (True, False):
                place(held, False, same, p).start()

        for xh in range(2):
            each(4, lambda p, xh=xh: fetch(xh, p).start())
        for same in (True, False):
            each(4, lambda p, same=same: place(own_ref, True, same, p).start())
        each(4, forward)
        for ref, core in ((own_ref, True), (held, False)):
            for same in (True, False):
                each(4, lambda p, ref=ref, core=core, same=same: place(ref, core, same, p).wait())

    shape = (2, 16, QUARTER, WIDTH)
    return order.run(
        body,
        "place_back",
        [in_vmem(own.reshape(shape)), other.reshape(shape)],
        [VMEM, ANY],
        [pltpu.HBM((16, 2, ROWS, WIDTH), BF)],
        [HBM],
        [
            pltpu.VMEM(shape, BF),
            pltpu.SemaphoreType.DMA((2, 2, 4)),
            pltpu.SemaphoreType.DMA((2, 4)),
        ],
    )[0]


def write_rows(order, wide_pieces, placed_pieces, blended, anchor, size=1024, late_in_hbm=False):
    n, m = len(wide_pieces), len(placed_pieces)
    counts = [len(arrays) for arrays, _, _ in wide_pieces]
    flat = [x for arrays, _, _ in wide_pieces for x in arrays]
    late = len(flat) - 1
    outs = [pltpu.HBM((ROWS, D), F32)] * (n > 0) + [pltpu.HBM((16, 2, ROWS, WIDTH), BF)] * (m > 0)
    earlier = [x for x, k in ((blended, n), (anchor, m)) if k and x is not None]

    def body(at, *refs):
        flat_refs, refs = list(refs[: len(flat)]), refs[len(flat) :]
        placed, refs = refs[:m], refs[m + len(earlier) :]
        out_refs, (wide, held, sems, placed_sems, held_sem) = refs[: len(outs)], refs[len(outs) :]

        def place(i, p):
            some = pl.ds(4 * p, 4)
            core, chip, same = placed_pieces[i][1:]
            there = pl.ds(first_row(at, core, chip, 0), QUARTER)
            return pltpu.make_async_copy(
                placed[i].at[some], out_refs[-1].at[some, plane(at, same), there, :], placed_sems.at[i, p]
            )

        def copy(i, p):
            there = pl.ds(first_row(at, *wide_pieces[i][1:], 0), QUARTER)
            return pltpu.make_async_copy(
                wide.at[i, :, span_of(p)], out_refs[0].at[there, span_of(p)], sems.at[i, p]
            )

        def work(i, tiles, p):
            for k in range(PER):
                if len(tiles) == 1:
                    tile = tiles[0][slot(p, k)]
                else:
                    tile = tiles[k % 2][p * (PER // 2) + k // 2]
                wide[i, :, columns(p * PER + k)] = tile.astype(F32)
            copy(i, p).start()

        if n:
            last = pltpu.make_async_copy(flat_refs[late], held, held_sem)
            last.start()
            flat_refs[late] = held
        for i in range(m):
            each(4, lambda p, i=i: place(i, p).start())
        for i in range(n):
            if i == n - 1:
                last.wait()
            tiles = flat_refs[sum(counts[:i]) : sum(counts[: i + 1])]
            each(PARTS, lambda p, i=i, tiles=tiles: work(i, tiles, p))
        for i in range(n):
            each(PARTS, lambda p, i=i: copy(i, p).wait())
        for i in range(m):
            each(4, lambda p, i=i: place(i, p).wait())

    args = [x if i == late else in_vmem(x) for i, x in enumerate(flat)]
    specs = [ANY if i == late else VMEM for i in range(len(flat))]
    if late_in_hbm:
        args[late] = pltpu.with_memory_space_constraint(args[late], pltpu.HBM)
        specs[late] = HBM
    return order.run(
        body,
        "write_rows",
        args + [in_vmem(x) for x, *_ in placed_pieces] + earlier,
        specs + [VMEM] * m + [HBM] * len(earlier),
        outs,
        [HBM] * len(outs),
        [
            pltpu.VMEM((max(n, 1), QUARTER, D if n else 128), F32),
            pltpu.VMEM(flat[late].shape if n else (1, 16, 128), BF),
            pltpu.SemaphoreType.DMA((max(n, 1), PARTS)),
            pltpu.SemaphoreType.DMA((max(m, 1), 4)),
            pltpu.SemaphoreType.DMA,
        ],
        {len(flat) + m + 1 + k: k for k in range(len(earlier))},
        size,
    )


def per_device(policies, anchor):
    policy = pltpu.with_memory_space_constraint(policies[0], pltpu.HBM)
    shards = pltpu.with_memory_space_constraint(anchor.reshape(16, 2, ROWS, WIDTH), pltpu.HBM)
    order = Order(jnp.stack([lax.axis_index(name) for name in ("xl", "c", "xh")]).astype(jnp.int32))
    swap = [(0, 1), (1, 0)]
    groups = exchange_groups()

    def exchange(tiles):
        return lax.all_to_all(
            tiles, AXES, split_axis=0, concat_axis=0, axis_index_groups=groups, tiled=True
        )

    def core(tiles):
        return lax.ppermute(tiles, "c", swap)

    def chip(tiles):
        return lax.ppermute(tiles, "xl", swap)

    theirs = core(cast_rows(order, policy))
    picked, rows = pick_rows(order, shards, policy)
    theirs, picked = add_theirs(order, rows, theirs, picked)
    other = chip(theirs)
    fetched = exchange(picked)
    own = add_own(order, policy, [core(tiles) for tiles in cast_own(order, policy)])

    own, *planes = blend_rows(order, own, other, fetched)
    finished = chip(own)
    back = exchange(own)
    pieces = [([core(tiles) for tiles in planes], False, True), ([own], True, True)]
    (blended,) = write_rows(order, pieces, [], None, None, WRITE_COST, late_in_hbm=True)

    back = order.behind(back)
    finished = order.behind(finished)
    first, high = split_planes(order, finished, back)
    back_first = lax.all_to_all(first, ("y", "z"), split_axis=0, concat_axis=0, tiled=True)
    back_second = chip(high)
    new_anchor = place_back(order, back, core(back))
    pieces = [([finished], True, False), ([core(finished)], False, False)]
    (blended,) = write_rows(order, pieces, [], blended, None)
    back_second = order.behind(back_second)
    back_first = order.behind(back_first)
    pieces = [(back_first, True, False, True), (back_second, True, True, False)]
    (new_anchor,) = write_rows(order, [], pieces, None, new_anchor, LAST_COST)
    pieces = [(core(back_first), False, False, True), (core(back_second), False, True, False)]
    (new_anchor,) = write_rows(order, [], pieces, None, new_anchor)
    return blended, new_anchor.reshape(SHARDS * ROWS, WIDTH)


def solution(mesh):
    fine = Mesh(mesh.devices.reshape(SIZES), AXES)
    shards = ("y", "z", "xh")
    return jax.shard_map(
        per_device,
        mesh=fine,
        in_specs=(P(("xl", "c"), shards, None), P(None, shards)),
        out_specs=(P(shards, None), P(None, shards)),
        check_vma=False,
    )
```

```python
import jax
import jax.numpy as jnp
import numpy as np
from jax import lax
from jax.experimental import pallas as pl
from jax.experimental.pallas import tpu as pltpu
from jax.sharding import Mesh, PartitionSpec as P

blend_rate = 0.3
GROUPS = 4

AXES = ("xl", "c", "y", "z", "xh")
SIZES = (2, 2, 4, 4, 2)
SHARDS = 32
ROWS = 256
WIDTH = 256
D = 8192
HALF = 128
QUARTER = 64
R = 32
BF = jnp.bfloat16
F32 = jnp.float32
VMEM_LIMIT = 10 << 20
PARTS = 8
PER = SHARDS // PARTS
WRITE_COST = 11 << 20
LAST_COST = 4 << 20
ANY = pl.BlockSpec(memory_space=pl.ANY)
HBM = pl.BlockSpec(memory_space=pltpu.HBM)
VMEM = pl.BlockSpec(memory_space=pltpu.VMEM)
TOKEN = jax.ShapeDtypeStruct((8, 128), jnp.int32)


def exchange_groups():
    ids = np.arange(128).reshape(SIZES)
    return [
        [int(ids[flip ^ xh, c, y, z, xh]) for xh in range(2) for y in range(4) for z in range(4)]
        for flip in range(2)
        for c in range(2)
    ]


def in_vmem(x):
    return pltpu.with_memory_space_constraint(x, pltpu.VMEM)


class Order:
    def __init__(self, place):
        self.place = place
        self.token = None

    def behind(self, x):
        x, self.token = lax.optimization_barrier((x, self.token))
        return x

    def run(self, body, name, args, specs, outs, out_specs, scratch, aliases=None, size=1024):
        held = [] if self.token is None else [self.token]

        def ordered(at, *refs):
            ins, rest = refs[: len(args)], refs[len(args) + len(held) :]
            results, others = rest[: len(outs)], rest[len(outs) + 1 :]
            body(at, *ins, *results, *others)

        *results, self.token = pl.pallas_call(
            ordered,
            out_shape=[*outs, TOKEN],
            grid_spec=pltpu.PrefetchScalarGridSpec(
                num_scalar_prefetch=1,
                grid=(),
                in_specs=[*specs, *[ANY] * len(held)],
                out_specs=[*out_specs, ANY],
                scratch_shapes=scratch,
            ),
            input_output_aliases=aliases or {},
            compiler_params=pltpu.CompilerParams(vmem_limit_bytes=VMEM_LIMIT),
            cost_estimate=pl.CostEstimate(flops=0, bytes_accessed=size, transcendentals=0),
            name=name,
        )(self.place, *args, *held)
        return results


def columns(g):
    return pl.ds(pl.multiple_of(g * WIDTH, WIDTH), WIDTH)


def slot(p, k):
    return (k % 2) * 16 + p * (PER // 2) + k // 2


def each(count, work):
    pl.loop(0, count)(work)


def first_row(at, core, chip, start, xl=None):
    xl = at[0] if xl is None else xl
    half = at[1] if core else 1 - at[1]
    quarter = xl if chip else 1 - xl
    return pl.multiple_of(half * HALF + quarter * QUARTER + start, 16)


def member_row(at, where, xh):
    differs = at[2] if xh == 0 else 1 - at[2]
    return first_row(at, *where, at[0] + differs - 2 * at[0] * differs)


def tiles_out(rows):
    return pltpu.VMEM((SHARDS, rows, WIDTH), BF)


def span_of(p):
    return pl.ds(pl.multiple_of(p * PER * WIDTH, WIDTH), PER * WIDTH)


def cast_rows(order, policy):
    def body(at, x_ref, o_ref, wide, sems):
        held = pl.ds(first_row(at, False, False, 0), QUARTER)

        def copy(p):
            return pltpu.make_async_copy(x_ref.at[held, span_of(p)], wide.at[:, span_of(p)], sems.at[p])

        def work(p):
            copy(p).wait()
            for k in range(PER):
                g = p * PER + k
                o_ref[slot(p, k)] = wide[:, columns(g)].astype(BF)

        each(PARTS, lambda p: copy(p).start())
        each(PARTS, work)

    (out,) = order.run(
        body,
        "cast_rows",
        (policy,),
        [HBM],
        [tiles_out(QUARTER)],
        [VMEM],
        [pltpu.VMEM((QUARTER, D), F32), pltpu.SemaphoreType.DMA((PARTS,))],
    )
    return out


def add_theirs(order, rows, tiles, picked):
    def body(at, x_ref, t_ref, p_ref, o_ref, q_ref, held, sems, picked_sems):
        def store(p):
            some = pl.ds(p * PER, PER)
            return pltpu.make_async_copy(held.at[some], o_ref.at[some], sems.at[p])

        def copy(p):
            some = pl.ds(p * PER, PER)
            return pltpu.make_async_copy(p_ref.at[some], q_ref.at[some], picked_sems.at[p])

        def work(p):
            for k in range(PER):
                at_slot = p * PER + k
                g = 2 * ((p & 3) * PER + k) + (p >> 2)
                held[at_slot] = (x_ref[:, columns(g)] + t_ref[at_slot].astype(F32)).astype(BF)
            store(p).start()

        each(PARTS, lambda p: copy(p).start())
        each(PARTS, work)
        each(PARTS, lambda p: copy(p).wait())
        each(PARTS, lambda p: store(p).wait())

    return order.run(
        body,
        "add_theirs",
        [in_vmem(x) for x in (rows, tiles, picked)],
        [VMEM] * 3,
        [pltpu.HBM((SHARDS, QUARTER, WIDTH), BF)] * 2,
        [HBM] * 2,
        [
            pltpu.VMEM((SHARDS, QUARTER, WIDTH), BF),
            pltpu.SemaphoreType.DMA((PARTS,)),
            pltpu.SemaphoreType.DMA((PARTS,)),
        ],
    )


def cast_own(order, policy):
    def body(at, x_ref, low_ref, high_ref, wide, sems):
        held = pl.ds(first_row(at, False, True, 0), QUARTER)

        def copy(p):
            return pltpu.make_async_copy(x_ref.at[held, span_of(p)], wide.at[:, span_of(p)], sems.at[p])

        def work(p):
            copy(p).wait()
            for k in range(PER):
                g = p * PER + k
                low_ref[slot(p, k)] = wide[:R, columns(g)].astype(BF)
                high_ref[slot(p, k)] = wide[R:, columns(g)].astype(BF)

        each(PARTS, lambda p: copy(p).start())
        each(PARTS, work)

    return order.run(
        body,
        "cast_own",
        (policy,),
        [HBM],
        [tiles_out(R)] * 2,
        [VMEM] * 2,
        [pltpu.VMEM((QUARTER, D), F32), pltpu.SemaphoreType.DMA((PARTS,))],
    )


def add_own(order, policy, chunks):
    def body(at, x_ref, low_ref, high_ref, o_ref, wide, sems):
        held = pl.ds(first_row(at, True, True, 0), QUARTER)

        def copy(p):
            return pltpu.make_async_copy(x_ref.at[held, span_of(p)], wide.at[:, span_of(p)], sems.at[p])

        def work(p):
            copy(p).wait()
            for k in range(PER):
                g = p * PER + k
                o_ref[slot(p, k), :R] = (wide[:R, columns(g)] + low_ref[slot(p, k)].astype(F32)).astype(BF)
                o_ref[slot(p, k), R:] = (wide[R:, columns(g)] + high_ref[slot(p, k)].astype(F32)).astype(BF)

        each(PARTS, lambda p: copy(p).start())
        each(PARTS, work)

    (out,) = order.run(
        body,
        "add_own",
        (policy, *[in_vmem(tiles) for tiles in chunks]),
        [HBM, VMEM, VMEM],
        [tiles_out(QUARTER)],
        [VMEM],
        [pltpu.VMEM((QUARTER, D), F32), pltpu.SemaphoreType.DMA((PARTS,))],
    )
    return out


def pick_rows(order, anchor, policy):
    def body(at, a_ref, x_ref, p_ref, rows_ref, a_sems, x_sems):
        rows = [member_row(at, (True, True, 0), xh) for xh in range(2)]
        theirs = pl.ds(first_row(at, True, False, 0), QUARTER)

        def fetch(p, xh):
            some = pl.ds(4 * p, 4)
            return pltpu.make_async_copy(
                a_ref.at[some, xh, pl.ds(rows[xh], QUARTER), :], p_ref.at[xh, some], a_sems.at[xh, p]
            )

        def copy(p):
            return pltpu.make_async_copy(
                x_ref.at[theirs, span_of(p)], rows_ref.at[:, span_of(p)], x_sems.at[p]
            )

        each(PARTS, lambda p: copy(p).start())
        for xh in range(2):
            each(4, lambda p, xh=xh: fetch(p, xh).start())
        each(PARTS, lambda p: copy(p).wait())
        for xh in range(2):
            each(4, lambda p, xh=xh: fetch(p, xh).wait())

    picked, rows = order.run(
        body,
        "pick_rows",
        (anchor, policy),
        [HBM, HBM],
        [pltpu.VMEM((2, 16, QUARTER, WIDTH), BF), pltpu.VMEM((QUARTER, D), F32)],
        [VMEM, VMEM],
        [pltpu.SemaphoreType.DMA((2, 4)), pltpu.SemaphoreType.DMA((PARTS,))],
    )
    return picked.reshape(SHARDS, QUARTER, WIDTH), rows


def blend_rows(order, own, other, anchor):
    def body(at, x_ref, t_ref, a_ref, o_ref, *rest):
        planes, held, sems = rest[:2], rest[2], rest[3]

        def stores(xh, p):
            some = pl.ds(p * PER, PER)
            all_some = pl.ds(xh * 16 + p * PER, PER)
            ends = (o_ref.at[all_some], planes[xh].at[some])
            return [
                pltpu.make_async_copy(held.at[all_some], end, sems.at[i, xh, p])
                for i, end in enumerate(ends)
            ]

        def work(xh, p):
            for k in range(PER):
                g = xh * 16 + p * PER + k
                total = x_ref[g].astype(F32) + t_ref[g].astype(F32)
                new = (1.0 - blend_rate) * a_ref[g].astype(F32) + (blend_rate / GROUPS) * total
                held[g] = new.astype(BF)
            for store in stores(xh, p):
                store.start()

        def finish(xh, p):
            for store in stores(xh, p):
                store.wait()

        for xh in range(2):
            each(4, lambda p, xh=xh: work(xh, p))
        for xh in range(2):
            each(4, lambda p, xh=xh: finish(xh, p))

    return order.run(
        body,
        "blend_rows",
        [in_vmem(x) for x in (own, other, anchor)],
        [VMEM] * 3,
        [pltpu.HBM((n, QUARTER, WIDTH), BF) for n in (SHARDS, 16, 16)],
        [HBM] * 3,
        [pltpu.VMEM((SHARDS, QUARTER, WIDTH), BF), pltpu.SemaphoreType.DMA((2, 2, 4))],
    )


def plane(at, same):
    return at[2] if same else 1 - at[2]


def split_planes(order, finished, back):
    def body(at, f_ref, b_ref, first_ref, high_ref, sems):
        def stores(p):
            some = pl.ds(4 * p, 4)
            ends = ((f_ref, True, first_ref), (b_ref, False, high_ref))
            return [
                pltpu.make_async_copy(x.at[plane(at, same), some], o.at[some], sems.at[i, p])
                for i, (x, same, o) in enumerate(ends)
            ]

        def start(p):
            for store in stores(p):
                store.start()

        def finish(p):
            for store in stores(p):
                store.wait()

        each(4, start)
        each(4, finish)

    half = (16, QUARTER, WIDTH)
    return order.run(
        body,
        "split_planes",
        [in_vmem(x.reshape(2, 16, QUARTER, WIDTH)) for x in (finished, back)],
        [VMEM, VMEM],
        [pltpu.HBM(half, BF)] * 2,
        [HBM] * 2,
        [pltpu.SemaphoreType.DMA((2, 4))],
    )


def place_back(order, own, other):
    def body(at, own_ref, other_ref, out_ref, held, sems, held_sems):
        def there(core, same, p):
            row = first_row(at, core, same, 0)
            return out_ref.at[pl.ds(4 * p, 4), plane(at, same), pl.ds(row, QUARTER), :]

        def place(ref, core, same, p):
            return pltpu.make_async_copy(
                ref.at[plane(at, same), pl.ds(4 * p, 4)],
                there(core, same, p),
                sems.at[int(core), int(same), p],
            )

        def fetch(xh, p):
            some = pl.ds(4 * p, 4)
            return pltpu.make_async_copy(other_ref.at[xh, some], held.at[xh, some], held_sems.at[xh, p])

        def forward(p):
            for xh in range(2):
                fetch(xh, p).wait()
            for same in (True, False):
                place(held, False, same, p).start()

        for xh in range(2):
            each(4, lambda p, xh=xh: fetch(xh, p).start())
        for same in (True, False):
            each(4, lambda p, same=same: place(own_ref, True, same, p).start())
        each(4, forward)
        for ref, core in ((own_ref, True), (held, False)):
            for same in (True, False):
                each(4, lambda p, ref=ref, core=core, same=same: place(ref, core, same, p).wait())

    shape = (2, 16, QUARTER, WIDTH)
    return order.run(
        body,
        "place_back",
        [in_vmem(own.reshape(shape)), other.reshape(shape)],
        [VMEM, ANY],
        [pltpu.HBM((16, 2, ROWS, WIDTH), BF)],
        [HBM],
        [
            pltpu.VMEM(shape, BF),
            pltpu.SemaphoreType.DMA((2, 2, 4)),
            pltpu.SemaphoreType.DMA((2, 4)),
        ],
    )[0]


def write_rows(order, wide_pieces, placed_pieces, blended, anchor, size=1024, late_in_hbm=False):
    n, m = len(wide_pieces), len(placed_pieces)
    counts = [len(arrays) for arrays, _, _ in wide_pieces]
    flat = [x for arrays, _, _ in wide_pieces for x in arrays]
    late = len(flat) - 1
    outs = [pltpu.HBM((ROWS, D), F32)] * (n > 0) + [pltpu.HBM((16, 2, ROWS, WIDTH), BF)] * (m > 0)
    earlier = [x for x, k in ((blended, n), (anchor, m)) if k and x is not None]

    def body(at, *refs):
        flat_refs, refs = list(refs[: len(flat)]), refs[len(flat) :]
        placed, refs = refs[:m], refs[m + len(earlier) :]
        out_refs, (wide, held, sems, placed_sems, held_sem) = refs[: len(outs)], refs[len(outs) :]

        def place(i, p):
            some = pl.ds(4 * p, 4)
            core, chip, same = placed_pieces[i][1:]
            there = pl.ds(first_row(at, core, chip, 0), QUARTER)
            return pltpu.make_async_copy(
                placed[i].at[some], out_refs[-1].at[some, plane(at, same), there, :], placed_sems.at[i, p]
            )

        def copy(i, p):
            there = pl.ds(first_row(at, *wide_pieces[i][1:], 0), QUARTER)
            return pltpu.make_async_copy(
                wide.at[i, :, span_of(p)], out_refs[0].at[there, span_of(p)], sems.at[i, p]
            )

        def work(i, tiles, p):
            for k in range(PER):
                if len(tiles) == 1:
                    tile = tiles[0][slot(p, k)]
                else:
                    tile = tiles[k % 2][p * (PER // 2) + k // 2]
                wide[i, :, columns(p * PER + k)] = tile.astype(F32)
            copy(i, p).start()

        if n:
            last = pltpu.make_async_copy(flat_refs[late], held, held_sem)
            last.start()
            flat_refs[late] = held
        for i in range(m):
            each(4, lambda p, i=i: place(i, p).start())
        for i in range(n):
            if i == n - 1:
                last.wait()
            tiles = flat_refs[sum(counts[:i]) : sum(counts[: i + 1])]
            each(PARTS, lambda p, i=i, tiles=tiles: work(i, tiles, p))
        for i in range(n):
            each(PARTS, lambda p, i=i: copy(i, p).wait())
        for i in range(m):
            each(4, lambda p, i=i: place(i, p).wait())

    args = [x if i == late else in_vmem(x) for i, x in enumerate(flat)]
    specs = [ANY if i == late else VMEM for i in range(len(flat))]
    if late_in_hbm:
        args[late] = pltpu.with_memory_space_constraint(args[late], pltpu.HBM)
        specs[late] = HBM
    return order.run(
        body,
        "write_rows",
        args + [in_vmem(x) for x, *_ in placed_pieces] + earlier,
        specs + [VMEM] * m + [HBM] * len(earlier),
        outs,
        [HBM] * len(outs),
        [
            pltpu.VMEM((max(n, 1), QUARTER, D if n else 128), F32),
            pltpu.VMEM(flat[late].shape if n else (1, 16, 128), BF),
            pltpu.SemaphoreType.DMA((max(n, 1), PARTS)),
            pltpu.SemaphoreType.DMA((max(m, 1), 4)),
            pltpu.SemaphoreType.DMA,
        ],
        {len(flat) + m + 1 + k: k for k in range(len(earlier))},
        size,
    )


def per_device(policies, anchor):
    policy = pltpu.with_memory_space_constraint(policies[0], pltpu.HBM)
    shards = pltpu.with_memory_space_constraint(anchor.reshape(16, 2, ROWS, WIDTH), pltpu.HBM)
    order = Order(jnp.stack([lax.axis_index(name) for name in ("xl", "c", "xh")]).astype(jnp.int32))
    swap = [(0, 1), (1, 0)]
    groups = exchange_groups()

    def exchange(tiles):
        return lax.all_to_all(
            tiles, AXES, split_axis=0, concat_axis=0, axis_index_groups=groups, tiled=True
        )

    def core(tiles):
        return lax.ppermute(tiles, "c", swap)

    def chip(tiles):
        return lax.ppermute(tiles, "xl", swap)

    theirs = core(cast_rows(order, policy))
    picked, rows = pick_rows(order, shards, policy)
    theirs, picked = add_theirs(order, rows, theirs, picked)
    other = chip(theirs)
    fetched = exchange(picked)
    own = add_own(order, policy, [core(tiles) for tiles in cast_own(order, policy)])

    own, *planes = blend_rows(order, own, other, fetched)
    finished = chip(own)
    back = exchange(own)
    pieces = [([core(tiles) for tiles in planes], False, True), ([own], True, True)]
    (blended,) = write_rows(order, pieces, [], None, None, WRITE_COST, late_in_hbm=True)

    back = order.behind(back)
    finished = order.behind(finished)
    first, high = split_planes(order, finished, back)
    back_first = lax.all_to_all(first, ("y", "z"), split_axis=0, concat_axis=0, tiled=True)
    back_second = chip(high)
    new_anchor = place_back(order, back, core(back))
    pieces = [([finished], True, False), ([core(finished)], False, False)]
    (blended,) = write_rows(order, pieces, [], blended, None)
    back_second = order.behind(back_second)
    there_second = core(back_second)
    (new_anchor,) = write_rows(order, [], [(back_second, True, True, False)], None, new_anchor)
    back_first = order.behind(back_first)
    there_first = core(back_first)
    pieces = [(back_first, True, False, True), (there_second, False, True, False)]
    (new_anchor,) = write_rows(order, [], pieces, None, new_anchor, LAST_COST)
    (new_anchor,) = write_rows(order, [], [(there_first, False, False, True)], None, new_anchor)
    return blended, new_anchor.reshape(SHARDS * ROWS, WIDTH)


def solution(mesh):
    fine = Mesh(mesh.devices.reshape(SIZES), AXES)
    shards = ("y", "z", "xh")
    return jax.shard_map(
        per_device,
        mesh=fine,
        in_specs=(P(("xl", "c"), shards, None), P(None, shards)),
        out_specs=(P(shards, None), P(None, shards)),
        check_vma=False,
    )
```

```python
import jax
import jax.numpy as jnp
import numpy as np
from jax import lax
from jax.experimental import pallas as pl
from jax.experimental.pallas import tpu as pltpu
from jax.sharding import Mesh, PartitionSpec as P

blend_rate = 0.3
GROUPS = 4

AXES = ("xl", "c", "y", "z", "xh")
SIZES = (2, 2, 4, 4, 2)
SHARDS = 32
ROWS = 256
WIDTH = 256
D = 8192
HALF = 128
QUARTER = 64
R = 32
BF = jnp.bfloat16
F32 = jnp.float32
VMEM_LIMIT = 10 << 20
PARTS = 8
PER = SHARDS // PARTS
WRITE_COST = 11 << 20
LAST_COST = 4 << 20
ANY = pl.BlockSpec(memory_space=pl.ANY)
HBM = pl.BlockSpec(memory_space=pltpu.HBM)
VMEM = pl.BlockSpec(memory_space=pltpu.VMEM)
TOKEN = jax.ShapeDtypeStruct((8, 128), jnp.int32)


def exchange_groups():
    ids = np.arange(128).reshape(SIZES)
    return [
        [int(ids[flip ^ xh, c, y, z, xh]) for xh in range(2) for y in range(4) for z in range(4)]
        for flip in range(2)
        for c in range(2)
    ]


def in_vmem(x):
    return pltpu.with_memory_space_constraint(x, pltpu.VMEM)


class Order:
    def __init__(self, place):
        self.place = place
        self.token = None

    def behind(self, x):
        x, self.token = lax.optimization_barrier((x, self.token))
        return x

    def run(self, body, name, args, specs, outs, out_specs, scratch, aliases=None, size=1024):
        held = [] if self.token is None else [self.token]

        def ordered(at, *refs):
            ins, rest = refs[: len(args)], refs[len(args) + len(held) :]
            results, others = rest[: len(outs)], rest[len(outs) + 1 :]
            body(at, *ins, *results, *others)

        *results, self.token = pl.pallas_call(
            ordered,
            out_shape=[*outs, TOKEN],
            grid_spec=pltpu.PrefetchScalarGridSpec(
                num_scalar_prefetch=1,
                grid=(),
                in_specs=[*specs, *[ANY] * len(held)],
                out_specs=[*out_specs, ANY],
                scratch_shapes=scratch,
            ),
            input_output_aliases=aliases or {},
            compiler_params=pltpu.CompilerParams(vmem_limit_bytes=VMEM_LIMIT),
            cost_estimate=pl.CostEstimate(flops=0, bytes_accessed=size, transcendentals=0),
            name=name,
        )(self.place, *args, *held)
        return results


def columns(g):
    return pl.ds(pl.multiple_of(g * WIDTH, WIDTH), WIDTH)


def slot(p, k):
    return (k % 2) * 16 + p * (PER // 2) + k // 2


def each(count, work):
    if count > 4:
        pl.loop(0, count)(work)
    else:
        for i in range(count):
            work(i)


def first_row(at, core, chip, start, xl=None):
    xl = at[0] if xl is None else xl
    half = at[1] if core else 1 - at[1]
    quarter = xl if chip else 1 - xl
    return pl.multiple_of(half * HALF + quarter * QUARTER + start, 16)


def member_row(at, where, xh):
    differs = at[2] if xh == 0 else 1 - at[2]
    return first_row(at, *where, at[0] + differs - 2 * at[0] * differs)


def tiles_out(rows):
    return pltpu.VMEM((SHARDS, rows, WIDTH), BF)


def span_of(p):
    return pl.ds(pl.multiple_of(p * PER * WIDTH, WIDTH), PER * WIDTH)


def cast_rows(order, policy):
    def body(at, x_ref, o_ref, wide, sems):
        held = pl.ds(first_row(at, False, False, 0), QUARTER)

        def copy(p):
            return pltpu.make_async_copy(x_ref.at[held, span_of(p)], wide.at[:, span_of(p)], sems.at[p])

        def work(p):
            copy(p).wait()
            for k in range(PER):
                g = p * PER + k
                o_ref[slot(p, k)] = wide[:, columns(g)].astype(BF)

        each(PARTS, lambda p: copy(p).start())
        each(PARTS, work)

    (out,) = order.run(
        body,
        "cast_rows",
        (policy,),
        [HBM],
        [tiles_out(QUARTER)],
        [VMEM],
        [pltpu.VMEM((QUARTER, D), F32), pltpu.SemaphoreType.DMA((PARTS,))],
    )
    return out


def add_theirs(order, rows, tiles, picked):
    def body(at, x_ref, t_ref, p_ref, o_ref, q_ref, held, sems, picked_sems):
        def store(p):
            some = pl.ds(p * PER, PER)
            return pltpu.make_async_copy(held.at[some], o_ref.at[some], sems.at[p])

        def copy(p):
            some = pl.ds(p * PER, PER)
            return pltpu.make_async_copy(p_ref.at[some], q_ref.at[some], picked_sems.at[p])

        def work(p):
            for k in range(PER):
                at_slot = p * PER + k
                g = 2 * ((p & 3) * PER + k) + (p >> 2)
                held[at_slot] = (x_ref[:, columns(g)] + t_ref[at_slot].astype(F32)).astype(BF)
            store(p).start()

        each(PARTS, lambda p: copy(p).start())
        each(PARTS, work)
        each(PARTS, lambda p: copy(p).wait())
        each(PARTS, lambda p: store(p).wait())

    return order.run(
        body,
        "add_theirs",
        [in_vmem(x) for x in (rows, tiles, picked)],
        [VMEM] * 3,
        [pltpu.HBM((SHARDS, QUARTER, WIDTH), BF)] * 2,
        [HBM] * 2,
        [
            pltpu.VMEM((SHARDS, QUARTER, WIDTH), BF),
            pltpu.SemaphoreType.DMA((PARTS,)),
            pltpu.SemaphoreType.DMA((PARTS,)),
        ],
    )


def cast_own(order, policy):
    def body(at, x_ref, low_ref, high_ref, wide, sems):
        held = pl.ds(first_row(at, False, True, 0), QUARTER)

        def copy(p):
            return pltpu.make_async_copy(x_ref.at[held, span_of(p)], wide.at[:, span_of(p)], sems.at[p])

        def work(p):
            copy(p).wait()
            for k in range(PER):
                g = p * PER + k
                low_ref[slot(p, k)] = wide[:R, columns(g)].astype(BF)
                high_ref[slot(p, k)] = wide[R:, columns(g)].astype(BF)

        each(PARTS, lambda p: copy(p).start())
        each(PARTS, work)

    return order.run(
        body,
        "cast_own",
        (policy,),
        [HBM],
        [tiles_out(R)] * 2,
        [VMEM] * 2,
        [pltpu.VMEM((QUARTER, D), F32), pltpu.SemaphoreType.DMA((PARTS,))],
    )


def add_own(order, policy, chunks):
    def body(at, x_ref, low_ref, high_ref, o_ref, wide, sems):
        held = pl.ds(first_row(at, True, True, 0), QUARTER)

        def copy(p):
            return pltpu.make_async_copy(x_ref.at[held, span_of(p)], wide.at[:, span_of(p)], sems.at[p])

        def work(p):
            copy(p).wait()
            for k in range(PER):
                g = p * PER + k
                o_ref[slot(p, k), :R] = (wide[:R, columns(g)] + low_ref[slot(p, k)].astype(F32)).astype(BF)
                o_ref[slot(p, k), R:] = (wide[R:, columns(g)] + high_ref[slot(p, k)].astype(F32)).astype(BF)

        each(PARTS, lambda p: copy(p).start())
        each(PARTS, work)

    (out,) = order.run(
        body,
        "add_own",
        (policy, *[in_vmem(tiles) for tiles in chunks]),
        [HBM, VMEM, VMEM],
        [tiles_out(QUARTER)],
        [VMEM],
        [pltpu.VMEM((QUARTER, D), F32), pltpu.SemaphoreType.DMA((PARTS,))],
    )
    return out


def pick_rows(order, anchor, policy):
    def body(at, a_ref, x_ref, p_ref, rows_ref, a_sems, x_sems):
        rows = [member_row(at, (True, True, 0), xh) for xh in range(2)]
        theirs = pl.ds(first_row(at, True, False, 0), QUARTER)

        def fetch(p, xh):
            some = pl.ds(4 * p, 4)
            return pltpu.make_async_copy(
                a_ref.at[some, xh, pl.ds(rows[xh], QUARTER), :], p_ref.at[xh, some], a_sems.at[xh, p]
            )

        def copy(p):
            return pltpu.make_async_copy(
                x_ref.at[theirs, span_of(p)], rows_ref.at[:, span_of(p)], x_sems.at[p]
            )

        each(PARTS, lambda p: copy(p).start())
        for xh in range(2):
            each(4, lambda p, xh=xh: fetch(p, xh).start())
        each(PARTS, lambda p: copy(p).wait())
        for xh in range(2):
            each(4, lambda p, xh=xh: fetch(p, xh).wait())

    picked, rows = order.run(
        body,
        "pick_rows",
        (anchor, policy),
        [HBM, HBM],
        [pltpu.VMEM((2, 16, QUARTER, WIDTH), BF), pltpu.VMEM((QUARTER, D), F32)],
        [VMEM, VMEM],
        [pltpu.SemaphoreType.DMA((2, 4)), pltpu.SemaphoreType.DMA((PARTS,))],
    )
    return picked.reshape(SHARDS, QUARTER, WIDTH), rows


def blend_rows(order, own, other, anchor):
    def body(at, x_ref, t_ref, a_ref, o_ref, *rest):
        planes, held, sems = rest[:2], rest[2], rest[3]

        def stores(xh, p):
            some = pl.ds(p * PER, PER)
            all_some = pl.ds(xh * 16 + p * PER, PER)
            ends = (o_ref.at[all_some], planes[xh].at[some])
            return [
                pltpu.make_async_copy(held.at[all_some], end, sems.at[i, xh, p])
                for i, end in enumerate(ends)
            ]

        def work(xh, p):
            for k in range(PER):
                g = xh * 16 + p * PER + k
                total = x_ref[g].astype(F32) + t_ref[g].astype(F32)
                new = (1.0 - blend_rate) * a_ref[g].astype(F32) + (blend_rate / GROUPS) * total
                held[g] = new.astype(BF)
            for store in stores(xh, p):
                store.start()

        def finish(xh, p):
            for store in stores(xh, p):
                store.wait()

        for xh in range(2):
            each(4, lambda p, xh=xh: work(xh, p))
        for xh in range(2):
            each(4, lambda p, xh=xh: finish(xh, p))

    return order.run(
        body,
        "blend_rows",
        [in_vmem(x) for x in (own, other, anchor)],
        [VMEM] * 3,
        [pltpu.HBM((n, QUARTER, WIDTH), BF) for n in (SHARDS, 16, 16)],
        [HBM] * 3,
        [pltpu.VMEM((SHARDS, QUARTER, WIDTH), BF), pltpu.SemaphoreType.DMA((2, 2, 4))],
    )


def plane(at, same):
    return at[2] if same else 1 - at[2]


def split_planes(order, finished, back):
    def body(at, f_ref, b_ref, first_ref, high_ref, sems):
        def stores(p):
            some = pl.ds(4 * p, 4)
            ends = ((f_ref, True, first_ref), (b_ref, False, high_ref))
            return [
                pltpu.make_async_copy(x.at[plane(at, same), some], o.at[some], sems.at[i, p])
                for i, (x, same, o) in enumerate(ends)
            ]

        def start(p):
            for store in stores(p):
                store.start()

        def finish(p):
            for store in stores(p):
                store.wait()

        each(4, start)
        each(4, finish)

    half = (16, QUARTER, WIDTH)
    return order.run(
        body,
        "split_planes",
        [in_vmem(x.reshape(2, 16, QUARTER, WIDTH)) for x in (finished, back)],
        [VMEM, VMEM],
        [pltpu.HBM(half, BF)] * 2,
        [HBM] * 2,
        [pltpu.SemaphoreType.DMA((2, 4))],
    )


def place_back(order, own, other):
    def body(at, own_ref, other_ref, out_ref, held, sems, held_sems):
        def there(core, same, p):
            row = first_row(at, core, same, 0)
            return out_ref.at[pl.ds(4 * p, 4), plane(at, same), pl.ds(row, QUARTER), :]

        def place(ref, core, same, p):
            return pltpu.make_async_copy(
                ref.at[plane(at, same), pl.ds(4 * p, 4)],
                there(core, same, p),
                sems.at[int(core), int(same), p],
            )

        def fetch(xh, p):
            some = pl.ds(4 * p, 4)
            return pltpu.make_async_copy(other_ref.at[xh, some], held.at[xh, some], held_sems.at[xh, p])

        def forward(p):
            for xh in range(2):
                fetch(xh, p).wait()
            for same in (True, False):
                place(held, False, same, p).start()

        for xh in range(2):
            each(4, lambda p, xh=xh: fetch(xh, p).start())
        for same in (True, False):
            each(4, lambda p, same=same: place(own_ref, True, same, p).start())
        each(4, forward)
        for ref, core in ((own_ref, True), (held, False)):
            for same in (True, False):
                each(4, lambda p, ref=ref, core=core, same=same: place(ref, core, same, p).wait())

    shape = (2, 16, QUARTER, WIDTH)
    return order.run(
        body,
        "place_back",
        [in_vmem(own.reshape(shape)), other.reshape(shape)],
        [VMEM, ANY],
        [pltpu.HBM((16, 2, ROWS, WIDTH), BF)],
        [HBM],
        [
            pltpu.VMEM(shape, BF),
            pltpu.SemaphoreType.DMA((2, 2, 4)),
            pltpu.SemaphoreType.DMA((2, 4)),
        ],
    )[0]


def write_rows(order, wide_pieces, placed_pieces, blended, anchor, size=1024, late_in_hbm=False):
    n, m = len(wide_pieces), len(placed_pieces)
    counts = [len(arrays) for arrays, _, _ in wide_pieces]
    flat = [x for arrays, _, _ in wide_pieces for x in arrays]
    late = len(flat) - 1
    outs = [pltpu.HBM((ROWS, D), F32)] * (n > 0) + [pltpu.HBM((16, 2, ROWS, WIDTH), BF)] * (m > 0)
    earlier = [x for x, k in ((blended, n), (anchor, m)) if k and x is not None]

    def body(at, *refs):
        flat_refs, refs = list(refs[: len(flat)]), refs[len(flat) :]
        placed, refs = refs[:m], refs[m + len(earlier) :]
        out_refs, (wide, held, sems, placed_sems, held_sem) = refs[: len(outs)], refs[len(outs) :]

        def place(i, p):
            some = pl.ds(4 * p, 4)
            core, chip, same = placed_pieces[i][1:]
            there = pl.ds(first_row(at, core, chip, 0), QUARTER)
            return pltpu.make_async_copy(
                placed[i].at[some], out_refs[-1].at[some, plane(at, same), there, :], placed_sems.at[i, p]
            )

        def copy(i, p):
            there = pl.ds(first_row(at, *wide_pieces[i][1:], 0), QUARTER)
            return pltpu.make_async_copy(
                wide.at[i, :, span_of(p)], out_refs[0].at[there, span_of(p)], sems.at[i, p]
            )

        def work(i, tiles, p):
            for k in range(PER):
                if len(tiles) == 1:
                    tile = tiles[0][slot(p, k)]
                else:
                    tile = tiles[k % 2][p * (PER // 2) + k // 2]
                wide[i, :, columns(p * PER + k)] = tile.astype(F32)
            copy(i, p).start()

        if n:
            last = pltpu.make_async_copy(flat_refs[late], held, held_sem)
            last.start()
            flat_refs[late] = held
        for i in range(m):
            each(4, lambda p, i=i: place(i, p).start())
        for i in range(n):
            if i == n - 1:
                last.wait()
            tiles = flat_refs[sum(counts[:i]) : sum(counts[: i + 1])]
            each(PARTS, lambda p, i=i, tiles=tiles: work(i, tiles, p))
        for i in range(n):
            each(PARTS, lambda p, i=i: copy(i, p).wait())
        for i in range(m):
            each(4, lambda p, i=i: place(i, p).wait())

    args = [x if i == late else in_vmem(x) for i, x in enumerate(flat)]
    specs = [ANY if i == late else VMEM for i in range(len(flat))]
    if late_in_hbm:
        args[late] = pltpu.with_memory_space_constraint(args[late], pltpu.HBM)
        specs[late] = HBM
    return order.run(
        body,
        "write_rows",
        args + [in_vmem(x) for x, *_ in placed_pieces] + earlier,
        specs + [VMEM] * m + [HBM] * len(earlier),
        outs,
        [HBM] * len(outs),
        [
            pltpu.VMEM((max(n, 1), QUARTER, D if n else 128), F32),
            pltpu.VMEM(flat[late].shape if n else (1, 16, 128), BF),
            pltpu.SemaphoreType.DMA((max(n, 1), PARTS)),
            pltpu.SemaphoreType.DMA((max(m, 1), 4)),
            pltpu.SemaphoreType.DMA,
        ],
        {len(flat) + m + 1 + k: k for k in range(len(earlier))},
        size,
    )


def per_device(policies, anchor):
    policy = pltpu.with_memory_space_constraint(policies[0], pltpu.HBM)
    shards = pltpu.with_memory_space_constraint(anchor.reshape(16, 2, ROWS, WIDTH), pltpu.HBM)
    order = Order(jnp.stack([lax.axis_index(name) for name in ("xl", "c", "xh")]).astype(jnp.int32))
    swap = [(0, 1), (1, 0)]
    groups = exchange_groups()

    def exchange(tiles):
        return lax.all_to_all(
            tiles, AXES, split_axis=0, concat_axis=0, axis_index_groups=groups, tiled=True
        )

    def core(tiles):
        return lax.ppermute(tiles, "c", swap)

    def chip(tiles):
        return lax.ppermute(tiles, "xl", swap)

    theirs = core(cast_rows(order, policy))
    picked, rows = pick_rows(order, shards, policy)
    theirs, picked = add_theirs(order, rows, theirs, picked)
    other = chip(theirs)
    fetched = exchange(picked)
    own = add_own(order, policy, [core(tiles) for tiles in cast_own(order, policy)])

    own, *planes = blend_rows(order, own, other, fetched)
    finished = chip(own)
    back = exchange(own)
    pieces = [([core(tiles) for tiles in planes], False, True), ([own], True, True)]
    (blended,) = write_rows(order, pieces, [], None, None, WRITE_COST, late_in_hbm=True)

    back = order.behind(back)
    finished = order.behind(finished)
    first, high = split_planes(order, finished, back)
    back_first = lax.all_to_all(first, ("y", "z"), split_axis=0, concat_axis=0, tiled=True)
    back_second = chip(high)
    new_anchor = place_back(order, back, core(back))
    pieces = [([finished], True, False), ([core(finished)], False, False)]
    (blended,) = write_rows(order, pieces, [], blended, None)
    back_second = order.behind(back_second)
    there_second = core(back_second)
    (new_anchor,) = write_rows(order, [], [(back_second, True, True, False)], None, new_anchor)
    back_first = order.behind(back_first)
    there_first = core(back_first)
    pieces = [(back_first, True, False, True), (there_second, False, True, False)]
    (new_anchor,) = write_rows(order, [], pieces, None, new_anchor, LAST_COST)
    (new_anchor,) = write_rows(order, [], [(there_first, False, False, True)], None, new_anchor)
    return blended, new_anchor.reshape(SHARDS * ROWS, WIDTH)


def solution(mesh):
    fine = Mesh(mesh.devices.reshape(SIZES), AXES)
    shards = ("y", "z", "xh")
    return jax.shard_map(
        per_device,
        mesh=fine,
        in_specs=(P(("xl", "c"), shards, None), P(None, shards)),
        out_specs=(P(shards, None), P(None, shards)),
        check_vma=False,
    )
```
